32 devices in a mesh: aux: 4 (over x, core), pair: 8 (over z, y).
Axes of the slice: x: 2, y: 2, z: 4, core: 2. Of those that a mesh axis runs over, the one named last changes fastest.
Arguments:
- chol_vv: bfloat16 [32, 896, 2304], P(None, 'pair', 'aux'), may hold values from -0.625 to 0.625
- chol_ov: bfloat16 [100, 896, 2304], P(None, 'pair', 'aux'), may hold values from -0.625 to 0.625
- t1_window: bfloat16 [100, 32], replicated, may hold values from -0.625 to 0.625
- amplitudes: bfloat16 [64, 896, 896], P(None, 'aux'), may hold values from -0.0068359375 to 0.0068359375
- assignment: int32 [8, 2], replicated, may hold values from 0 to 7
Outputs:
- residual: float32 [64, 128], P('aux', 'pair')
The draws below stay inside these ranges and needn't reach their ends.
All inputs are finite; a program needn't handle non-finite values.
Results may differ from the reference program's by a relative error of at most 0.0049.
Values may be sent and summed in bfloat16 or wider, within the bound.
No kernel may reach another device: no remote copies, remote signals or barrier semaphores. Data moves between devices by JAX's collectives and lax.ppermute only.
A program may use at most 256 MiB of HBM per device.

```python
import jax
import jax.numpy as jnp
from jax import lax

O = 100
V = 896
NAUX = 2304
BLK = 4
WIN = 32
IJ = 64
NBLK = 8
N_PAIR = 8


def place_ends(drawn, stream_key, least, largest):
    shape = drawn.shape
    place = [jax.random.randint(jax.random.fold_in(stream_key, axis), (), 0, shape[axis]) for axis in range(len(shape))]
    drawn = drawn.at[tuple(place)].set(least)
    longest = shape.index(max(shape))
    place[longest] = (place[longest] + 1) % shape[longest]
    return drawn.at[tuple(place)].set(largest)


def level_of(rng, dims, pieces, low, high):
    factor_of, own = 1.0, jax.random.fold_in(rng, 6)
    for axis_at, shards_of in pieces:
        steps = jnp.exp(jax.random.uniform(jax.random.fold_in(own, axis_at), (shards_of,), jnp.float32, low / len(pieces), high / len(pieces)))
        factor_of = factor_of * jnp.repeat(steps, dims[axis_at] // shards_of).reshape([-1 if axis == axis_at else 1 for axis in range(len(dims))])
    return factor_of


def normal_values(stream_key, extent, deviation, limit, split=(), dtype=jnp.bfloat16):
    array = jax.random.normal(stream_key, extent, jnp.float32) * deviation
    if len(split) > 0:
        array = level_of(stream_key, extent, split, -0.22, 0.18) * array
    return jnp.clip(array, min=-limit, max=limit).astype(dtype)


def setup_inputs(seed: int = 0) -> dict:
    key_of = jax.random.split(jax.random.key(seed), 6)
    chol_vv = normal_values(key_of[0], (WIN, V, NAUX), 0.1, 0.625, ((1, 8), (2, 4)))
    chol_ov = normal_values(key_of[1], (O, V, NAUX), 0.1, 0.625, ((1, 8), (2, 4)))
    t1_window = normal_values(key_of[2], (O, WIN), 0.1, 0.625)
    amplitudes = normal_values(key_of[3], (IJ, V, V), (V * V) ** -0.5, 0.0068359375, ((1, 4),))
    assignment = place_ends(jax.random.randint(key_of[4], (N_PAIR, 2), 0, NBLK), jax.random.fold_in(key_of[4], 1), 0, NBLK - 1).astype(jnp.int32)
    return dict(chol_vv=chol_vv, chol_ov=chol_ov, t1_window=t1_window, amplitudes=amplitudes, assignment=assignment)


def reference(chol_vv, chol_ov, t1_window, amplitudes, assignment):
    shift = jnp.dot(t1_window.T, chol_ov.reshape(O, V * NAUX), preferred_element_type=jnp.float32)
    dressed = (chol_vv.astype(jnp.float32).reshape(WIN, V * NAUX) - shift).astype(jnp.bfloat16)
    dressed = dressed.reshape(WIN, V, NAUX)
    flat_amps = amplitudes.reshape(IJ, V * V)

    def one_group(blocks):
        first = lax.dynamic_slice_in_dim(dressed, (blocks[0] * BLK).astype(jnp.int32), BLK, 0)
        second = lax.dynamic_slice_in_dim(dressed, (blocks[1] * BLK).astype(jnp.int32), BLK, 0)
        tiles = jnp.dot(first.reshape(BLK * V, NAUX), second.reshape(BLK * V, NAUX).T, preferred_element_type=jnp.float32)
        tiles = tiles.astype(jnp.bfloat16).reshape(BLK, V, BLK, V)
        tiles = tiles.transpose(1, 3, 0, 2).reshape(V * V, BLK * BLK)
        return jnp.dot(flat_amps, tiles, preferred_element_type=jnp.float32)

    results = lax.map(one_group, assignment)
    return results.transpose(1, 0, 2).reshape(IJ, N_PAIR * BLK * BLK)
```

```python
import functools

import jax
import jax.numpy as jnp
from jax import lax
from jax.experimental import pallas as pl
from jax.experimental.pallas import tpu as pltpu
from jax.sharding import PartitionSpec as P

BLK = 4
QUAD = 4
ROWS = 16
LANES = 128
CORES = 2
NT = (((1,), (1,)), ((), ()))
NN = (((1,), (0,)), ((), ()))


def round_up(value, unit):
    return (value + unit - 1) // unit * unit


class Plan:
    def __init__(self, window, occupied, cols, aux_dev, n_aux, n_pair, pairs_all):
        self.window, self.occupied, self.cols, self.aux_dev = window, occupied, cols, aux_dev
        self.n_aux, self.n_pair, self.ij = n_aux, n_pair, pairs_all
        self.xs = n_aux // CORES
        self.js = n_pair // CORES
        self.cpad = round_up(cols, ROWS)
        chunk = aux_dev // self.js
        self.main = chunk // LANES * LANES
        self.tail = chunk - self.main
        self.slot = 1
        while self.slot < self.tail:
            self.slot *= 2
        self.per_row = LANES // self.slot
        self.nm = self.main // LANES
        self.nt = window // self.per_row
        self.planes = self.nm * window + self.nt
        self.per = n_pair // n_aux
        self.c = self.per * self.cpad
        self.d = n_pair * self.cpad
        self.k = self.xs * LANES
        self.groups = n_pair
        self.blocks = window // BLK
        self.gf = self.groups * BLK
        self.tail_from = self.js * self.main
        self.tail_width = round_up(self.js * self.tail, LANES)


def dress_kernel(p, z_ref, a_ref, ov_ref, vv_ref, *refs):
    outs, (dressed, packed) = refs[: p.js], refs[p.js :]
    w = p.window

    @pl.when(pl.program_id(0) == 0)
    def _():
        dressed[...] = jnp.zeros_like(dressed)

    shift = lax.dot_general(
        a_ref[...],
        ov_ref[...].reshape(p.occupied * ROWS, p.aux_dev),
        NN,
        preferred_element_type=jnp.float32,
    )
    vv = vv_ref[...].astype(jnp.float32)
    dressed[:, :, : p.aux_dev] = vv - shift.reshape(w, ROWS, p.aux_dev)
    lane = lax.broadcasted_iota(jnp.int32, (p.nt, ROWS, LANES), 2)
    for j in range(p.js):
        for m in range(p.nm):
            low = j * p.main + m * LANES
            packed[j, m * w : (m + 1) * w] = dressed[:, :, low : low + LANES].astype(jnp.bfloat16)
        rest = jnp.zeros((p.nt, ROWS, LANES), jnp.float32)
        source = dressed[:, :, p.tail_from : p.tail_from + p.tail_width]
        source = source.reshape(p.nt, p.per_row, ROWS, p.tail_width)
        for s in range(p.per_row):
            turn = (s * p.slot - j * p.tail) % p.tail_width
            moved = pltpu.roll(source[:, s].reshape(p.nt * ROWS, p.tail_width), turn, 1)
            moved = moved[:, :LANES].reshape(p.nt, ROWS, LANES)
            here = (lane >= s * p.slot) & (lane < s * p.slot + p.tail)
            rest = jnp.where(here, moved, rest)
        packed[j, p.nm * w :] = rest.astype(jnp.bfloat16)
    z = z_ref[0]
    for o, out in enumerate(outs):
        out[...] = packed[lax.rem(z + o, p.js)]


def dress(p, z, chol_vv, chol_ov, t1_window):
    spread = jnp.einsum(
        "kw,cd->wckd", t1_window, jnp.eye(ROWS, dtype=jnp.bfloat16)
    ).reshape(p.window * ROWS, p.occupied * ROWS)
    message = jax.ShapeDtypeStruct((p.planes, p.cpad, LANES), jnp.bfloat16)
    return pl.pallas_call(
        functools.partial(dress_kernel, p),
        out_shape=[message] * p.js,
        grid_spec=pltpu.PrefetchScalarGridSpec(
            num_scalar_prefetch=1,
            grid=(p.cpad // ROWS,),
            in_specs=[
                pl.BlockSpec((p.window * ROWS, p.occupied * ROWS), lambda i, z: (0, 0)),
                pl.BlockSpec((p.occupied, ROWS, p.aux_dev), lambda i, z: (0, i, 0)),
                pl.BlockSpec((p.window, ROWS, p.aux_dev), lambda i, z: (0, i, 0)),
            ],
            out_specs=[pl.BlockSpec((p.planes, ROWS, LANES), lambda i, z: (0, i, 0))] * p.js,
            scratch_shapes=[
                pltpu.VMEM((p.window, ROWS, p.tail_from + p.tail_width), jnp.float32),
                pltpu.VMEM((p.js, p.planes, ROWS, LANES), jnp.bfloat16),
            ],
        ),
        compiler_params=pltpu.CompilerParams(vmem_limit_bytes=48 * 2**20),
        cost_estimate=pl.CostEstimate(
            flops=2 * p.window * p.occupied * p.cpad * p.aux_dev * ROWS,
            bytes_accessed=2 * (p.occupied + 2 * p.window) * p.cpad * p.aux_dev,
            transcendentals=0,
        ),
        name="dress",
    )(z, spread, chol_ov, chol_vv)


def ladder_kernel(p, parts, group, place_ref, blocks_ref, *refs):
    count = 2 * p.js * p.xs
    pieces, (amps, out), scratch = refs[:count], refs[count : count + 2], refs[count + 2 :]
    vectors, left_main, left_tail, spread_tail, tiles, held, total, piece_sem, amp_sem = scratch
    w, z, core, chunk = p.window, place_ref[0], place_ref[1], place_ref[2]
    quads = p.c // QUAD
    here = quads // parts
    rows = here * ROWS
    steps = here // group
    wide = group * QUAD * p.ij

    def fetch(step, slot):
        return pltpu.make_async_copy(
            amps.at[pl.ds(pl.multiple_of(step * wide, wide), wide)], held.at[slot], amp_sem.at[slot]
        )

    copies = []
    for o in range(p.js):
        for r in range(p.xs):
            for other in range(CORES):
                parity = core if other == 0 else 1 - core
                origin = CORES * lax.rem(z - o + p.js, p.js) + parity
                row = pl.multiple_of(origin * p.cpad, ROWS)
                copies.append(
                    pltpu.make_async_copy(
                        pieces[(o * p.xs + r) * CORES + other],
                        vectors.at[:, pl.ds(row, p.cpad), r * LANES : (r + 1) * LANES],
                        piece_sem.at[(o * p.xs + r) * CORES + other],
                    )
                )
    for copy in copies:
        copy.start()
    fetch(0, 0).start()
    for copy in copies:
        copy.wait()

    mixed = QUAD * ROWS
    to = lax.broadcasted_iota(jnp.int32, (mixed, mixed), 0)
    frm = lax.broadcasted_iota(jnp.int32, (mixed, mixed), 1)
    weave = ((to % BLK) * ROWS + to // BLK == frm).astype(jnp.float32).astype(jnp.bfloat16)
    lane_in = lax.broadcasted_iota(jnp.int32, (LANES, LANES), 0)
    lane_out = lax.broadcasted_iota(jnp.int32, (LANES, LANES), 1)
    same = lane_in % p.slot == lane_out % p.slot
    first = pl.multiple_of(chunk * p.c, ROWS)

    def woven(stack):
        return lax.dot_general(weave, stack, NN, preferred_element_type=jnp.float32).astype(
            jnp.bfloat16
        )

    @pl.loop(0, p.blocks)
    def _(b):
        for e in range(BLK):
            index = b * BLK + e
            plane = p.nm * w + index // p.per_row
            copier = (same & (lane_in // p.slot == index % p.per_row)).astype(jnp.float32)
            copier = copier.astype(jnp.bfloat16)
            for r in range(p.xs):
                span = slice(r * LANES, (r + 1) * LANES)
                spread_tail[e, :, span] = lax.dot_general(
                    vectors[plane, pl.ds(first, p.c), span],
                    copier,
                    NN,
                    preferred_element_type=jnp.float32,
                ).astype(jnp.bfloat16)
        for i in range(p.c // ROWS):
            span = slice(i * mixed, (i + 1) * mixed)
            tail = [spread_tail[e, i * ROWS : (i + 1) * ROWS, :] for e in range(BLK)]
            left_tail[b, span] = woven(jnp.concatenate(tail, axis=0))
            for m in range(p.nm):
                at = pl.ds(pl.multiple_of(first + i * ROWS, ROWS), ROWS)
                stack = [vectors[m * w + b * BLK + e, at] for e in range(BLK)]
                left_main[m, b, span] = woven(jnp.concatenate(stack, axis=0))

    total[...] = jnp.zeros_like(total)
    slot_of = lax.broadcasted_iota(jnp.int32, (1, p.k), 1) % LANES // p.slot

    @pl.loop(0, parts)
    def _(part):
        part_rows = pl.ds(pl.multiple_of(part * rows, rows), rows)

        @pl.loop(0, p.gf)
        def _(gf):
            left = blocks_ref[gf // BLK, 0]
            index = blocks_ref[gf // BLK, 1] * BLK + gf % BLK
            only = (slot_of == index % p.per_row).astype(jnp.float32).astype(jnp.bfloat16)
            lhs = [left_tail[left, part_rows] * only]
            planes = [p.nm * w + index // p.per_row]
            for m in range(p.nm):
                lhs.append(left_main[m, left, part_rows])
                planes.append(m * w + index)
            lhs = jnp.concatenate(lhs, axis=1)
            for low in range(0, p.d, 256):
                span = slice(low, min(low + 256, p.d))
                rhs = jnp.concatenate([vectors[plane, span] for plane in planes], axis=1)
                block = lax.dot_general(lhs, rhs, NT, preferred_element_type=jnp.float32)
                block = block.astype(jnp.bfloat16).reshape(here, ROWS, span.stop - low)
                tiles[:, gf, :, span] = block

        @pl.loop(0, steps)
        def _(step):
            at = part * steps + step
            slot = lax.rem(at, 2)

            @pl.when(at + 1 < parts * steps)
            def _():
                fetch(at + 1, 1 - slot).start()

            fetch(at, slot).wait()
            width = QUAD * p.ij
            for n in range(group):
                total[...] += lax.dot_general(
                    tiles[step * group + n].reshape(p.gf * ROWS, p.d),
                    held[slot, n * width : (n + 1) * width],
                    NT,
                    preferred_element_type=jnp.float32,
                )

    width = QUAD * p.ij
    row = lax.broadcasted_iota(jnp.int32, (p.gf * ROWS, width), 0) % ROWS // BLK
    col = lax.broadcasted_iota(jnp.int32, (p.gf * ROWS, width), 1) // p.ij
    kept = jnp.where(row == col, total[...], 0.0)
    folded = kept[:, :LANES]
    for low in range(LANES, width, LANES):
        folded += kept[:, low : low + LANES]
    shift = LANES
    while shift > p.ij:
        shift //= 2
        folded += pltpu.roll(folded, shift, 1)
    folded = folded.reshape(p.gf, 2, 8, LANES).sum(axis=1)
    out[...] = folded[:, :4] + folded[:, 4:]


def ladder(p, place, blocks, pieces, amps):
    parts, group = 2, 1
    quads = p.c // QUAD
    for wanted in (4, 2):
        if quads // parts % wanted == 0:
            group = wanted
            break
    width = QUAD * p.ij
    return pl.pallas_call(
        functools.partial(ladder_kernel, p, parts, group),
        out_shape=jax.ShapeDtypeStruct((p.gf, BLK, LANES), jnp.float32),
        in_specs=[pl.BlockSpec(memory_space=pltpu.SMEM)] * 2
        + [pl.BlockSpec(memory_space=pl.ANY)] * (len(pieces) + 1),
        out_specs=pl.BlockSpec(memory_space=pltpu.VMEM),
        scratch_shapes=[
            pltpu.VMEM((p.planes, p.d, p.k), jnp.bfloat16),
            pltpu.VMEM((max(p.nm, 1), p.blocks, BLK * p.c if p.nm else ROWS, p.k), jnp.bfloat16),
            pltpu.VMEM((p.blocks, BLK * p.c, p.k), jnp.bfloat16),
            pltpu.VMEM((BLK, p.c, p.k), jnp.bfloat16),
            pltpu.VMEM((quads // parts, p.gf, ROWS, p.d), jnp.bfloat16),
            pltpu.VMEM((2, group * width, p.d), jnp.bfloat16),
            pltpu.VMEM((p.gf * ROWS, width), jnp.float32),
            pltpu.SemaphoreType.DMA((len(pieces),)),
            pltpu.SemaphoreType.DMA((2,)),
        ],
        compiler_params=pltpu.CompilerParams(vmem_limit_bytes=63 * 2**20),
        cost_estimate=pl.CostEstimate(
            flops=2 * p.gf * BLK * p.c * p.d * p.k,
            bytes_accessed=2 * (len(pieces) * p.planes * p.cpad * LANES + p.c * p.ij * p.d),
            transcendentals=0,
        ),
        name="ladder",
    )(place, blocks, *pieces, amps)


def pad_columns(array, axis, cols, cpad):
    if cols == cpad:
        return array
    shape = array.shape
    split = array.reshape(shape[:axis] + (shape[axis] // cols, cols) + shape[axis + 1 :])
    widths = [(0, 0)] * split.ndim
    widths[axis + 1] = (0, cpad - cols)
    split = jnp.pad(split, widths)
    return split.reshape(shape[:axis] + (shape[axis] // cols * cpad,) + shape[axis + 1 :])


def shards(chol_vv, chol_ov, t1_window, amplitudes, assignment):
    window, cols, aux_dev = chol_vv.shape
    n_aux, n_pair = lax.axis_size("aux"), lax.axis_size("pair")
    p = Plan(window, chol_ov.shape[0], cols, aux_dev, n_aux, n_pair, amplitudes.shape[0])
    me_aux, me_pair = lax.axis_index("aux"), lax.axis_index("pair")
    z = me_pair // CORES
    place = jnp.stack([z, me_aux % CORES, me_aux]).astype(jnp.int32)

    chol_vv = pad_columns(chol_vv, 1, cols, p.cpad)
    chol_ov = pad_columns(chol_ov, 1, cols, p.cpad)
    messages = dress(p, place, chol_vv, chol_ov, t1_window)

    def permute(array, target):
        pairs = []
        for a in range(n_aux):
            for q in range(n_pair):
                to_a, to_q = target(a, q)
                pairs.append((a * n_pair + q, to_a * n_pair + to_q))
        return lax.ppermute(array, ("aux", "pair"), pairs)

    pieces = []
    for o in range(p.js):
        own = permute(
            messages[o],
            lambda a, q: (
                a // CORES * CORES + q % CORES,
                CORES * ((q // CORES + o) % p.js) + a % CORES,
            ),
        )
        for r in range(p.xs):
            turned = own
            if r:
                turned = permute(
                    own, lambda a, q: (CORES * ((a // CORES + r) % p.xs) + a % CORES, q)
                )
            pieces += [turned, permute(turned, lambda a, q: (a ^ 1, q))]

    amps = pad_columns(pad_columns(amplitudes, 1, cols, p.cpad), 2, cols, p.cpad)
    amps = jnp.transpose(amps, (1, 0, 2)).reshape(p.c * p.ij, p.d)

    partial_terms = ladder(p, place, assignment, pieces, amps)
    share = p.ij // n_aux
    terms = partial_terms[:, :, : p.ij].reshape(n_pair, BLK, BLK, n_aux, share)
    terms = terms.transpose(3, 0, 4, 2, 1).reshape(n_aux * n_pair, share, BLK * BLK)
    terms = lax.all_to_all(terms, ("aux", "pair"), split_axis=0, concat_axis=0, tiled=True)
    return terms.sum(axis=0)


def solution(mesh):
    in_specs = (P(None, "pair", "aux"), P(None, "pair", "aux"), P(), P(None, "aux", None), P())
    out_specs = P("aux", "pair")
    return jax.shard_map(shards, mesh=mesh, in_specs=in_specs, out_specs=out_specs, check_vma=False)
```

```python
import functools

import jax
import jax.numpy as jnp
from jax import lax
from jax.experimental import pallas as pl
from jax.experimental.pallas import tpu as pltpu
from jax.sharding import PartitionSpec as P

BLK = 4
QUAD = 4
ROWS = 16
LANES = 128
CORES = 2
NT = (((1,), (1,)), ((), ()))
NN = (((1,), (0,)), ((), ()))


def round_up(value, unit):
    return (value + unit - 1) // unit * unit


class Plan:
    def __init__(self, window, occupied, cols, aux_dev, n_aux, n_pair, pairs_all):
        self.window, self.occupied, self.cols, self.aux_dev = window, occupied, cols, aux_dev
        self.n_aux, self.n_pair, self.ij = n_aux, n_pair, pairs_all
        self.xs = n_aux // CORES
        self.js = n_pair // CORES
        self.cpad = round_up(cols, ROWS)
        chunk = aux_dev // self.js
        self.main = chunk // LANES * LANES
        self.tail = chunk - self.main
        self.slot = 1
        while self.slot < self.tail:
            self.slot *= 2
        self.per_row = LANES // self.slot
        self.nm = self.main // LANES
        self.nt = window // self.per_row
        self.planes = self.nm * window + self.nt
        self.per = n_pair // n_aux
        self.c = self.per * self.cpad
        self.d = n_pair * self.cpad
        self.k = self.xs * LANES
        self.groups = n_pair
        self.blocks = window // BLK
        self.gf = self.groups * BLK
        self.tail_from = self.js * self.main
        self.tail_width = round_up(self.js * self.tail, LANES)


def spread_kernel(p, t1_ref, out_ref):
    def repeat(rows, cols, per_row, per_col):
        row = lax.broadcasted_iota(jnp.int32, (rows, cols), 0) // per_row
        col = lax.broadcasted_iota(jnp.int32, (rows, cols), 1) // per_col
        return (row == col).astype(jnp.float32).astype(jnp.bfloat16)

    rows, cols = p.window * ROWS, p.occupied * ROWS
    tall = lax.dot_general(
        repeat(rows, p.window, ROWS, 1), t1_ref[...], NT, preferred_element_type=jnp.float32
    ).astype(jnp.bfloat16)
    full = jnp.dot(
        tall, repeat(p.occupied, cols, 1, ROWS), preferred_element_type=jnp.float32
    )
    row = lax.broadcasted_iota(jnp.int32, (rows, cols), 0) % ROWS
    col = lax.broadcasted_iota(jnp.int32, (rows, cols), 1) % ROWS
    out_ref[...] = jnp.where(row == col, full, 0.0).astype(jnp.bfloat16)


def spread_amplitudes(p, t1_window):
    return pl.pallas_call(
        functools.partial(spread_kernel, p),
        out_shape=jax.ShapeDtypeStruct((p.window * ROWS, p.occupied * ROWS), jnp.bfloat16),
        compiler_params=pltpu.CompilerParams(vmem_limit_bytes=48 * 2**20),
        name="spread",
    )(t1_window)


def dress_kernel(p, offset, z_ref, a_ref, *refs):
    ov, vv, out = refs[: p.nm + 1], refs[p.nm + 1 : 2 * p.nm + 2], refs[-1]
    w = p.window
    j = lax.rem(z_ref[0] + offset, p.js)
    vectors = jnp.concatenate([ref[...].reshape(p.occupied * ROWS, -1) for ref in ov], axis=1)
    shift = lax.dot_general(a_ref[...], vectors, NN, preferred_element_type=jnp.float32)
    for m in range(p.nm):
        here = shift[:, m * LANES : (m + 1) * LANES].reshape(w, ROWS, LANES)
        out[m * w : (m + 1) * w] = (vv[m][...].astype(jnp.float32) - here).astype(jnp.bfloat16)
    here = shift[:, p.nm * LANES :].reshape(w, ROWS, p.tail_width)
    source = vv[p.nm][...].astype(jnp.float32) - here
    source = source.reshape(p.nt, p.per_row, ROWS, p.tail_width)
    lane = lax.broadcasted_iota(jnp.int32, (p.nt, ROWS, LANES), 2)
    rest = jnp.zeros((p.nt, ROWS, LANES), jnp.float32)
    for s in range(p.per_row):
        turn = lax.rem(s * p.slot - j * p.tail + 2 * p.tail_width, p.tail_width)
        moved = pltpu.roll(source[:, s].reshape(p.nt * ROWS, p.tail_width), turn, 1)
        moved = moved[:, :LANES].reshape(p.nt, ROWS, LANES)
        keep = (lane >= s * p.slot) & (lane < s * p.slot + p.tail)
        rest = jnp.where(keep, moved, rest)
    out[p.nm * w :] = rest.astype(jnp.bfloat16)


def dress(p, offset, z, spread, chol_vv, chol_ov):
    def specs(lead):
        found = []
        for m in range(p.nm):
            found.append(
                pl.BlockSpec(
                    (lead, ROWS, LANES),
                    lambda i, z, m=m: (0, i, lax.rem(z[0] + offset, p.js) * p.nm + m),
                )
            )
        found.append(
            pl.BlockSpec(
                (lead, ROWS, p.tail_width), lambda i, z: (0, i, p.tail_from // p.tail_width)
            )
        )
        return found

    count = p.nm + 1
    return pl.pallas_call(
        functools.partial(dress_kernel, p, offset),
        out_shape=jax.ShapeDtypeStruct((p.planes, p.cpad, LANES), jnp.bfloat16),
        grid_spec=pltpu.PrefetchScalarGridSpec(
            num_scalar_prefetch=1,
            grid=(p.cpad // ROWS,),
            in_specs=[pl.BlockSpec((p.window * ROWS, p.occupied * ROWS), lambda i, z: (0, 0))]
            + specs(p.occupied)
            + specs(p.window),
            out_specs=pl.BlockSpec((p.planes, ROWS, LANES), lambda i, z: (0, i, 0)),
        ),
        compiler_params=pltpu.CompilerParams(vmem_limit_bytes=48 * 2**20),
        cost_estimate=pl.CostEstimate(
            flops=2 * p.window * p.occupied * p.cpad * LANES * count * ROWS,
            bytes_accessed=2 * (p.occupied + 2 * p.window) * p.cpad * LANES * count,
            transcendentals=0,
        ),
        name="dress",
    )(z, spread, *([chol_ov] * count), *([chol_vv] * count))


def ladder_kernel(p, parts, group, place_ref, blocks_ref, *refs):
    count = 2 * p.js * p.xs
    pieces, (amps, out), scratch = refs[:count], refs[count : count + 2], refs[count + 2 :]
    vectors, left_main, left_tail, spread_tail, tiles, held, total, piece_sem, amp_sem = scratch
    w, z, core, chunk = p.window, place_ref[0], place_ref[1], place_ref[2]
    quads = p.c // QUAD
    here = quads // parts
    rows = here * ROWS
    steps = here // group
    wide = group * QUAD * p.ij

    def fetch(step, slot):
        return pltpu.make_async_copy(
            amps.at[pl.ds(pl.multiple_of(step * wide, wide), wide)], held.at[slot], amp_sem.at[slot]
        )

    copies = []
    for o in range(p.js):
        for r in range(p.xs):
            for other in range(CORES):
                parity = core if other == 0 else 1 - core
                origin = CORES * lax.rem(z - o + p.js, p.js) + parity
                row = pl.multiple_of(origin * p.cpad, ROWS)
                copies.append(
                    pltpu.make_async_copy(
                        pieces[(o * p.xs + r) * CORES + other],
                        vectors.at[:, pl.ds(row, p.cpad), r * LANES : (r + 1) * LANES],
                        piece_sem.at[(o * p.xs + r) * CORES + other],
                    )
                )
    for copy in copies:
        copy.start()
    fetch(0, 0).start()
    for copy in copies:
        copy.wait()

    mixed = QUAD * ROWS
    to = lax.broadcasted_iota(jnp.int32, (mixed, mixed), 0)
    frm = lax.broadcasted_iota(jnp.int32, (mixed, mixed), 1)
    weave = ((to % BLK) * ROWS + to // BLK == frm).astype(jnp.float32).astype(jnp.bfloat16)
    lane_in = lax.broadcasted_iota(jnp.int32, (LANES, LANES), 0)
    lane_out = lax.broadcasted_iota(jnp.int32, (LANES, LANES), 1)
    same = lane_in % p.slot == lane_out % p.slot
    first = pl.multiple_of(chunk * p.c, ROWS)

    def woven(stack):
        return lax.dot_general(weave, stack, NN, preferred_element_type=jnp.float32).astype(
            jnp.bfloat16
        )

    @pl.loop(0, p.blocks)
    def _(b):
        for e in range(BLK):
            index = b * BLK + e
            plane = p.nm * w + index // p.per_row
            copier = (same & (lane_in // p.slot == index % p.per_row)).astype(jnp.float32)
            copier = copier.astype(jnp.bfloat16)
            for r in range(p.xs):
                span = slice(r * LANES, (r + 1) * LANES)
                spread_tail[e, :, span] = lax.dot_general(
                    vectors[plane, pl.ds(first, p.c), span],
                    copier,
                    NN,
                    preferred_element_type=jnp.float32,
                ).astype(jnp.bfloat16)
        for i in range(p.c // ROWS):
            span = slice(i * mixed, (i + 1) * mixed)
            tail = [spread_tail[e, i * ROWS : (i + 1) * ROWS, :] for e in range(BLK)]
            left_tail[b, span] = woven(jnp.concatenate(tail, axis=0))
            for m in range(p.nm):
                at = pl.ds(pl.multiple_of(first + i * ROWS, ROWS), ROWS)
                stack = [vectors[m * w + b * BLK + e, at] for e in range(BLK)]
                left_main[m, b, span] = woven(jnp.concatenate(stack, axis=0))

    total[...] = jnp.zeros_like(total)
    slot_of = lax.broadcasted_iota(jnp.int32, (1, p.k), 1) % LANES // p.slot

    @pl.loop(0, parts)
    def _(part):
        part_rows = pl.ds(pl.multiple_of(part * rows, rows), rows)

        @pl.loop(0, p.gf)
        def _(gf):
            left = blocks_ref[gf // BLK, 0]
            index = blocks_ref[gf // BLK, 1] * BLK + gf % BLK
            only = (slot_of == index % p.per_row).astype(jnp.float32).astype(jnp.bfloat16)
            lhs = [left_tail[left, part_rows] * only]
            planes = [p.nm * w + index // p.per_row]
            for m in range(p.nm):
                lhs.append(left_main[m, left, part_rows])
                planes.append(m * w + index)
            lhs = jnp.concatenate(lhs, axis=1)
            for low in range(0, p.d, 256):
                span = slice(low, min(low + 256, p.d))
                rhs = jnp.concatenate([vectors[plane, span] for plane in planes], axis=1)
                block = lax.dot_general(lhs, rhs, NT, preferred_element_type=jnp.float32)
                block = block.astype(jnp.bfloat16).reshape(here, ROWS, span.stop - low)
                tiles[:, gf, :, span] = block

        @pl.loop(0, steps)
        def _(step):
            at = part * steps + step
            slot = lax.rem(at, 2)

            @pl.when(at + 1 < parts * steps)
            def _():
                fetch(at + 1, 1 - slot).start()

            fetch(at, slot).wait()
            width = QUAD * p.ij
            for n in range(group):
                total[...] += lax.dot_general(
                    tiles[step * group + n].reshape(p.gf * ROWS, p.d),
                    held[slot, n * width : (n + 1) * width],
                    NT,
                    preferred_element_type=jnp.float32,
                )

    width = QUAD * p.ij
    row = lax.broadcasted_iota(jnp.int32, (p.gf * ROWS, width), 0) % ROWS // BLK
    col = lax.broadcasted_iota(jnp.int32, (p.gf * ROWS, width), 1) // p.ij
    kept = jnp.where(row == col, total[...], 0.0)
    folded = kept[:, :LANES]
    for low in range(LANES, width, LANES):
        folded += kept[:, low : low + LANES]
    shift = LANES
    while shift > p.ij:
        shift //= 2
        folded += pltpu.roll(folded, shift, 1)
    folded = folded.reshape(p.gf, 2, 8, LANES).sum(axis=1)
    out[...] = folded[:, :4] + folded[:, 4:]


def ladder(p, place, blocks, pieces, amps):
    parts, group = 2, 1
    quads = p.c // QUAD
    for wanted in (4, 2):
        if quads // parts % wanted == 0:
            group = wanted
            break
    width = QUAD * p.ij
    return pl.pallas_call(
        functools.partial(ladder_kernel, p, parts, group),
        out_shape=jax.ShapeDtypeStruct((p.gf, BLK, LANES), jnp.float32),
        in_specs=[pl.BlockSpec(memory_space=pltpu.SMEM)] * 2
        + [pl.BlockSpec(memory_space=pl.ANY)] * (len(pieces) + 1),
        out_specs=pl.BlockSpec(memory_space=pltpu.VMEM),
        scratch_shapes=[
            pltpu.VMEM((p.planes, p.d, p.k), jnp.bfloat16),
            pltpu.VMEM((max(p.nm, 1), p.blocks, BLK * p.c if p.nm else ROWS, p.k), jnp.bfloat16),
            pltpu.VMEM((p.blocks, BLK * p.c, p.k), jnp.bfloat16),
            pltpu.VMEM((BLK, p.c, p.k), jnp.bfloat16),
            pltpu.VMEM((quads // parts, p.gf, ROWS, p.d), jnp.bfloat16),
            pltpu.VMEM((2, group * width, p.d), jnp.bfloat16),
            pltpu.VMEM((p.gf * ROWS, width), jnp.float32),
            pltpu.SemaphoreType.DMA((len(pieces),)),
            pltpu.SemaphoreType.DMA((2,)),
        ],
        compiler_params=pltpu.CompilerParams(vmem_limit_bytes=63 * 2**20),
        cost_estimate=pl.CostEstimate(
            flops=2 * p.gf * BLK * p.c * p.d * p.k,
            bytes_accessed=2 * (len(pieces) * p.planes * p.cpad * LANES + p.c * p.ij * p.d),
            transcendentals=0,
        ),
        name="ladder",
    )(place, blocks, *pieces, amps)


def pad_columns(array, axis, cols, cpad):
    if cols == cpad:
        return array
    shape = array.shape
    split = array.reshape(shape[:axis] + (shape[axis] // cols, cols) + shape[axis + 1 :])
    widths = [(0, 0)] * split.ndim
    widths[axis + 1] = (0, cpad - cols)
    split = jnp.pad(split, widths)
    return split.reshape(shape[:axis] + (shape[axis] // cols * cpad,) + shape[axis + 1 :])


def shards(chol_vv, chol_ov, t1_window, amplitudes, assignment):
    window, cols, aux_dev = chol_vv.shape
    n_aux, n_pair = lax.axis_size("aux"), lax.axis_size("pair")
    p = Plan(window, chol_ov.shape[0], cols, aux_dev, n_aux, n_pair, amplitudes.shape[0])
    me_aux, me_pair = lax.axis_index("aux"), lax.axis_index("pair")
    z = me_pair // CORES
    place = jnp.stack([z, me_aux % CORES, me_aux]).astype(jnp.int32)

    chol_vv = pad_columns(chol_vv, 1, cols, p.cpad)
    chol_ov = pad_columns(chol_ov, 1, cols, p.cpad)
    spread = spread_amplitudes(p, t1_window)

    def permute(array, target):
        pairs = []
        for a in range(n_aux):
            for q in range(n_pair):
                to_a, to_q = target(a, q)
                pairs.append((a * n_pair + q, to_a * n_pair + to_q))
        return lax.ppermute(array, ("aux", "pair"), pairs)

    def to_slice(array, o):
        return permute(
            array,
            lambda a, q: (
                a // CORES * CORES + q % CORES,
                CORES * ((q // CORES + o) % p.js) + a % CORES,
            ),
        )

    def along_x(array, r):
        return permute(array, lambda a, q: (CORES * ((a // CORES + r) % p.xs) + a % CORES, q))

    def to_core(array):
        return permute(array, lambda a, q: (a ^ 1, q))

    order = sorted(range(p.js), key=lambda o: min(o, p.js - o))
    messages = {}
    for place_in_order, o in enumerate(order):
        messages[o] = dress(p, o, place, spread, chol_vv, chol_ov)
        if o == 0:
            turned_here = to_slice(messages[0], 0)
        if place_in_order == 1:
            spread, messages[o], turned_here = lax.optimization_barrier(
                (spread, messages[o], turned_here)
            )
        else:
            spread, messages[o] = lax.optimization_barrier((spread, messages[o]))

    messages[order[-1]], amplitudes = lax.optimization_barrier((messages[order[-1]], amplitudes))
    amps = pad_columns(pad_columns(amplitudes, 1, cols, p.cpad), 2, cols, p.cpad)
    amps = jnp.transpose(amps, (1, 0, 2)).reshape(p.c * p.ij, p.d)

    found = {}
    before = None
    for place_in_order, o in enumerate(order):
        if o == 0:
            turned = [turned_here]
            turned += [to_slice(along_x(messages[0], r), 0) for r in range(1, p.xs)]
        else:
            message = messages[o]
            if before is not None:
                message, before = lax.optimization_barrier((message, before))
            own = to_slice(message, o)
            before = own
            if place_in_order == p.js - 2:
                own, amps = lax.optimization_barrier((own, amps))
            turned = [own] + [along_x(own, r) for r in range(1, p.xs)]
        found[o] = [piece for array in turned for piece in (array, to_core(array))]
    pieces = [piece for o in range(p.js) for piece in found[o]]

    partial_terms = ladder(p, place, assignment, pieces, amps)
    share = p.ij // n_aux
    terms = partial_terms[:, :, : p.ij].reshape(n_pair, BLK, BLK, n_aux, share)
    terms = terms.transpose(3, 0, 4, 2, 1).reshape(n_aux * n_pair, share, BLK * BLK)
    terms = lax.all_to_all(terms, ("aux", "pair"), split_axis=0, concat_axis=0, tiled=True)
    return terms.sum(axis=0)


def solution(mesh):
    in_specs = (P(None, "pair", "aux"), P(None, "pair", "aux"), P(), P(None, "aux", None), P())
    out_specs = P("aux", "pair")
    return jax.shard_map(shards, mesh=mesh, in_specs=in_specs, out_specs=out_specs, check_vma=False)
```

```python
import functools

import jax
import jax.numpy as jnp
from jax import lax
from jax.experimental import pallas as pl
from jax.experimental.pallas import tpu as pltpu
from jax.sharding import PartitionSpec as P

BLK = 4
QUAD = 4
AMPS = 2
ROWS = 16
LANES = 128
CORES = 2
NT = (((1,), (1,)), ((), ()))
NN = (((1,), (0,)), ((), ()))


def round_up(value, unit):
    return (value + unit - 1) // unit * unit


class Plan:
    def __init__(self, window, occupied, cols, aux_dev, n_aux, n_pair, pairs_all):
        self.window, self.occupied, self.cols, self.aux_dev = window, occupied, cols, aux_dev
        self.n_aux, self.n_pair, self.ij = n_aux, n_pair, pairs_all
        self.xs = n_aux // CORES
        self.js = n_pair // CORES
        self.cpad = round_up(cols, ROWS)
        chunk = aux_dev // self.js
        self.main = chunk // LANES * LANES
        self.tail = chunk - self.main
        self.slot = 1
        while self.slot < self.tail:
            self.slot *= 2
        self.per_row = LANES // self.slot
        self.nm = self.main // LANES
        self.nt = window // self.per_row
        self.planes = self.nm * window + self.nt
        self.per = n_pair // n_aux
        self.c = self.per * self.cpad
        self.d = n_pair * self.cpad
        self.k = self.xs * LANES
        self.groups = n_pair
        self.blocks = window // BLK
        self.gf = self.groups * BLK
        self.tail_from = self.js * self.main
        self.tail_width = round_up(self.js * self.tail, LANES)


def spread_kernel(p, t1_ref, out_ref):
    def repeat(rows, cols, per_row, per_col):
        row = lax.broadcasted_iota(jnp.int32, (rows, cols), 0) // per_row
        col = lax.broadcasted_iota(jnp.int32, (rows, cols), 1) // per_col
        return (row == col).astype(jnp.float32).astype(jnp.bfloat16)

    rows, cols = p.window * ROWS, p.occupied * ROWS
    tall = lax.dot_general(
        repeat(rows, p.window, ROWS, 1), t1_ref[...], NT, preferred_element_type=jnp.float32
    ).astype(jnp.bfloat16)
    full = jnp.dot(
        tall, repeat(p.occupied, cols, 1, ROWS), preferred_element_type=jnp.float32
    )
    row = lax.broadcasted_iota(jnp.int32, (rows, cols), 0) % ROWS
    col = lax.broadcasted_iota(jnp.int32, (rows, cols), 1) % ROWS
    out_ref[...] = jnp.where(row == col, full, 0.0).astype(jnp.bfloat16)


def spread_amplitudes(p, t1_window):
    return pl.pallas_call(
        functools.partial(spread_kernel, p),
        out_shape=jax.ShapeDtypeStruct((p.window * ROWS, p.occupied * ROWS), jnp.bfloat16),
        compiler_params=pltpu.CompilerParams(vmem_limit_bytes=48 * 2**20),
        name="spread",
    )(t1_window)


def dress_kernel(p, offset, z_ref, a_ref, *refs):
    ov, vv, out = refs[: p.nm + 1], refs[p.nm + 1 : 2 * p.nm + 2], refs[-1]
    w = p.window
    j = lax.rem(z_ref[0] + offset, p.js)
    vectors = jnp.concatenate([ref[...].reshape(p.occupied * ROWS, -1) for ref in ov], axis=1)
    shift = lax.dot_general(a_ref[...], vectors, NN, preferred_element_type=jnp.float32)
    for m in range(p.nm):
        here = shift[:, m * LANES : (m + 1) * LANES].reshape(w, ROWS, LANES)
        out[m * w : (m + 1) * w] = (vv[m][...].astype(jnp.float32) - here).astype(jnp.bfloat16)
    here = shift[:, p.nm * LANES :].reshape(w, ROWS, p.tail_width)
    source = vv[p.nm][...].astype(jnp.float32) - here
    source = source.reshape(p.nt, p.per_row, ROWS, p.tail_width)
    lane = lax.broadcasted_iota(jnp.int32, (p.nt, ROWS, LANES), 2)
    rest = jnp.zeros((p.nt, ROWS, LANES), jnp.float32)
    for s in range(p.per_row):
        turn = lax.rem(s * p.slot - j * p.tail + 2 * p.tail_width, p.tail_width)
        moved = pltpu.roll(source[:, s].reshape(p.nt * ROWS, p.tail_width), turn, 1)
        moved = moved[:, :LANES].reshape(p.nt, ROWS, LANES)
        keep = (lane >= s * p.slot) & (lane < s * p.slot + p.tail)
        rest = jnp.where(keep, moved, rest)
    out[p.nm * w :] = rest.astype(jnp.bfloat16)


def dress(p, offset, z, spread, chol_vv, chol_ov):
    def specs(lead):
        found = []
        for m in range(p.nm):
            found.append(
                pl.BlockSpec(
                    (lead, ROWS, LANES),
                    lambda i, z, m=m: (0, i, lax.rem(z[0] + offset, p.js) * p.nm + m),
                )
            )
        found.append(
            pl.BlockSpec(
                (lead, ROWS, p.tail_width), lambda i, z: (0, i, p.tail_from // p.tail_width)
            )
        )
        return found

    count = p.nm + 1
    return pl.pallas_call(
        functools.partial(dress_kernel, p, offset),
        out_shape=jax.ShapeDtypeStruct((p.planes, p.cpad, LANES), jnp.bfloat16),
        grid_spec=pltpu.PrefetchScalarGridSpec(
            num_scalar_prefetch=1,
            grid=(p.cpad // ROWS,),
            in_specs=[pl.BlockSpec((p.window * ROWS, p.occupied * ROWS), lambda i, z: (0, 0))]
            + specs(p.occupied)
            + specs(p.window),
            out_specs=pl.BlockSpec((p.planes, ROWS, LANES), lambda i, z: (0, i, 0)),
        ),
        compiler_params=pltpu.CompilerParams(vmem_limit_bytes=48 * 2**20),
        cost_estimate=pl.CostEstimate(
            flops=2 * p.window * p.occupied * p.cpad * LANES * count * ROWS,
            bytes_accessed=2 * (p.occupied + 2 * p.window) * p.cpad * LANES * count,
            transcendentals=0,
        ),
        name="dress",
    )(z, spread, *([chol_ov] * count), *([chol_vv] * count))


def relayout_kernel(p, in_ref, out_ref):
    rows = ROWS * ROWS
    to = lax.broadcasted_iota(jnp.int32, (rows, rows), 0)
    frm = lax.broadcasted_iota(jnp.int32, (rows, rows), 1)
    turn = (to % ROWS * ROWS + to // ROWS == frm).astype(jnp.float32).astype(jnp.bfloat16)
    turned = lax.dot_general(
        turn, in_ref[...].reshape(rows, p.d), NN, preferred_element_type=jnp.float32
    )
    out_ref[...] = turned.astype(jnp.bfloat16).reshape(ROWS, ROWS, p.d)


def relayout(p, amplitudes, part):
    count = p.c // AMPS
    blocks = count // ROWS
    return pl.pallas_call(
        functools.partial(relayout_kernel, p),
        out_shape=jax.ShapeDtypeStruct((count, p.ij, p.d), jnp.bfloat16),
        grid=(blocks, p.ij // ROWS),
        in_specs=[pl.BlockSpec((ROWS, ROWS, p.d), lambda c, i: (i, part * blocks + c, 0))],
        out_specs=pl.BlockSpec((ROWS, ROWS, p.d), lambda c, i: (c, i, 0)),
        cost_estimate=pl.CostEstimate(
            flops=2 * count * p.ij * p.d * ROWS * ROWS,
            bytes_accessed=4 * count * p.ij * p.d,
            transcendentals=0,
        ),
        name="relayout",
    )(amplitudes)


def ladder_kernel(p, parts, group, place_ref, blocks_ref, *refs):
    pieces, amps, out = refs[: p.js], refs[p.js : p.js + AMPS], refs[p.js + AMPS]
    scratch = refs[p.js + AMPS + 1 :]
    vectors, left_main, left_tail, spread_tail, tiles, held, total, piece_sem, amp_sem = scratch
    w, z, chunk = p.window, place_ref[0], place_ref[1]
    quads = p.c // QUAD
    here = quads // parts
    rows = here * ROWS
    steps = here // group
    wide = group * QUAD * p.ij
    each = parts * steps // AMPS

    class Fetch:
        def __init__(self, step, slot):
            self.step, self.slot = step, slot

        def copy(self, amp, step):
            at = pl.ds(pl.multiple_of(step * wide, wide), wide)
            return pltpu.make_async_copy(amp.at[at], held.at[self.slot], amp_sem.at[self.slot])

        def start(self):
            for n, amp in enumerate(amps):

                @pl.when(self.step // each == n)
                def _():
                    self.copy(amp, self.step - n * each).start()

        def wait(self):
            self.copy(amps[0], 0).wait()

    copies = []
    for o in range(p.js):
        for source in range(p.n_aux):
            r, parity = source // CORES, source % CORES
            origin = CORES * lax.rem(z - o + p.js, p.js) + parity
            row = pl.multiple_of(origin * p.cpad, ROWS)
            copies.append(
                pltpu.make_async_copy(
                    pieces[o].at[source],
                    vectors.at[:, pl.ds(row, p.cpad), r * LANES : (r + 1) * LANES],
                    piece_sem.at[o * p.n_aux + source],
                )
            )
    for copy in copies:
        copy.start()
    Fetch(jnp.int32(0), 0).start()
    for copy in copies:
        copy.wait()

    mixed = QUAD * ROWS
    to = lax.broadcasted_iota(jnp.int32, (mixed, mixed), 0)
    frm = lax.broadcasted_iota(jnp.int32, (mixed, mixed), 1)
    weave = ((to % BLK) * ROWS + to // BLK == frm).astype(jnp.float32).astype(jnp.bfloat16)
    lane_in = lax.broadcasted_iota(jnp.int32, (LANES, LANES), 0)
    lane_out = lax.broadcasted_iota(jnp.int32, (LANES, LANES), 1)
    same = lane_in % p.slot == lane_out % p.slot
    first = pl.multiple_of(chunk * p.c, ROWS)

    def woven(stack):
        return lax.dot_general(weave, stack, NN, preferred_element_type=jnp.float32).astype(
            jnp.bfloat16
        )

    @pl.loop(0, p.blocks)
    def _(b):
        for e in range(BLK):
            index = b * BLK + e
            plane = p.nm * w + index // p.per_row
            copier = (same & (lane_in // p.slot == index % p.per_row)).astype(jnp.float32)
            copier = copier.astype(jnp.bfloat16)
            for r in range(p.xs):
                span = slice(r * LANES, (r + 1) * LANES)
                spread_tail[e, :, span] = lax.dot_general(
                    vectors[plane, pl.ds(first, p.c), span],
                    copier,
                    NN,
                    preferred_element_type=jnp.float32,
                ).astype(jnp.bfloat16)
        for i in range(p.c // ROWS):
            span = slice(i * mixed, (i + 1) * mixed)
            tail = [spread_tail[e, i * ROWS : (i + 1) * ROWS, :] for e in range(BLK)]
            left_tail[b, span] = woven(jnp.concatenate(tail, axis=0))
            for m in range(p.nm):
                at = pl.ds(pl.multiple_of(first + i * ROWS, ROWS), ROWS)
                stack = [vectors[m * w + b * BLK + e, at] for e in range(BLK)]
                left_main[m, b, span] = woven(jnp.concatenate(stack, axis=0))

    total[...] = jnp.zeros_like(total)
    slot_of = lax.broadcasted_iota(jnp.int32, (1, p.k), 1) % LANES // p.slot

    @pl.loop(0, parts)
    def _(part):
        part_rows = pl.ds(pl.multiple_of(part * rows, rows), rows)

        @pl.loop(0, p.gf)
        def _(gf):
            left = blocks_ref[gf // BLK, 0]
            index = blocks_ref[gf // BLK, 1] * BLK + gf % BLK
            only = (slot_of == index % p.per_row).astype(jnp.float32).astype(jnp.bfloat16)
            lhs = [left_tail[left, part_rows] * only]
            planes = [p.nm * w + index // p.per_row]
            for m in range(p.nm):
                lhs.append(left_main[m, left, part_rows])
                planes.append(m * w + index)
            lhs = jnp.concatenate(lhs, axis=1)
            for low in range(0, p.d, 256):
                span = slice(low, min(low + 256, p.d))
                rhs = jnp.concatenate([vectors[plane, span] for plane in planes], axis=1)
                block = lax.dot_general(lhs, rhs, NT, preferred_element_type=jnp.float32)
                block = block.astype(jnp.bfloat16).reshape(here, ROWS, span.stop - low)
                tiles[:, gf, :, span] = block

        @pl.loop(0, steps)
        def _(step):
            at = part * steps + step
            slot = lax.rem(at, 2)

            @pl.when(at + 1 < parts * steps)
            def _():
                Fetch(at + 1, 1 - slot).start()

            Fetch(at, slot).wait()
            width = QUAD * p.ij
            for n in range(group):
                total[...] += lax.dot_general(
                    tiles[step * group + n].reshape(p.gf * ROWS, p.d),
                    held[slot, n * width : (n + 1) * width],
                    NT,
                    preferred_element_type=jnp.float32,
                )

    width = QUAD * p.ij
    row = lax.broadcasted_iota(jnp.int32, (p.gf * ROWS, width), 0) % ROWS // BLK
    col = lax.broadcasted_iota(jnp.int32, (p.gf * ROWS, width), 1) // p.ij
    kept = jnp.where(row == col, total[...], 0.0)
    folded = kept[:, :LANES]
    for low in range(LANES, width, LANES):
        folded += kept[:, low : low + LANES]
    shift = LANES
    while shift > p.ij:
        shift //= 2
        folded += pltpu.roll(folded, shift, 1)
    folded = folded.reshape(p.gf, 2, 8, LANES).sum(axis=1)
    out[...] = folded[:, :4] + folded[:, 4:]


def ladder(p, place, blocks, pieces, amps):
    parts, group = 2, 1
    quads = p.c // QUAD
    for wanted in (4, 2):
        if quads // parts % wanted == 0:
            group = wanted
            break
    width = QUAD * p.ij
    return pl.pallas_call(
        functools.partial(ladder_kernel, p, parts, group),
        out_shape=jax.ShapeDtypeStruct((p.gf, BLK, LANES), jnp.float32),
        in_specs=[pl.BlockSpec(memory_space=pltpu.SMEM)] * 2
        + [pl.BlockSpec(memory_space=pl.ANY)] * (len(pieces) + AMPS),
        out_specs=pl.BlockSpec(memory_space=pltpu.VMEM),
        scratch_shapes=[
            pltpu.VMEM((p.planes, p.d, p.k), jnp.bfloat16),
            pltpu.VMEM((max(p.nm, 1), p.blocks, BLK * p.c if p.nm else ROWS, p.k), jnp.bfloat16),
            pltpu.VMEM((p.blocks, BLK * p.c, p.k), jnp.bfloat16),
            pltpu.VMEM((BLK, p.c, p.k), jnp.bfloat16),
            pltpu.VMEM((quads // parts, p.gf, ROWS, p.d), jnp.bfloat16),
            pltpu.VMEM((2, group * width, p.d), jnp.bfloat16),
            pltpu.VMEM((p.gf * ROWS, width), jnp.float32),
            pltpu.SemaphoreType.DMA((p.js * p.n_aux,)),
            pltpu.SemaphoreType.DMA((2,)),
        ],
        compiler_params=pltpu.CompilerParams(vmem_limit_bytes=63 * 2**20),
        cost_estimate=pl.CostEstimate(
            flops=2 * p.gf * BLK * p.c * p.d * p.k,
            bytes_accessed=2 * (p.js * p.n_aux * p.planes * p.cpad * LANES + p.c * p.ij * p.d),
            transcendentals=0,
        ),
        name="ladder",
    )(place, blocks, *pieces, *amps)


def pad_columns(array, axis, cols, cpad):
    if cols == cpad:
        return array
    shape = array.shape
    split = array.reshape(shape[:axis] + (shape[axis] // cols, cols) + shape[axis + 1 :])
    widths = [(0, 0)] * split.ndim
    widths[axis + 1] = (0, cpad - cols)
    split = jnp.pad(split, widths)
    return split.reshape(shape[:axis] + (shape[axis] // cols * cpad,) + shape[axis + 1 :])


def shards(chol_vv, chol_ov, t1_window, amplitudes, assignment):
    window, cols, aux_dev = chol_vv.shape
    n_aux, n_pair = lax.axis_size("aux"), lax.axis_size("pair")
    p = Plan(window, chol_ov.shape[0], cols, aux_dev, n_aux, n_pair, amplitudes.shape[0])
    me_aux, me_pair = lax.axis_index("aux"), lax.axis_index("pair")
    z = me_pair // CORES
    place = jnp.stack([z, me_aux]).astype(jnp.int32)

    chol_vv = pad_columns(chol_vv, 1, cols, p.cpad)
    chol_ov = pad_columns(chol_ov, 1, cols, p.cpad)
    spread = spread_amplitudes(p, t1_window)

    def permute(array, target):
        pairs = []
        for a in range(n_aux):
            for q in range(n_pair):
                to_a, to_q = target(a, q)
                pairs.append((a * n_pair + q, to_a * n_pair + to_q))
        return lax.ppermute(array, ("aux", "pair"), pairs)

    def to_slice(array, o):
        return permute(
            array,
            lambda a, q: (
                a // CORES * CORES + q % CORES,
                CORES * ((q // CORES + o) % p.js) + a % CORES,
            ),
        )

    order = sorted(range(p.js), key=lambda o: min(o, p.js - o))
    messages = {}
    for place_in_order, o in enumerate(order):
        messages[o] = dress(p, o, place, spread, chol_vv, chol_ov)
        if o == 0:
            turned_here = to_slice(messages[0], 0)
        if place_in_order == 1:
            spread, messages[o], turned_here = lax.optimization_barrier(
                (spread, messages[o], turned_here)
            )
        else:
            spread, messages[o] = lax.optimization_barrier((spread, messages[o]))

    messages[order[-1]], amplitudes = lax.optimization_barrier((messages[order[-1]], amplitudes))
    amplitudes = pad_columns(pad_columns(amplitudes, 1, cols, p.cpad), 2, cols, p.cpad)
    amps = [relayout(p, amplitudes, part) for part in range(AMPS)]

    found = {}
    before = turned_here
    for place_in_order, o in enumerate(order):
        if o == 0:
            own = turned_here
        else:
            message, before = lax.optimization_barrier((messages[o], before))
            own = before = to_slice(message, o)
        if place_in_order == 1:
            own, messages[order[2]] = lax.optimization_barrier((own, messages[order[2]]))
        part = place_in_order - (p.js - AMPS)
        if part >= 0:
            own, amps[part] = lax.optimization_barrier((own, amps[part]))
        found[o] = lax.all_gather(own, "aux", axis=0, tiled=False)
    amps = [amp.reshape(-1, p.d) for amp in amps]
    pieces = [found[o] for o in range(p.js)]

    partial_terms = ladder(p, place, assignment, pieces, amps)
    share = p.ij // n_aux
    terms = partial_terms[:, :, : p.ij].reshape(n_pair, BLK, BLK, n_aux, share)
    terms = terms.transpose(3, 0, 4, 2, 1).reshape(n_aux * n_pair, share, BLK * BLK)
    terms = lax.all_to_all(terms, ("aux", "pair"), split_axis=0, concat_axis=0, tiled=True)
    return terms.sum(axis=0)


def solution(mesh):
    in_specs = (P(None, "pair", "aux"), P(None, "pair", "aux"), P(), P(None, "aux", None), P())
    out_specs = P("aux", "pair")
    return jax.shard_map(shards, mesh=mesh, in_specs=in_specs, out_specs=out_specs, check_vma=False)
```

```python
import functools

import jax
import jax.numpy as jnp
from jax import lax
from jax.experimental import pallas as pl
from jax.experimental.pallas import tpu as pltpu
from jax.sharding import PartitionSpec as P

BLK = 4
QUAD = 4
AMPS = 2
DEEP = 256
ROWS = 16
LANES = 128
CORES = 2
NT = (((1,), (1,)), ((), ()))
NN = (((1,), (0,)), ((), ()))


def round_up(value, unit):
    return (value + unit - 1) // unit * unit


class Plan:
    def __init__(self, window, occupied, cols, aux_dev, n_aux, n_pair, pairs_all):
        self.window, self.occupied, self.cols, self.aux_dev = window, occupied, cols, aux_dev
        self.n_aux, self.n_pair, self.ij = n_aux, n_pair, pairs_all
        self.xs = n_aux // CORES
        self.js = n_pair // CORES
        self.cpad = round_up(cols, ROWS)
        chunk = aux_dev // self.js
        self.main = chunk // LANES * LANES
        self.tail = chunk - self.main
        self.slot = 1
        while self.slot < self.tail:
            self.slot *= 2
        self.per_row = LANES // self.slot
        self.nm = self.main // LANES
        self.nt = window // self.per_row
        self.planes = self.nm * window + self.nt
        self.per = n_pair // n_aux
        self.c = self.per * self.cpad
        self.d = n_pair * self.cpad
        self.k = self.xs * LANES
        self.groups = n_pair
        self.blocks = window // BLK
        self.gf = self.groups * BLK
        self.tail_from = self.js * self.main
        self.tail_width = round_up(self.js * self.tail, LANES)


def spread_kernel(p, t1_ref, out_ref):
    def repeat(rows, cols, per_row, per_col):
        row = lax.broadcasted_iota(jnp.int32, (rows, cols), 0) // per_row
        col = lax.broadcasted_iota(jnp.int32, (rows, cols), 1) // per_col
        return (row == col).astype(jnp.float32).astype(jnp.bfloat16)

    rows, cols = p.window * ROWS, p.occupied * ROWS
    tall = lax.dot_general(
        repeat(rows, p.window, ROWS, 1), t1_ref[...], NT, preferred_element_type=jnp.float32
    ).astype(jnp.bfloat16)
    full = jnp.dot(
        tall, repeat(p.occupied, cols, 1, ROWS), preferred_element_type=jnp.float32
    )
    row = lax.broadcasted_iota(jnp.int32, (rows, cols), 0) % ROWS
    col = lax.broadcasted_iota(jnp.int32, (rows, cols), 1) % ROWS
    out_ref[...] = jnp.where(row == col, full, 0.0).astype(jnp.bfloat16)


def spread_amplitudes(p, t1_window):
    return pl.pallas_call(
        functools.partial(spread_kernel, p),
        out_shape=jax.ShapeDtypeStruct((p.window * ROWS, p.occupied * ROWS), jnp.bfloat16),
        compiler_params=pltpu.CompilerParams(vmem_limit_bytes=48 * 2**20),
        name="spread",
    )(t1_window)


def dress_kernel(p, offset, z_ref, a_ref, *refs):
    ov, vv, out = refs[: p.nm + 1], refs[p.nm + 1 : 2 * p.nm + 2], refs[-1]
    w = p.window
    j = lax.rem(z_ref[0] + offset, p.js)
    vectors = jnp.concatenate([ref[...].reshape(p.occupied * ROWS, -1) for ref in ov], axis=1)
    shift = lax.dot_general(a_ref[...], vectors, NN, preferred_element_type=jnp.float32)
    for m in range(p.nm):
        here = shift[:, m * LANES : (m + 1) * LANES].reshape(w, ROWS, LANES)
        out[m * w : (m + 1) * w] = (vv[m][...].astype(jnp.float32) - here).astype(jnp.bfloat16)
    here = shift[:, p.nm * LANES :].reshape(w, ROWS, p.tail_width)
    source = vv[p.nm][...].astype(jnp.float32) - here
    source = source.reshape(p.nt, p.per_row, ROWS, p.tail_width)
    lane = lax.broadcasted_iota(jnp.int32, (p.nt, ROWS, LANES), 2)
    rest = jnp.zeros((p.nt, ROWS, LANES), jnp.float32)
    for s in range(p.per_row):
        turn = lax.rem(s * p.slot - j * p.tail + 2 * p.tail_width, p.tail_width)
        moved = pltpu.roll(source[:, s].reshape(p.nt * ROWS, p.tail_width), turn, 1)
        moved = moved[:, :LANES].reshape(p.nt, ROWS, LANES)
        keep = (lane >= s * p.slot) & (lane < s * p.slot + p.tail)
        rest = jnp.where(keep, moved, rest)
    out[p.nm * w :] = rest.astype(jnp.bfloat16)


def dress(p, offset, z, spread, chol_vv, chol_ov):
    def specs(lead):
        found = []
        for m in range(p.nm):
            found.append(
                pl.BlockSpec(
                    (lead, ROWS, LANES),
                    lambda i, z, m=m: (0, i, lax.rem(z[0] + offset, p.js) * p.nm + m),
                )
            )
        found.append(
            pl.BlockSpec(
                (lead, ROWS, p.tail_width),
                lambda i, z: (0, i, p.tail_from // p.tail_width),
            )
        )
        return found

    count = p.nm + 1
    return pl.pallas_call(
        functools.partial(dress_kernel, p, offset),
        out_shape=jax.ShapeDtypeStruct((p.planes, p.cpad, LANES), jnp.bfloat16),
        grid_spec=pltpu.PrefetchScalarGridSpec(
            num_scalar_prefetch=1,
            grid=(p.cpad // ROWS,),
            in_specs=[pl.BlockSpec((p.window * ROWS, p.occupied * ROWS), lambda i, z: (0, 0))]
            + specs(p.occupied)
            + specs(p.window),
            out_specs=pl.BlockSpec((p.planes, ROWS, LANES), lambda i, z: (0, i, 0)),
        ),
        compiler_params=pltpu.CompilerParams(vmem_limit_bytes=48 * 2**20),
        cost_estimate=pl.CostEstimate(
            flops=2 * p.window * p.occupied * p.cpad * LANES * count * ROWS,
            bytes_accessed=2 * (p.occupied + 2 * p.window) * p.cpad * LANES * count,
            transcendentals=0,
        ),
        name="dress",
    )(z, spread, *([chol_ov] * count), *([chol_vv] * count))


def relayout_kernel(p, in_ref, out_ref):
    rows = ROWS * ROWS
    to = lax.broadcasted_iota(jnp.int32, (rows, rows), 0)
    frm = lax.broadcasted_iota(jnp.int32, (rows, rows), 1)
    turn = (to % ROWS * ROWS + to // ROWS == frm).astype(jnp.float32).astype(jnp.bfloat16)
    for low in range(0, p.ij, ROWS):
        block = in_ref[low : low + ROWS].reshape(rows, p.d)
        turned = lax.dot_general(turn, block, NN, preferred_element_type=jnp.float32)
        out_ref[:, low : low + ROWS] = turned.astype(jnp.bfloat16).reshape(ROWS, ROWS, p.d)


def relayout(p, amplitudes, part):
    count = p.c // AMPS
    blocks = count // ROWS
    return pl.pallas_call(
        functools.partial(relayout_kernel, p),
        out_shape=jax.ShapeDtypeStruct((count, p.ij, p.d), jnp.bfloat16),
        grid=(blocks,),
        in_specs=[pl.BlockSpec((p.ij, ROWS, p.d), lambda c: (0, part * blocks + c, 0))],
        out_specs=pl.BlockSpec((ROWS, p.ij, p.d), lambda c: (c, 0, 0)),
        compiler_params=pltpu.CompilerParams(vmem_limit_bytes=40 * 2**20),
        cost_estimate=pl.CostEstimate(
            flops=2 * count * p.ij * p.d * ROWS * ROWS,
            bytes_accessed=4 * count * p.ij * p.d,
            transcendentals=0,
        ),
        name="relayout",
    )(amplitudes)


def ladder_kernel(p, group, place_ref, blocks_ref, *refs):
    count = p.js * p.xs
    pieces, amps, out = refs[:count], refs[count : count + AMPS], refs[count + AMPS]
    scratch = refs[count + AMPS + 1 :]
    vectors, left, strided, tiles, held, total, piece_sem, amp_sem = scratch
    w, z, chunk = p.window, place_ref[0], place_ref[1]
    quads = p.c // QUAD
    width = QUAD * p.ij
    steps = quads // group
    each = steps // AMPS
    spans = [slice(low, min(low + DEEP, p.d)) for low in range(0, p.d, DEEP)]

    def fetch(span, step, slot, act):
        for n, amp in enumerate(amps):

            @pl.when(step // each == n)
            def _():
                at = pl.multiple_of((step - n * each) * group * width, group * width)
                copy = pltpu.make_async_copy(
                    amp.at[pl.ds(at, group * width), span],
                    held.at[slot, :, : span.stop - span.start],
                    amp_sem.at[slot],
                )
                copy.start() if act == "start" else copy.wait()

    copies = []
    for o in range(p.js):
        for r in range(p.xs):
            for parity in range(CORES):
                origin = CORES * lax.rem(z - o + p.js, p.js) + parity
                row = pl.multiple_of(origin * p.cpad, ROWS)
                copies.append(
                    pltpu.make_async_copy(
                        pieces[o * p.xs + r].at[parity],
                        vectors.at[:, pl.ds(row, p.cpad), r * LANES : (r + 1) * LANES],
                        piece_sem.at[(o * p.xs + r) * CORES + parity],
                    )
                )
    for copy in copies:
        copy.start()
    fetch(spans[0], 0, 0, "start")
    total[...] = jnp.zeros_like(total)
    for copy in copies:
        copy.wait()

    first = pl.multiple_of(chunk * p.c, ROWS)
    lane = lax.broadcasted_iota(jnp.int32, (p.c, LANES), 1)

    @pl.loop(0, p.blocks)
    def _(b):
        for r in range(p.xs):
            span = slice(r * LANES, (r + 1) * LANES)
            for m in range(p.nm + 1):
                for e in range(BLK):
                    index = b * BLK + e
                    plane = m * w + index if m < p.nm else m * w + index // p.per_row
                    rows = vectors[plane, pl.ds(first, p.c), span].astype(jnp.float32)
                    if m == p.nm:
                        rows = jnp.where(lane // p.slot == index % p.per_row, rows, 0.0)
                        turn = p.slot
                        while turn < LANES:
                            rows += pltpu.roll(rows, turn, 1)
                            turn *= 2
                    strided[pl.ds(e, p.c, stride=BLK), :] = rows
                at = slice((m * p.xs + r) * LANES, (m * p.xs + r + 1) * LANES)
                left[b, :, at] = strided[...].astype(jnp.bfloat16)

    slot_of = lax.broadcasted_iota(jnp.int32, (1, p.k), 1) % LANES // p.slot

    for number, span in enumerate(spans):
        size = span.stop - span.start

        @pl.loop(0, p.gf)
        def _(gf):
            block = blocks_ref[gf // BLK, 0]
            index = blocks_ref[gf // BLK, 1] * BLK + gf % BLK
            only = (slot_of == index % p.per_row).astype(jnp.float32).astype(jnp.bfloat16)
            lhs, rhs = [], []
            for m in range(p.nm):
                lhs.append(left[block, :, m * p.k : (m + 1) * p.k])
                rhs.append(vectors[m * w + index, span])
            lhs.append(left[block, :, p.nm * p.k :] * only)
            rhs.append(vectors[p.nm * w + index // p.per_row, span])
            tile = lax.dot_general(
                jnp.concatenate(lhs, axis=1),
                jnp.concatenate(rhs, axis=1),
                NT,
                preferred_element_type=jnp.float32,
            )
            tiles[:, gf, :, :size] = tile.astype(jnp.bfloat16).reshape(quads, ROWS, size)

        @pl.loop(0, steps)
        def _(step):
            slot = lax.rem(number * steps + step, 2)

            @pl.when(step + 1 < steps)
            def _():
                fetch(span, step + 1, 1 - slot, "start")

            if number + 1 < len(spans):

                @pl.when(step + 1 == steps)
                def _():
                    fetch(spans[number + 1], 0, 1 - slot, "start")

            fetch(span, step, slot, "wait")
            lhs = [
                tiles[step * group + n, :, :, :size].reshape(p.gf * ROWS, size)
                for n in range(group)
            ]
            rhs = [held[slot, n * width : (n + 1) * width, :size] for n in range(group)]
            total[...] += lax.dot_general(
                jnp.concatenate(lhs, axis=1),
                jnp.concatenate(rhs, axis=1),
                NT,
                preferred_element_type=jnp.float32,
            )

    row = lax.broadcasted_iota(jnp.int32, (p.gf * ROWS, width), 0) % ROWS // BLK
    col = lax.broadcasted_iota(jnp.int32, (p.gf * ROWS, width), 1) // p.ij
    kept = jnp.where(row == col, total[...], 0.0)
    folded = kept[:, :LANES]
    for low in range(LANES, width, LANES):
        folded += kept[:, low : low + LANES]
    shift = LANES
    while shift > p.ij:
        shift //= 2
        folded += pltpu.roll(folded, shift, 1)
    folded = folded.reshape(p.gf, 2, 8, LANES).sum(axis=1)
    out[...] = folded[:, :4] + folded[:, 4:]


def ladder(p, place, blocks, pieces, amps):
    quads = p.c // QUAD
    group = 4 if quads // AMPS % 4 == 0 else 2
    width = QUAD * p.ij
    return pl.pallas_call(
        functools.partial(ladder_kernel, p, group),
        out_shape=jax.ShapeDtypeStruct((p.gf, BLK, LANES), jnp.float32),
        in_specs=[pl.BlockSpec(memory_space=pltpu.SMEM)] * 2
        + [pl.BlockSpec(memory_space=pl.ANY)] * (len(pieces) + AMPS),
        out_specs=pl.BlockSpec(memory_space=pltpu.VMEM),
        scratch_shapes=[
            pltpu.VMEM((p.planes, p.d, p.k), jnp.bfloat16),
            pltpu.VMEM((p.blocks, BLK * p.c, (p.nm + 1) * p.k), jnp.bfloat16),
            pltpu.VMEM((BLK * p.c, LANES), jnp.float32),
            pltpu.VMEM((quads, p.gf, ROWS, DEEP), jnp.bfloat16),
            pltpu.VMEM((2, group * width, DEEP), jnp.bfloat16),
            pltpu.VMEM((p.gf * ROWS, width), jnp.float32),
            pltpu.SemaphoreType.DMA((len(pieces) * CORES,)),
            pltpu.SemaphoreType.DMA((2,)),
        ],
        compiler_params=pltpu.CompilerParams(vmem_limit_bytes=60 * 2**20),
        cost_estimate=pl.CostEstimate(
            flops=2 * p.gf * BLK * p.c * p.d * p.k,
            bytes_accessed=2 * (p.planes * p.d * p.k + p.c * p.ij * p.d),
            transcendentals=0,
        ),
        name="ladder",
    )(place, blocks, *pieces, *amps)


def pad_columns(array, axis, cols, cpad):
    if cols == cpad:
        return array
    shape = array.shape
    split = array.reshape(shape[:axis] + (shape[axis] // cols, cols) + shape[axis + 1 :])
    widths = [(0, 0)] * split.ndim
    widths[axis + 1] = (0, cpad - cols)
    split = jnp.pad(split, widths)
    return split.reshape(shape[:axis] + (shape[axis] // cols * cpad,) + shape[axis + 1 :])


def shards(chol_vv, chol_ov, t1_window, amplitudes, assignment):
    window, cols, aux_dev = chol_vv.shape
    n_aux, n_pair = lax.axis_size("aux"), lax.axis_size("pair")
    p = Plan(window, chol_ov.shape[0], cols, aux_dev, n_aux, n_pair, amplitudes.shape[0])
    me_aux, me_pair = lax.axis_index("aux"), lax.axis_index("pair")
    z = me_pair // CORES
    place = jnp.stack([z, me_aux]).astype(jnp.int32)

    chol_vv = pad_columns(chol_vv, 1, cols, p.cpad)
    chol_ov = pad_columns(chol_ov, 1, cols, p.cpad)
    spread = spread_amplitudes(p, t1_window)

    def permute(array, target):
        pairs = []
        for a in range(n_aux):
            for q in range(n_pair):
                to_a, to_q = target(a, q)
                pairs.append((a * n_pair + q, to_a * n_pair + to_q))
        return lax.ppermute(array, ("aux", "pair"), pairs)

    def to_slice(array, o):
        return permute(
            array,
            lambda a, q: (
                a // CORES * CORES + q % CORES,
                CORES * ((q // CORES + o) % p.js) + a % CORES,
            ),
        )

    order = sorted(range(p.js), key=lambda o: min(o, p.js - o))
    messages = {}
    for place_in_order, o in enumerate(order):
        messages[o] = dress(p, o, place, spread, chol_vv, chol_ov)
        if o == 0:
            turned_here = to_slice(messages[0], 0)
        if place_in_order == 1:
            spread, messages[o], turned_here = lax.optimization_barrier(
                (spread, messages[o], turned_here)
            )
        else:
            spread, messages[o] = lax.optimization_barrier((spread, messages[o]))

    messages[order[-1]], amplitudes = lax.optimization_barrier((messages[order[-1]], amplitudes))
    amplitudes = pad_columns(pad_columns(amplitudes, 1, cols, p.cpad), 2, cols, p.cpad)
    amps = [relayout(p, amplitudes, part) for part in range(AMPS)]

    def along_x(array, r):
        return permute(array, lambda a, q: (CORES * ((a // CORES + r) % p.xs) + a % CORES, q))

    cores = [list(range(a, a + CORES)) for a in range(0, n_aux, CORES)]

    def share(array):
        return lax.all_gather(array, "aux", axis_index_groups=cores, axis=0, tiled=False)

    def beside(array, work):
        return lax.optimization_barrier((array, work))[0]

    late = [messages[o] for o in order[2:]]
    found = {}
    before = earlier = swapped = None
    for place_in_order, o in enumerate(order):
        if o == 0:
            own = turned_here
        else:
            message, before, earlier = lax.optimization_barrier((messages[o], before, earlier))
            own = to_slice(message, o)
        last = p.js - 1 - place_in_order
        if place_in_order == 1:
            own = beside(own, late)
        turned = [own] + [along_x(own, r) for r in range(1, p.xs)]
        if place_in_order == 0:
            turned[1:] = beside(turned[1:], late)
        if last == 2:
            turned[1:] = beside(turned[1:], amps[0])
        if last == 1:
            turned[0] = beside(turned[0], amps[0])
        if last == 0:
            turned[1:] = beside(turned[1:], amps[1:])
        before, earlier, swapped = own, swapped, turned[1:]
        found[o] = [share(array) for array in turned]
    amps = [amp.reshape(-1, p.d) for amp in amps]
    pieces = [piece for o in range(p.js) for piece in found[o]]

    partial_terms = ladder(p, place, assignment, pieces, amps)
    share = p.ij // n_aux
    terms = partial_terms[:, :, : p.ij].reshape(n_pair, BLK, BLK, n_aux, share)
    terms = terms.transpose(3, 0, 4, 2, 1).reshape(n_aux * n_pair, share, BLK * BLK)
    terms = lax.all_to_all(terms, ("aux", "pair"), split_axis=0, concat_axis=0, tiled=True)
    return terms.sum(axis=0)


def solution(mesh):
    in_specs = (P(None, "pair", "aux"), P(None, "pair", "aux"), P(), P(None, "aux", None), P())
    out_specs = P("aux", "pair")
    return jax.shard_map(shards, mesh=mesh, in_specs=in_specs, out_specs=out_specs, check_vma=False)
```

```python
import functools

import jax
import jax.numpy as jnp
from jax import lax
from jax.experimental import pallas as pl
from jax.experimental.pallas import tpu as pltpu
from jax.sharding import PartitionSpec as P

BLK = 4
QUAD = 4
AMPS = 2
DEEP = 256
ROWS = 16
LANES = 128
CORES = 2
NT = (((1,), (1,)), ((), ()))
NN = (((1,), (0,)), ((), ()))


def round_up(value, unit):
    return (value + unit - 1) // unit * unit


class Plan:
    def __init__(self, window, occupied, cols, aux_dev, n_aux, n_pair, pairs_all):
        self.window, self.occupied, self.cols, self.aux_dev = window, occupied, cols, aux_dev
        self.n_aux, self.n_pair, self.ij = n_aux, n_pair, pairs_all
        self.xs = n_aux // CORES
        self.js = n_pair // CORES
        self.cpad = round_up(cols, ROWS)
        chunk = aux_dev // self.js
        self.main = chunk // LANES * LANES
        self.tail = chunk - self.main
        self.slot = 1
        while self.slot < self.tail:
            self.slot *= 2
        self.per_row = LANES // self.slot
        self.nm = self.main // LANES
        self.nt = window // self.per_row
        self.planes = self.nm * window + self.nt
        self.per = n_pair // n_aux
        self.c = self.per * self.cpad
        self.d = n_pair * self.cpad
        self.k = self.xs * LANES
        self.groups = n_pair
        self.blocks = window // BLK
        self.gf = self.groups * BLK
        self.tail_from = self.js * self.main
        self.tail_width = round_up(self.js * self.tail, LANES)


def spread_kernel(p, t1_ref, out_ref):
    def repeat(rows, cols, per_row, per_col):
        row = lax.broadcasted_iota(jnp.int32, (rows, cols), 0) // per_row
        col = lax.broadcasted_iota(jnp.int32, (rows, cols), 1) // per_col
        return (row == col).astype(jnp.float32).astype(jnp.bfloat16)

    rows, cols = p.window * ROWS, p.occupied * ROWS
    tall = lax.dot_general(
        repeat(rows, p.window, ROWS, 1), t1_ref[...], NT, preferred_element_type=jnp.float32
    ).astype(jnp.bfloat16)
    full = jnp.dot(
        tall, repeat(p.occupied, cols, 1, ROWS), preferred_element_type=jnp.float32
    )
    row = lax.broadcasted_iota(jnp.int32, (rows, cols), 0) % ROWS
    col = lax.broadcasted_iota(jnp.int32, (rows, cols), 1) % ROWS
    out_ref[...] = jnp.where(row == col, full, 0.0).astype(jnp.bfloat16)


def spread_amplitudes(p, t1_window):
    return pl.pallas_call(
        functools.partial(spread_kernel, p),
        out_shape=jax.ShapeDtypeStruct((p.window * ROWS, p.occupied * ROWS), jnp.bfloat16),
        compiler_params=pltpu.CompilerParams(vmem_limit_bytes=48 * 2**20),
        name="spread",
    )(t1_window)


def dress_kernel(p, offset, z_ref, a_ref, *refs):
    ov, vv, out = refs[: p.nm + 1], refs[p.nm + 1 : 2 * p.nm + 2], refs[-1]
    w = p.window
    j = lax.rem(z_ref[0] + offset, p.js)
    lane = lax.broadcasted_iota(jnp.int32, (p.nt, ROWS, LANES), 2)
    for low in range(0, p.cpad, ROWS):
        cols = slice(low, low + ROWS)
        vectors = [ref[:, cols].reshape(p.occupied * ROWS, -1) for ref in ov]
        shift = lax.dot_general(
            a_ref[...], jnp.concatenate(vectors, axis=1), NN, preferred_element_type=jnp.float32
        )
        for m in range(p.nm):
            here = shift[:, m * LANES : (m + 1) * LANES].reshape(w, ROWS, LANES)
            here = vv[m][:, cols].astype(jnp.float32) - here
            out[m * w : (m + 1) * w, cols] = here.astype(jnp.bfloat16)
        here = shift[:, p.nm * LANES :].reshape(w, ROWS, p.tail_width)
        source = vv[p.nm][:, cols].astype(jnp.float32) - here
        source = source.reshape(p.nt, p.per_row, ROWS, p.tail_width)
        rest = jnp.zeros((p.nt, ROWS, LANES), jnp.float32)
        for s in range(p.per_row):
            turn = lax.rem(s * p.slot - j * p.tail + 2 * p.tail_width, p.tail_width)
            moved = pltpu.roll(source[:, s].reshape(p.nt * ROWS, p.tail_width), turn, 1)
            moved = moved[:, :LANES].reshape(p.nt, ROWS, LANES)
            keep = (lane >= s * p.slot) & (lane < s * p.slot + p.tail)
            rest = jnp.where(keep, moved, rest)
        out[p.nm * w :, cols] = rest.astype(jnp.bfloat16)


def dress(p, offset, z, spread, chol_vv, chol_ov):
    def specs(lead):
        found = []
        for m in range(p.nm):
            found.append(
                pl.BlockSpec(
                    (lead, p.cpad, LANES),
                    lambda i, z, m=m: (0, 0, lax.rem(z[0] + offset, p.js) * p.nm + m),
                )
            )
        found.append(
            pl.BlockSpec(
                (lead, p.cpad, p.tail_width),
                lambda i, z: (0, 0, p.tail_from // p.tail_width),
            )
        )
        return found

    count = p.nm + 1
    return pl.pallas_call(
        functools.partial(dress_kernel, p, offset),
        out_shape=jax.ShapeDtypeStruct((p.planes, p.cpad, LANES), jnp.bfloat16),
        grid_spec=pltpu.PrefetchScalarGridSpec(
            num_scalar_prefetch=1,
            grid=(1,),
            in_specs=[pl.BlockSpec((p.window * ROWS, p.occupied * ROWS), lambda i, z: (0, 0))]
            + specs(p.occupied)
            + specs(p.window),
            out_specs=pl.BlockSpec((p.planes, p.cpad, LANES), lambda i, z: (0, 0, 0)),
        ),
        compiler_params=pltpu.CompilerParams(vmem_limit_bytes=48 * 2**20),
        cost_estimate=pl.CostEstimate(
            flops=2 * p.window * p.occupied * p.cpad * LANES * count * ROWS,
            bytes_accessed=2 * (p.occupied + 2 * p.window) * p.cpad * LANES * count,
            transcendentals=0,
        ),
        name="dress",
    )(z, spread, *([chol_ov] * count), *([chol_vv] * count))


def relayout_kernel(p, in_ref, out_ref):
    rows = ROWS * ROWS
    to = lax.broadcasted_iota(jnp.int32, (rows, rows), 0)
    frm = lax.broadcasted_iota(jnp.int32, (rows, rows), 1)
    turn = (to % ROWS * ROWS + to // ROWS == frm).astype(jnp.float32).astype(jnp.bfloat16)
    for low in range(0, p.ij, ROWS):
        block = in_ref[low : low + ROWS].reshape(rows, p.d)
        turned = lax.dot_general(turn, block, NN, preferred_element_type=jnp.float32)
        out_ref[:, low : low + ROWS] = turned.astype(jnp.bfloat16).reshape(ROWS, ROWS, p.d)


def relayout(p, amplitudes, part):
    count = p.c // AMPS
    blocks = count // ROWS
    return pl.pallas_call(
        functools.partial(relayout_kernel, p),
        out_shape=jax.ShapeDtypeStruct((count, p.ij, p.d), jnp.bfloat16),
        grid=(blocks,),
        in_specs=[pl.BlockSpec((p.ij, ROWS, p.d), lambda c: (0, part * blocks + c, 0))],
        out_specs=pl.BlockSpec((ROWS, p.ij, p.d), lambda c: (c, 0, 0)),
        compiler_params=pltpu.CompilerParams(vmem_limit_bytes=40 * 2**20),
        cost_estimate=pl.CostEstimate(
            flops=2 * count * p.ij * p.d * ROWS * ROWS,
            bytes_accessed=4 * count * p.ij * p.d,
            transcendentals=0,
        ),
        name="relayout",
    )(amplitudes)


def ladder_kernel(p, group, place_ref, blocks_ref, *refs):
    count = p.js * p.xs * CORES
    pieces, amps, out = refs[:count], refs[count : count + AMPS], refs[count + AMPS]
    scratch = refs[count + AMPS + 1 :]
    vectors, left, strided, tiles, held, total, piece_sem, amp_sem = scratch
    w, z, core, chunk = p.window, place_ref[0], place_ref[1], place_ref[2]
    quads = p.c // QUAD
    width = QUAD * p.ij
    steps = quads // group
    spans = [slice(low, min(low + DEEP, p.d)) for low in range(0, p.d, DEEP)]

    def fetches(span):
        rows = p.c * p.ij // AMPS
        return [
            pltpu.make_async_copy(
                amp.at[:, span],
                held.at[n * rows : (n + 1) * rows, : span.stop - span.start],
                amp_sem.at[n],
            )
            for n, amp in enumerate(amps)
        ]

    copies = []
    for o in range(p.js):
        for r in range(p.xs):
            for other in range(CORES):
                parity = core if other == 0 else 1 - core
                origin = CORES * lax.rem(z - o + p.js, p.js) + parity
                row = pl.multiple_of(origin * p.cpad, ROWS)
                number = (o * p.xs + r) * CORES + other
                copies.append(
                    pltpu.make_async_copy(
                        pieces[number],
                        vectors.at[:, pl.ds(row, p.cpad), r * LANES : (r + 1) * LANES],
                        piece_sem.at[number],
                    )
                )
    for copy in copies:
        copy.start()
    total[...] = jnp.zeros_like(total)
    for copy in copies:
        copy.wait()

    first = pl.multiple_of(chunk * p.c, ROWS)
    lane = lax.broadcasted_iota(jnp.int32, (p.c, LANES), 1)

    @pl.loop(0, p.blocks)
    def _(b):
        for r in range(p.xs):
            span = slice(r * LANES, (r + 1) * LANES)
            for m in range(p.nm + 1):
                for e in range(BLK):
                    index = b * BLK + e
                    plane = m * w + index if m < p.nm else m * w + index // p.per_row
                    rows = vectors[plane, pl.ds(first, p.c), span].astype(jnp.float32)
                    if m == p.nm:
                        rows = jnp.where(lane // p.slot == index % p.per_row, rows, 0.0)
                        turn = p.slot
                        while turn < LANES:
                            rows += pltpu.roll(rows, turn, 1)
                            turn *= 2
                    strided[pl.ds(e, p.c, stride=BLK), :] = rows
                at = slice((m * p.xs + r) * LANES, (m * p.xs + r + 1) * LANES)
                left[b, :, at] = strided[...].astype(jnp.bfloat16)

    slot_of = lax.broadcasted_iota(jnp.int32, (1, p.k), 1) % LANES // p.slot

    for span in spans:
        size = span.stop - span.start
        for copy in fetches(span):
            copy.start()

        @pl.loop(0, p.gf)
        def _(gf):
            block = blocks_ref[gf // BLK, 0]
            index = blocks_ref[gf // BLK, 1] * BLK + gf % BLK
            only = (slot_of == index % p.per_row).astype(jnp.float32).astype(jnp.bfloat16)
            rhs = [vectors[m * w + index, span] for m in range(p.nm)]
            rhs.append(vectors[p.nm * w + index // p.per_row, span] * only)
            tile = lax.dot_general(
                left[block], jnp.concatenate(rhs, axis=1), NT, preferred_element_type=jnp.float32
            )
            tiles[:, gf, :, :size] = tile.astype(jnp.bfloat16).reshape(quads, ROWS, size)

        for copy in fetches(span):
            copy.wait()

        @pl.loop(0, steps)
        def _(step):
            lhs = [
                tiles[step * group + n, :, :, :size].reshape(p.gf * ROWS, size)
                for n in range(group)
            ]
            low = pl.multiple_of(step * group * width, width)
            rhs = [held[pl.ds(low + n * width, width), :size] for n in range(group)]
            total[...] += lax.dot_general(
                jnp.concatenate(lhs, axis=1),
                jnp.concatenate(rhs, axis=1),
                NT,
                preferred_element_type=jnp.float32,
            )

    row = lax.broadcasted_iota(jnp.int32, (p.gf * ROWS, width), 0) % ROWS // BLK
    col = lax.broadcasted_iota(jnp.int32, (p.gf * ROWS, width), 1) // p.ij
    kept = jnp.where(row == col, total[...], 0.0)
    folded = kept[:, :LANES]
    for low in range(LANES, width, LANES):
        folded += kept[:, low : low + LANES]
    shift = LANES
    while shift > p.ij:
        shift //= 2
        folded += pltpu.roll(folded, shift, 1)
    folded = folded.reshape(p.gf, 2, 8, LANES).sum(axis=1)
    out[...] = folded[:, :4] + folded[:, 4:]


def ladder(p, place, blocks, pieces, amps):
    quads = p.c // QUAD
    group = 4 if quads % 4 == 0 else 2
    width = QUAD * p.ij
    return pl.pallas_call(
        functools.partial(ladder_kernel, p, group),
        out_shape=jax.ShapeDtypeStruct((p.gf, BLK, LANES), jnp.float32),
        in_specs=[pl.BlockSpec(memory_space=pltpu.SMEM)] * 2
        + [pl.BlockSpec(memory_space=pl.ANY)] * (len(pieces) + AMPS),
        out_specs=pl.BlockSpec(memory_space=pltpu.VMEM),
        scratch_shapes=[
            pltpu.VMEM((p.planes, p.d, p.k), jnp.bfloat16),
            pltpu.VMEM((p.blocks, BLK * p.c, (p.nm + 1) * p.k), jnp.bfloat16),
            pltpu.VMEM((BLK * p.c, LANES), jnp.float32),
            pltpu.VMEM((quads, p.gf, ROWS, DEEP), jnp.bfloat16),
            pltpu.VMEM((p.c * p.ij, DEEP), jnp.bfloat16),
            pltpu.VMEM((p.gf * ROWS, width), jnp.float32),
            pltpu.SemaphoreType.DMA((len(pieces),)),
            pltpu.SemaphoreType.DMA((AMPS,)),
        ],
        compiler_params=pltpu.CompilerParams(vmem_limit_bytes=60 * 2**20),
        cost_estimate=pl.CostEstimate(
            flops=2 * p.gf * BLK * p.c * p.d * p.k,
            bytes_accessed=2 * (p.planes * p.d * p.k + p.c * p.ij * p.d),
            transcendentals=0,
        ),
        name="ladder",
    )(place, blocks, *pieces, *amps)


def pad_columns(array, axis, cols, cpad):
    if cols == cpad:
        return array
    shape = array.shape
    split = array.reshape(shape[:axis] + (shape[axis] // cols, cols) + shape[axis + 1 :])
    widths = [(0, 0)] * split.ndim
    widths[axis + 1] = (0, cpad - cols)
    split = jnp.pad(split, widths)
    return split.reshape(shape[:axis] + (shape[axis] // cols * cpad,) + shape[axis + 1 :])


def shards(chol_vv, chol_ov, t1_window, amplitudes, assignment):
    window, cols, aux_dev = chol_vv.shape
    n_aux, n_pair = lax.axis_size("aux"), lax.axis_size("pair")
    p = Plan(window, chol_ov.shape[0], cols, aux_dev, n_aux, n_pair, amplitudes.shape[0])
    me_aux, me_pair = lax.axis_index("aux"), lax.axis_index("pair")
    z = me_pair // CORES
    place = jnp.stack([z, me_aux % CORES, me_aux]).astype(jnp.int32)

    chol_vv = pad_columns(chol_vv, 1, cols, p.cpad)
    chol_ov = pad_columns(chol_ov, 1, cols, p.cpad)
    spread = spread_amplitudes(p, t1_window)

    def permute(array, target):
        pairs = []
        for a in range(n_aux):
            for q in range(n_pair):
                to_a, to_q = target(a, q)
                pairs.append((a * n_pair + q, to_a * n_pair + to_q))
        return lax.ppermute(array, ("aux", "pair"), pairs)

    def to_slice(array, o):
        return permute(
            array,
            lambda a, q: (
                a // CORES * CORES + q % CORES,
                CORES * ((q // CORES + o) % p.js) + a % CORES,
            ),
        )

    def along_x(array, r):
        return permute(array, lambda a, q: (CORES * ((a // CORES + r) % p.xs) + a % CORES, q))

    def to_core(array):
        return permute(array, lambda a, q: (a ^ 1, q))

    amplitudes = pad_columns(pad_columns(amplitudes, 1, cols, p.cpad), 2, cols, p.cpad)

    groups = [sorted({n, (p.js - n) % p.js}) for n in range(p.js // 2 + 1)]
    messages = {0: dress(p, 0, place, spread, chol_vv, chol_ov)}
    messages, spread = lax.optimization_barrier((messages, spread))
    own, turned, shared, amps = {}, {}, {}, []
    for n in range(len(groups) + 2):
        new_own, new_turned, new_shared, work, new_amps = {}, {}, {}, {}, []
        if n < len(groups):
            for o in groups[n]:
                new_own[o] = to_slice(messages[o], o)
        if 1 <= n <= len(groups):
            for o in groups[n - 1]:
                for r in range(1, p.xs):
                    new_turned[o, r] = along_x(own[o], r)
            for o in groups[n - 1]:
                new_shared[o, 0] = to_core(own[o])
        if n >= 2:
            for o in groups[n - 2]:
                for r in range(1, p.xs):
                    new_shared[o, r] = to_core(turned[o, r])
        if n + 1 < len(groups):
            for o in groups[n + 1]:
                work[o] = dress(p, o, place, spread, chol_vv, chol_ov)
        if n == len(groups) - 1:
            new_amps = [relayout(p, amplitudes, part) for part in range(AMPS)]
        moved = (new_own, new_turned, new_shared, work, new_amps)
        everything = (moved, own, turned, shared, amps, spread, amplitudes)
        moved, own, turned, shared, amps, spread, amplitudes = lax.optimization_barrier(everything)
        own.update(moved[0])
        turned.update(moved[1])
        shared.update(moved[2])
        messages = moved[3]
        amps = amps or moved[4]
    amps = [amp.reshape(-1, p.d) for amp in amps]
    pieces = []
    for o in range(p.js):
        for r in range(p.xs):
            pieces += [turned[o, r] if r else own[o], shared[o, r]]

    partial_terms = ladder(p, place, assignment, pieces, amps)
    share = p.ij // n_aux
    terms = partial_terms[:, :, : p.ij].reshape(n_pair, BLK, BLK, n_aux, share)
    terms = terms.transpose(3, 0, 4, 2, 1).reshape(n_aux * n_pair, share, BLK * BLK)
    terms = lax.all_to_all(terms, ("aux", "pair"), split_axis=0, concat_axis=0, tiled=True)
    return terms.sum(axis=0)


def solution(mesh):
    in_specs = (P(None, "pair", "aux"), P(None, "pair", "aux"), P(), P(None, "aux", None), P())
    out_specs = P("aux", "pair")
    return jax.shard_map(shards, mesh=mesh, in_specs=in_specs, out_specs=out_specs, check_vma=False)
```

```python
import functools

import jax
import jax.numpy as jnp
from jax import lax
from jax.experimental import pallas as pl
from jax.experimental.pallas import tpu as pltpu
from jax.sharding import PartitionSpec as P

BLK = 4
QUAD = 4
AMPS = 2
SLOTS = 3
ROWS = 16
LANES = 128
CORES = 2
NT = (((1,), (1,)), ((), ()))
NN = (((1,), (0,)), ((), ()))


def round_up(value, unit):
    return (value + unit - 1) // unit * unit


class Plan:
    def __init__(self, window, occupied, cols, aux_dev, n_aux, n_pair, pairs_all):
        self.window, self.occupied, self.cols, self.aux_dev = window, occupied, cols, aux_dev
        self.n_aux, self.n_pair, self.ij = n_aux, n_pair, pairs_all
        self.xs = n_aux // CORES
        self.js = n_pair // CORES
        self.cpad = round_up(cols, ROWS)
        chunk = aux_dev // self.js
        self.main = chunk // LANES * LANES
        self.tail = chunk - self.main
        self.slot = 1
        while self.slot < self.tail:
            self.slot *= 2
        self.per_row = LANES // self.slot
        self.nm = self.main // LANES
        self.nt = window // self.per_row
        self.planes = self.nm * window + self.nt
        self.per = n_pair // n_aux
        self.c = self.per * self.cpad
        self.d = n_pair * self.cpad
        self.k = self.xs * LANES
        self.groups = n_pair
        self.blocks = window // BLK
        self.gf = self.groups * BLK
        self.tail_from = self.js * self.main
        self.tail_width = round_up(self.js * self.tail, LANES)


def spread_kernel(p, t1_ref, out_ref):
    def repeat(rows, cols, per_row, per_col):
        row = lax.broadcasted_iota(jnp.int32, (rows, cols), 0) // per_row
        col = lax.broadcasted_iota(jnp.int32, (rows, cols), 1) // per_col
        return (row == col).astype(jnp.float32).astype(jnp.bfloat16)

    rows, cols = p.window * ROWS, p.occupied * ROWS
    tall = lax.dot_general(
        repeat(rows, p.window, ROWS, 1), t1_ref[...], NT, preferred_element_type=jnp.float32
    ).astype(jnp.bfloat16)
    full = jnp.dot(
        tall, repeat(p.occupied, cols, 1, ROWS), preferred_element_type=jnp.float32
    )
    row = lax.broadcasted_iota(jnp.int32, (rows, cols), 0) % ROWS
    col = lax.broadcasted_iota(jnp.int32, (rows, cols), 1) % ROWS
    out_ref[...] = jnp.where(row == col, full, 0.0).astype(jnp.bfloat16)


def spread_amplitudes(p, t1_window):
    return pl.pallas_call(
        functools.partial(spread_kernel, p),
        out_shape=jax.ShapeDtypeStruct((p.window * ROWS, p.occupied * ROWS), jnp.bfloat16),
        compiler_params=pltpu.CompilerParams(vmem_limit_bytes=48 * 2**20),
        name="spread",
    )(t1_window)


def dress_kernel(p, offset, z_ref, a_ref, *refs):
    ov, vv, out = refs[: p.nm + 1], refs[p.nm + 1 : 2 * p.nm + 2], refs[-1]
    w = p.window
    j = lax.rem(z_ref[0] + offset, p.js)
    lane = lax.broadcasted_iota(jnp.int32, (p.nt, ROWS, LANES), 2)
    for low in range(0, p.cpad, ROWS):
        cols = slice(low, low + ROWS)
        vectors = [ref[:, cols].reshape(p.occupied * ROWS, -1) for ref in ov]
        shift = lax.dot_general(
            a_ref[...], jnp.concatenate(vectors, axis=1), NN, preferred_element_type=jnp.float32
        )
        for m in range(p.nm):
            here = shift[:, m * LANES : (m + 1) * LANES].reshape(w, ROWS, LANES)
            here = vv[m][:, cols].astype(jnp.float32) - here
            out[m * w : (m + 1) * w, cols] = here.astype(jnp.bfloat16)
        here = shift[:, p.nm * LANES :].reshape(w, ROWS, p.tail_width)
        source = vv[p.nm][:, cols].astype(jnp.float32) - here
        source = source.reshape(p.nt, p.per_row, ROWS, p.tail_width)
        rest = jnp.zeros((p.nt, ROWS, LANES), jnp.float32)
        for s in range(p.per_row):
            turn = lax.rem(s * p.slot - j * p.tail + 2 * p.tail_width, p.tail_width)
            moved = pltpu.roll(source[:, s].reshape(p.nt * ROWS, p.tail_width), turn, 1)
            moved = moved[:, :LANES].reshape(p.nt, ROWS, LANES)
            keep = (lane >= s * p.slot) & (lane < s * p.slot + p.tail)
            rest = jnp.where(keep, moved, rest)
        out[p.nm * w :, cols] = rest.astype(jnp.bfloat16)


def dress(p, offset, z, spread, chol_vv, chol_ov):
    def specs(lead):
        found = []
        for m in range(p.nm):
            found.append(
                pl.BlockSpec(
                    (lead, p.cpad, LANES),
                    lambda i, z, m=m: (0, 0, lax.rem(z[0] + offset, p.js) * p.nm + m),
                )
            )
        found.append(
            pl.BlockSpec(
                (lead, p.cpad, p.tail_width),
                lambda i, z: (0, 0, p.tail_from // p.tail_width),
            )
        )
        return found

    count = p.nm + 1
    return pl.pallas_call(
        functools.partial(dress_kernel, p, offset),
        out_shape=jax.ShapeDtypeStruct((p.planes, p.cpad, LANES), jnp.bfloat16),
        grid_spec=pltpu.PrefetchScalarGridSpec(
            num_scalar_prefetch=1,
            grid=(1,),
            in_specs=[pl.BlockSpec((p.window * ROWS, p.occupied * ROWS), lambda i, z: (0, 0))]
            + specs(p.occupied)
            + specs(p.window),
            out_specs=pl.BlockSpec((p.planes, p.cpad, LANES), lambda i, z: (0, 0, 0)),
        ),
        compiler_params=pltpu.CompilerParams(vmem_limit_bytes=48 * 2**20),
        cost_estimate=pl.CostEstimate(
            flops=2 * p.window * p.occupied * p.cpad * LANES * count * ROWS,
            bytes_accessed=2 * (p.occupied + 2 * p.window) * p.cpad * LANES * count,
            transcendentals=0,
        ),
        name="dress",
    )(z, spread, *([chol_ov] * count), *([chol_vv] * count))


def relayout_kernel(p, in_ref, out_ref):
    rows = ROWS * ROWS
    to = lax.broadcasted_iota(jnp.int32, (rows, rows), 0)
    frm = lax.broadcasted_iota(jnp.int32, (rows, rows), 1)
    turn = (to % ROWS * ROWS + to // ROWS == frm).astype(jnp.float32).astype(jnp.bfloat16)
    for low in range(0, p.ij, ROWS):
        block = in_ref[low : low + ROWS].reshape(rows, p.d)
        turned = lax.dot_general(turn, block, NN, preferred_element_type=jnp.float32)
        out_ref[:, low : low + ROWS] = turned.astype(jnp.bfloat16).reshape(ROWS, ROWS, p.d)


def relayout(p, amplitudes, part):
    count = p.c // AMPS
    blocks = count // ROWS
    return pl.pallas_call(
        functools.partial(relayout_kernel, p),
        out_shape=jax.ShapeDtypeStruct((count, p.ij, p.d), jnp.bfloat16),
        grid=(blocks,),
        in_specs=[pl.BlockSpec((p.ij, ROWS, p.d), lambda c: (0, part * blocks + c, 0))],
        out_specs=pl.BlockSpec((ROWS, p.ij, p.d), lambda c: (c, 0, 0)),
        compiler_params=pltpu.CompilerParams(vmem_limit_bytes=40 * 2**20),
        cost_estimate=pl.CostEstimate(
            flops=2 * count * p.ij * p.d * ROWS * ROWS,
            bytes_accessed=4 * count * p.ij * p.d,
            transcendentals=0,
        ),
        name="relayout",
    )(amplitudes)


def ladder_kernel(p, units, parts, group, place_ref, blocks_ref, *refs):
    count = len(units) * p.xs * CORES
    pieces, amps, out = refs[:count], refs[count : count + AMPS], refs[count + AMPS]
    scratch = refs[count + AMPS + 1 :]
    vectors, left_main, left_tail, spread_tail, tiles, held, total, piece_sem, amp_sem = scratch
    w, z, core, chunk = p.window, place_ref[0], place_ref[1], place_ref[2]
    quads = p.c // QUAD
    here = quads // parts
    rows = here * ROWS
    steps = here // group
    wide = group * QUAD * p.ij
    each = parts * steps // AMPS

    class Fetch:
        def __init__(self, step, slot):
            self.step, self.slot = step, slot

        def copy(self, amp, step):
            at = pl.ds(pl.multiple_of(step * wide, wide), wide)
            return pltpu.make_async_copy(amp.at[at], held.at[self.slot], amp_sem.at[self.slot])

        def start(self):
            for n, amp in enumerate(amps):

                @pl.when(self.step // each == n)
                def _():
                    self.copy(amp, self.step - n * each).start()

        def wait(self):
            self.copy(amps[0], 0).wait()

    copies = []
    for n, (o, low, high) in enumerate(units):
        for r in range(p.xs):
            for other in range(CORES):
                parity = core if other == 0 else 1 - core
                origin = CORES * lax.rem(z - o + p.js, p.js) + parity
                row = pl.multiple_of(origin * p.cpad, ROWS)
                number = (n * p.xs + r) * CORES + other
                copies.append(
                    pltpu.make_async_copy(
                        pieces[number],
                        vectors.at[
                            low:high, pl.ds(row, p.cpad), r * LANES : (r + 1) * LANES
                        ],
                        piece_sem.at[number],
                    )
                )
    for copy in copies:
        copy.start()
    for ahead in range(min(SLOTS - 1, parts * steps)):
        Fetch(jnp.int32(ahead), ahead).start()
    for copy in copies:
        copy.wait()

    mixed = QUAD * ROWS
    to = lax.broadcasted_iota(jnp.int32, (mixed, mixed), 0)
    frm = lax.broadcasted_iota(jnp.int32, (mixed, mixed), 1)
    weave = ((to % BLK) * ROWS + to // BLK == frm).astype(jnp.float32).astype(jnp.bfloat16)
    lane_in = lax.broadcasted_iota(jnp.int32, (LANES, LANES), 0)
    lane_out = lax.broadcasted_iota(jnp.int32, (LANES, LANES), 1)
    same = lane_in % p.slot == lane_out % p.slot
    first = pl.multiple_of(chunk * p.c, ROWS)

    def woven(stack):
        return lax.dot_general(weave, stack, NN, preferred_element_type=jnp.float32).astype(
            jnp.bfloat16
        )

    @pl.loop(0, p.blocks)
    def _(b):
        for e in range(BLK):
            index = b * BLK + e
            plane = p.nm * w + index // p.per_row
            copier = (same & (lane_in // p.slot == index % p.per_row)).astype(jnp.float32)
            copier = copier.astype(jnp.bfloat16)
            for r in range(p.xs):
                span = slice(r * LANES, (r + 1) * LANES)
                spread_tail[e, :, span] = lax.dot_general(
                    vectors[plane, pl.ds(first, p.c), span],
                    copier,
                    NN,
                    preferred_element_type=jnp.float32,
                ).astype(jnp.bfloat16)
        for i in range(p.c // ROWS):
            span = slice(i * mixed, (i + 1) * mixed)
            tail = [spread_tail[e, i * ROWS : (i + 1) * ROWS, :] for e in range(BLK)]
            left_tail[b, span] = woven(jnp.concatenate(tail, axis=0))
            for m in range(p.nm):
                at = pl.ds(pl.multiple_of(first + i * ROWS, ROWS), ROWS)
                stack = [vectors[m * w + b * BLK + e, at] for e in range(BLK)]
                left_main[m, b, span] = woven(jnp.concatenate(stack, axis=0))

    total[...] = jnp.zeros_like(total)
    slot_of = lax.broadcasted_iota(jnp.int32, (1, p.k), 1) % LANES // p.slot

    @pl.loop(0, parts)
    def _(part):
        part_rows = pl.ds(pl.multiple_of(part * rows, rows), rows)

        @pl.loop(0, p.gf)
        def _(gf):
            left = blocks_ref[gf // BLK, 0]
            index = blocks_ref[gf // BLK, 1] * BLK + gf % BLK
            only = (slot_of == index % p.per_row).astype(jnp.float32).astype(jnp.bfloat16)
            lhs = [left_main[m, left, part_rows] for m in range(p.nm)]
            lhs = jnp.concatenate(lhs + [left_tail[left, part_rows]], axis=1)
            for low in range(0, p.d, 256):
                span = slice(low, min(low + 256, p.d))
                rhs = [vectors[m * w + index, span] for m in range(p.nm)]
                rhs.append(vectors[p.nm * w + index // p.per_row, span] * only)
                rhs = jnp.concatenate(rhs, axis=1)
                block = lax.dot_general(lhs, rhs, NT, preferred_element_type=jnp.float32)
                block = block.astype(jnp.bfloat16).reshape(here, ROWS, span.stop - low)
                tiles[:, gf, :, span] = block

        @pl.loop(0, steps)
        def _(step):
            at = part * steps + step
            slot = lax.rem(at, SLOTS)

            @pl.when(at + SLOTS - 1 < parts * steps)
            def _():
                Fetch(at + SLOTS - 1, lax.rem(at + SLOTS - 1, SLOTS)).start()

            Fetch(at, slot).wait()
            width = QUAD * p.ij
            for n in range(group):
                total[...] += lax.dot_general(
                    tiles[step * group + n].reshape(p.gf * ROWS, p.d),
                    held[slot, n * width : (n + 1) * width],
                    NT,
                    preferred_element_type=jnp.float32,
                )

    width = QUAD * p.ij
    row = lax.broadcasted_iota(jnp.int32, (p.gf * ROWS, width), 0) % ROWS // BLK
    col = lax.broadcasted_iota(jnp.int32, (p.gf * ROWS, width), 1) // p.ij
    kept = jnp.where(row == col, total[...], 0.0)
    folded = kept[:, :LANES]
    for low in range(LANES, width, LANES):
        folded += kept[:, low : low + LANES]
    shift = LANES
    while shift > p.ij:
        shift //= 2
        folded += pltpu.roll(folded, shift, 1)
    folded = folded.reshape(p.gf, 2, 8, LANES).sum(axis=1)
    out[...] = folded[:, :4] + folded[:, 4:]


def ladder(p, units, place, blocks, pieces, amps):
    parts, group = 2, 1
    quads = p.c // QUAD
    for wanted in (4, 2):
        if quads // parts % wanted == 0:
            group = wanted
            break
    width = QUAD * p.ij
    return pl.pallas_call(
        functools.partial(ladder_kernel, p, units, parts, group),
        out_shape=jax.ShapeDtypeStruct((p.gf, BLK, LANES), jnp.float32),
        in_specs=[pl.BlockSpec(memory_space=pltpu.SMEM)] * 2
        + [pl.BlockSpec(memory_space=pl.ANY)] * (len(pieces) + AMPS),
        out_specs=pl.BlockSpec(memory_space=pltpu.VMEM),
        scratch_shapes=[
            pltpu.VMEM((p.planes, p.d, p.k), jnp.bfloat16),
            pltpu.VMEM((max(p.nm, 1), p.blocks, BLK * p.c if p.nm else ROWS, p.k), jnp.bfloat16),
            pltpu.VMEM((p.blocks, BLK * p.c, p.k), jnp.bfloat16),
            pltpu.VMEM((BLK, p.c, p.k), jnp.bfloat16),
            pltpu.VMEM((quads // parts, p.gf, ROWS, p.d), jnp.bfloat16),
            pltpu.VMEM((SLOTS, group * width, p.d), jnp.bfloat16),
            pltpu.VMEM((p.gf * ROWS, width), jnp.float32),
            pltpu.SemaphoreType.DMA((len(pieces),)),
            pltpu.SemaphoreType.DMA((SLOTS,)),
        ],
        compiler_params=pltpu.CompilerParams(vmem_limit_bytes=60 * 2**20),
        cost_estimate=pl.CostEstimate(
            flops=2 * p.gf * BLK * p.c * p.d * p.k,
            bytes_accessed=2 * (p.js * p.n_aux * p.planes * p.cpad * LANES + p.c * p.ij * p.d),
            transcendentals=0,
        ),
        name="ladder",
    )(place, blocks, *pieces, *amps)


def pad_columns(array, axis, cols, cpad):
    if cols == cpad:
        return array
    shape = array.shape
    split = array.reshape(shape[:axis] + (shape[axis] // cols, cols) + shape[axis + 1 :])
    widths = [(0, 0)] * split.ndim
    widths[axis + 1] = (0, cpad - cols)
    split = jnp.pad(split, widths)
    return split.reshape(shape[:axis] + (shape[axis] // cols * cpad,) + shape[axis + 1 :])


def shards(chol_vv, chol_ov, t1_window, amplitudes, assignment):
    window, cols, aux_dev = chol_vv.shape
    n_aux, n_pair = lax.axis_size("aux"), lax.axis_size("pair")
    p = Plan(window, chol_ov.shape[0], cols, aux_dev, n_aux, n_pair, amplitudes.shape[0])
    me_aux, me_pair = lax.axis_index("aux"), lax.axis_index("pair")
    z = me_pair // CORES
    place = jnp.stack([z, me_aux % CORES, me_aux]).astype(jnp.int32)

    chol_vv = pad_columns(chol_vv, 1, cols, p.cpad)
    chol_ov = pad_columns(chol_ov, 1, cols, p.cpad)
    spread = spread_amplitudes(p, t1_window)

    def permute(array, target):
        pairs = []
        for a in range(n_aux):
            for q in range(n_pair):
                to_a, to_q = target(a, q)
                pairs.append((a * n_pair + q, to_a * n_pair + to_q))
        return lax.ppermute(array, ("aux", "pair"), pairs)

    def to_slice(array, o):
        return permute(
            array,
            lambda a, q: (
                a // CORES * CORES + q % CORES,
                CORES * ((q // CORES + o) % p.js) + a % CORES,
            ),
        )

    def along_x(array, r):
        return permute(array, lambda a, q: (CORES * ((a // CORES + r) % p.xs) + a % CORES, q))

    def to_core(array):
        return permute(array, lambda a, q: (a ^ 1, q))

    amplitudes = pad_columns(pad_columns(amplitudes, 1, cols, p.cpad), 2, cols, p.cpad)

    order = sorted(range(p.js), key=lambda o: min(o, p.js - o))
    units = [(o, 0, p.planes) for o in order]
    if p.js > 2:
        half = p.planes // 2
        units[-1:] = [(order[-1], 0, half), (order[-1], half, p.planes)]
        rounds = [[units[1], units[0]]] + [[unit] for unit in units[2:]]
        swaps = [[units[0]], [units[1]]] + [[unit] for unit in units[2:-2]] + [units[-2:]]
    else:
        rounds, swaps = [units], [units]

    def make(o, spread):
        return dress(p, o, place, spread, chol_vv, chol_ov)

    def cut(message, unit):
        if unit[1:] == (0, p.planes):
            return message
        return message[unit[1] : unit[2]]

    messages = {}
    for o, _, _ in rounds[0]:
        messages[o] = make(o, spread)
        messages[o], spread = lax.optimization_barrier((messages[o], spread))
    amps = [None] * AMPS
    sources = [amplitudes] * AMPS
    held = {}
    share_next = []
    count = max(len(rounds), len(swaps) + 1) + 1
    for n in range(count):
        new, made, laid = {}, {}, {}
        to_share, share_next = share_next, []
        if n < len(rounds):
            for unit in rounds[n]:
                new[unit, 0, 0] = to_slice(cut(messages[unit[0]], unit), unit[0])
                share_next.append((unit, 0))
        if 1 <= n <= len(swaps):
            for unit in swaps[n - 1]:
                for r in range(1, p.xs):
                    new[unit, r, 0] = along_x(held[unit, 0, 0], r)
                    share_next.append((unit, r))
        for unit, r in to_share:
            new[unit, r, 1] = to_core(held[unit, r, 0])
        if n + 1 < len(rounds):
            for o, _, _ in rounds[n + 1]:
                if o not in messages:
                    made[o] = make(o, spread)
        part = n - (len(swaps) - AMPS)
        if 0 <= part < AMPS:
            laid[part] = relayout(p, sources[part], part)
        moved = (list(new.values()), list(made.values()), list(laid.values()))
        kept = (list(held.values()), spread, sources)
        moved, (old, spread, sources) = lax.optimization_barrier((moved, kept))
        held = dict(zip(held, old))
        held.update(zip(new, moved[0]))
        messages.update(zip(made, moved[1]))
        for part, amp in zip(laid, moved[2]):
            amps[part] = amp
    amps = [amp.reshape(-1, p.d) for amp in amps]
    pieces = [
        held[unit, r, other] for unit in units for r in range(p.xs) for other in range(CORES)
    ]

    partial_terms = ladder(p, units, place, assignment, pieces, amps)
    share = p.ij // n_aux
    terms = partial_terms[:, :, : p.ij].reshape(n_pair, BLK, BLK, n_aux, share)
    terms = terms.transpose(3, 0, 4, 2, 1).reshape(n_aux * n_pair, share, BLK * BLK)
    terms = lax.all_to_all(terms, ("aux", "pair"), split_axis=0, concat_axis=0, tiled=True)
    return terms.sum(axis=0)


def solution(mesh):
    in_specs = (P(None, "pair", "aux"), P(None, "pair", "aux"), P(), P(None, "aux", None), P())
    out_specs = P("aux", "pair")
    return jax.shard_map(shards, mesh=mesh, in_specs=in_specs, out_specs=out_specs, check_vma=False)
```

```python
import functools

import jax
import jax.numpy as jnp
from jax import lax
from jax.experimental import pallas as pl
from jax.experimental.pallas import tpu as pltpu
from jax.sharding import PartitionSpec as P

BLK = 4
QUAD = 4
AMPS = 2
SLOTS = 3
ROWS = 16
LANES = 128
CORES = 2
NT = (((1,), (1,)), ((), ()))
NN = (((1,), (0,)), ((), ()))


def round_up(value, unit):
    return (value + unit - 1) // unit * unit


class Plan:
    def __init__(self, window, occupied, cols, aux_dev, n_aux, n_pair, pairs_all):
        self.window, self.occupied, self.cols, self.aux_dev = window, occupied, cols, aux_dev
        self.n_aux, self.n_pair, self.ij = n_aux, n_pair, pairs_all
        self.xs = n_aux // CORES
        self.js = n_pair // CORES
        self.cpad = round_up(cols, ROWS)
        chunk = aux_dev // self.js
        self.main = chunk // LANES * LANES
        self.tail = chunk - self.main
        self.slot = 1
        while self.slot < self.tail:
            self.slot *= 2
        self.per_row = LANES // self.slot
        self.nm = self.main // LANES
        self.nt = window // self.per_row
        self.planes = self.nm * window + self.nt
        self.per = n_pair // n_aux
        self.c = self.per * self.cpad
        self.d = n_pair * self.cpad
        self.k = self.xs * LANES
        self.groups = n_pair
        self.blocks = window // BLK
        self.gf = self.groups * BLK
        self.tail_from = self.js * self.main
        self.tail_width = round_up(self.js * self.tail, LANES)


def spread_kernel(p, t1_ref, out_ref):
    def repeat(rows, cols, per_row, per_col):
        row = lax.broadcasted_iota(jnp.int32, (rows, cols), 0) // per_row
        col = lax.broadcasted_iota(jnp.int32, (rows, cols), 1) // per_col
        return (row == col).astype(jnp.float32).astype(jnp.bfloat16)

    rows, cols = p.window * ROWS, p.occupied * ROWS
    tall = lax.dot_general(
        repeat(rows, p.window, ROWS, 1), t1_ref[...], NT, preferred_element_type=jnp.float32
    ).astype(jnp.bfloat16)
    full = jnp.dot(
        tall, repeat(p.occupied, cols, 1, ROWS), preferred_element_type=jnp.float32
    )
    row = lax.broadcasted_iota(jnp.int32, (rows, cols), 0) % ROWS
    col = lax.broadcasted_iota(jnp.int32, (rows, cols), 1) % ROWS
    out_ref[...] = jnp.where(row == col, full, 0.0).astype(jnp.bfloat16)


def spread_amplitudes(p, t1_window):
    return pl.pallas_call(
        functools.partial(spread_kernel, p),
        out_shape=jax.ShapeDtypeStruct((p.window * ROWS, p.occupied * ROWS), jnp.bfloat16),
        compiler_params=pltpu.CompilerParams(vmem_limit_bytes=48 * 2**20),
        name="spread",
    )(t1_window)


def dress_kernel(p, offset, z_ref, a_ref, *refs):
    ov, vv, out = refs[: p.nm + 1], refs[p.nm + 1 : 2 * p.nm + 2], refs[-1]
    w = p.window
    j = lax.rem(z_ref[0] + offset, p.js)
    lane = lax.broadcasted_iota(jnp.int32, (p.nt, ROWS, LANES), 2)
    for low in range(0, p.cpad, ROWS):
        cols = slice(low, low + ROWS)
        vectors = [ref[:, cols].reshape(p.occupied * ROWS, -1) for ref in ov]
        shift = lax.dot_general(
            a_ref[...], jnp.concatenate(vectors, axis=1), NN, preferred_element_type=jnp.float32
        )
        for m in range(p.nm):
            here = shift[:, m * LANES : (m + 1) * LANES].reshape(w, ROWS, LANES)
            here = vv[m][:, cols].astype(jnp.float32) - here
            out[m * w : (m + 1) * w, cols] = here.astype(jnp.bfloat16)
        here = shift[:, p.nm * LANES :].reshape(w, ROWS, p.tail_width)
        source = vv[p.nm][:, cols].astype(jnp.float32) - here
        source = source.reshape(p.nt, p.per_row, ROWS, p.tail_width)
        rest = jnp.zeros((p.nt, ROWS, LANES), jnp.float32)
        for s in range(p.per_row):
            turn = lax.rem(s * p.slot - j * p.tail + 2 * p.tail_width, p.tail_width)
            moved = pltpu.roll(source[:, s].reshape(p.nt * ROWS, p.tail_width), turn, 1)
            moved = moved[:, :LANES].reshape(p.nt, ROWS, LANES)
            keep = (lane >= s * p.slot) & (lane < s * p.slot + p.tail)
            rest = jnp.where(keep, moved, rest)
        out[p.nm * w :, cols] = rest.astype(jnp.bfloat16)


def dress(p, offset, z, spread, chol_vv, chol_ov):
    def specs(lead):
        found = []
        for m in range(p.nm):
            found.append(
                pl.BlockSpec(
                    (lead, p.cpad, LANES),
                    lambda i, z, m=m: (0, 0, lax.rem(z[0] + offset, p.js) * p.nm + m),
                )
            )
        found.append(
            pl.BlockSpec(
                (lead, p.cpad, p.tail_width),
                lambda i, z: (0, 0, p.tail_from // p.tail_width),
            )
        )
        return found

    count = p.nm + 1
    return pl.pallas_call(
        functools.partial(dress_kernel, p, offset),
        out_shape=jax.ShapeDtypeStruct((p.planes, p.cpad, LANES), jnp.bfloat16),
        grid_spec=pltpu.PrefetchScalarGridSpec(
            num_scalar_prefetch=1,
            grid=(1,),
            in_specs=[pl.BlockSpec((p.window * ROWS, p.occupied * ROWS), lambda i, z: (0, 0))]
            + specs(p.occupied)
            + specs(p.window),
            out_specs=pl.BlockSpec((p.planes, p.cpad, LANES), lambda i, z: (0, 0, 0)),
        ),
        compiler_params=pltpu.CompilerParams(vmem_limit_bytes=48 * 2**20),
        cost_estimate=pl.CostEstimate(
            flops=2 * p.window * p.occupied * p.cpad * LANES * count * ROWS,
            bytes_accessed=2 * (p.occupied + 2 * p.window) * p.cpad * LANES * count,
            transcendentals=0,
        ),
        name="dress",
    )(z, spread, *([chol_ov] * count), *([chol_vv] * count))


def relayout_kernel(p, in_ref, out_ref):
    rows = ROWS * ROWS
    to = lax.broadcasted_iota(jnp.int32, (rows, rows), 0)
    frm = lax.broadcasted_iota(jnp.int32, (rows, rows), 1)
    turn = (to % ROWS * ROWS + to // ROWS == frm).astype(jnp.float32).astype(jnp.bfloat16)
    for low in range(0, p.ij, ROWS):
        block = in_ref[low : low + ROWS].reshape(rows, p.d)
        turned = lax.dot_general(turn, block, NN, preferred_element_type=jnp.float32)
        out_ref[:, low : low + ROWS] = turned.astype(jnp.bfloat16).reshape(ROWS, ROWS, p.d)


def relayout(p, amplitudes, part):
    count = p.c // AMPS
    blocks = count // ROWS
    return pl.pallas_call(
        functools.partial(relayout_kernel, p),
        out_shape=jax.ShapeDtypeStruct((count, p.ij, p.d), jnp.bfloat16),
        grid=(blocks,),
        in_specs=[pl.BlockSpec((p.ij, ROWS, p.d), lambda c: (0, part * blocks + c, 0))],
        out_specs=pl.BlockSpec((ROWS, p.ij, p.d), lambda c: (c, 0, 0)),
        compiler_params=pltpu.CompilerParams(vmem_limit_bytes=40 * 2**20),
        cost_estimate=pl.CostEstimate(
            flops=2 * count * p.ij * p.d * ROWS * ROWS,
            bytes_accessed=4 * count * p.ij * p.d,
            transcendentals=0,
        ),
        name="relayout",
    )(amplitudes)


def ladder_kernel(p, units, parts, group, place_ref, blocks_ref, *refs):
    count = len(units) * p.xs * CORES
    pieces, amps, out = refs[:count], refs[count : count + AMPS], refs[count + AMPS]
    scratch = refs[count + AMPS + 1 :]
    vectors, left, tiles, held, total, sums, piece_sem, amp_sem = scratch
    w, z, core, chunk = p.window, place_ref[0], place_ref[1], place_ref[2]
    quads = p.c // QUAD
    here = quads // parts
    rows = here * ROWS
    steps = here // group
    wide = group * QUAD * p.ij
    each = parts * steps // AMPS

    class Fetch:
        def __init__(self, step, slot):
            self.step, self.slot = step, slot

        def copy(self, amp, step):
            at = pl.ds(pl.multiple_of(step * wide, wide), wide)
            return pltpu.make_async_copy(amp.at[at], held.at[self.slot], amp_sem.at[self.slot])

        def start(self):
            for n, amp in enumerate(amps):

                @pl.when(self.step // each == n)
                def _():
                    self.copy(amp, self.step - n * each).start()

        def wait(self):
            self.copy(amps[0], 0).wait()

    copies = []
    for n, (o, low, high) in enumerate(units):
        for r in range(p.xs):
            for other in range(CORES):
                parity = core if other == 0 else 1 - core
                origin = CORES * lax.rem(z - o + p.js, p.js) + parity
                row = pl.multiple_of(origin * p.cpad, ROWS)
                number = (n * p.xs + r) * CORES + other
                copies.append(
                    pltpu.make_async_copy(
                        pieces[number],
                        vectors.at[
                            low:high, pl.ds(row, p.cpad), r * LANES : (r + 1) * LANES
                        ],
                        piece_sem.at[number],
                    )
                )
    for copy in copies:
        copy.start()
    for ahead in range(min(SLOTS - 1, parts * steps)):
        Fetch(jnp.int32(ahead), ahead).start()
    for copy in copies:
        copy.wait()

    first = pl.multiple_of(chunk * p.c, ROWS)
    lane = lax.broadcasted_iota(jnp.int32, (p.c, LANES), 1)
    upper = lax.broadcasted_iota(jnp.int32, (p.c // 8, 8, LANES), 1) < QUAD

    def woven(stack):
        stack = [rows.reshape(p.c // 8, 8, LANES) for rows in stack]
        even, odd = [], []
        for one, two in (stack[:2], stack[2:]):
            even.append(jnp.where(upper, one, pltpu.roll(two, QUAD, 1)))
            odd.append(jnp.where(upper, pltpu.roll(one, QUAD, 1), two))
        rows = jnp.stack(even + odd, axis=1)
        return rows.reshape(BLK * p.c, LANES).astype(jnp.bfloat16)

    @pl.loop(0, p.blocks)
    def _(b):
        for r in range(p.xs):
            span = slice(r * LANES, (r + 1) * LANES)
            for m in range(p.nm + 1):
                stack = []
                for e in range(BLK):
                    index = b * BLK + e
                    plane = m * w + index if m < p.nm else m * w + index // p.per_row
                    rows = vectors[plane, pl.ds(first, p.c), span].astype(jnp.float32)
                    if m == p.nm:
                        rows = jnp.where(lane // p.slot == index % p.per_row, rows, 0.0)
                        turn = p.slot
                        while turn < LANES:
                            rows += pltpu.roll(rows, turn, 1)
                            turn *= 2
                    stack.append(rows)
                at = slice((m * p.xs + r) * LANES, (m * p.xs + r + 1) * LANES)
                left[b, :, at] = woven(stack)

    total[...] = jnp.zeros_like(total)
    slot_of = lax.broadcasted_iota(jnp.int32, (1, p.k), 1) % LANES // p.slot

    @pl.loop(0, parts)
    def _(part):
        part_rows = pl.ds(pl.multiple_of(part * rows, rows), rows)

        @pl.loop(0, p.gf)
        def _(gf):
            block = blocks_ref[gf // BLK, 0]
            index = blocks_ref[gf // BLK, 1] * BLK + gf % BLK
            only = (slot_of == index % p.per_row).astype(jnp.float32).astype(jnp.bfloat16)
            lhs = left[block, part_rows]
            for low in range(0, p.d, 256):
                span = slice(low, min(low + 256, p.d))
                rhs = [vectors[m * w + index, span] for m in range(p.nm)]
                rhs.append(vectors[p.nm * w + index // p.per_row, span] * only)
                rhs = jnp.concatenate(rhs, axis=1)
                tile = lax.dot_general(lhs, rhs, NT, preferred_element_type=jnp.float32)
                tile = tile.astype(jnp.bfloat16).reshape(here, ROWS, span.stop - low)
                tiles[:, gf, :, span] = tile

        @pl.loop(0, steps)
        def _(step):
            at = part * steps + step
            slot = lax.rem(at, SLOTS)

            @pl.when(at + SLOTS - 1 < parts * steps)
            def _():
                Fetch(at + SLOTS - 1, lax.rem(at + SLOTS - 1, SLOTS)).start()

            Fetch(at, slot).wait()
            width = QUAD * p.ij
            for n in range(group):
                total[...] += lax.dot_general(
                    tiles[step * group + n].reshape(p.gf * ROWS, p.d),
                    held[slot, n * width : (n + 1) * width],
                    NT,
                    preferred_element_type=jnp.float32,
                )

    width = QUAD * p.ij
    row = lax.broadcasted_iota(jnp.int32, (p.gf * ROWS, width), 0) % QUAD
    col = lax.broadcasted_iota(jnp.int32, (p.gf * ROWS, width), 1) // p.ij
    kept = jnp.where(row == col, total[...], 0.0)
    folded = kept[:, :LANES]
    for low in range(LANES, width, LANES):
        folded += kept[:, low : low + LANES]
    shift = LANES
    while shift > p.ij:
        shift //= 2
        folded += pltpu.roll(folded, shift, 1)
    folded = folded.reshape(-1, 8, LANES)
    folded += pltpu.roll(folded, 1, 1)
    folded += pltpu.roll(folded, 2, 1)
    sums[...] = folded.reshape(p.gf * ROWS, LANES)
    out[...] = sums[pl.ds(QUAD - 1, p.gf * BLK, stride=QUAD), :]


def ladder(p, units, place, blocks, pieces, amps):
    parts, group = 2, 1
    quads = p.c // QUAD
    for wanted in (4, 2):
        if quads // parts % wanted == 0:
            group = wanted
            break
    width = QUAD * p.ij
    return pl.pallas_call(
        functools.partial(ladder_kernel, p, units, parts, group),
        out_shape=jax.ShapeDtypeStruct((p.gf * BLK, LANES), jnp.float32),
        in_specs=[pl.BlockSpec(memory_space=pltpu.SMEM)] * 2
        + [pl.BlockSpec(memory_space=pl.ANY)] * (len(pieces) + AMPS),
        out_specs=pl.BlockSpec(memory_space=pltpu.VMEM),
        scratch_shapes=[
            pltpu.VMEM((p.planes, p.d, p.k), jnp.bfloat16),
            pltpu.VMEM((p.blocks, BLK * p.c, (p.nm + 1) * p.k), jnp.bfloat16),
            pltpu.VMEM((quads // parts, p.gf, ROWS, p.d), jnp.bfloat16),
            pltpu.VMEM((SLOTS, group * width, p.d), jnp.bfloat16),
            pltpu.VMEM((p.gf * ROWS, width), jnp.float32),
            pltpu.VMEM((p.gf * ROWS, LANES), jnp.float32),
            pltpu.SemaphoreType.DMA((len(pieces),)),
            pltpu.SemaphoreType.DMA((SLOTS,)),
        ],
        compiler_params=pltpu.CompilerParams(vmem_limit_bytes=60 * 2**20),
        cost_estimate=pl.CostEstimate(
            flops=2 * p.gf * BLK * p.c * p.d * p.k,
            bytes_accessed=2 * (p.js * p.n_aux * p.planes * p.cpad * LANES + p.c * p.ij * p.d),
            transcendentals=0,
        ),
        name="ladder",
    )(place, blocks, *pieces, *amps)


def pad_columns(array, axis, cols, cpad):
    if cols == cpad:
        return array
    shape = array.shape
    split = array.reshape(shape[:axis] + (shape[axis] // cols, cols) + shape[axis + 1 :])
    widths = [(0, 0)] * split.ndim
    widths[axis + 1] = (0, cpad - cols)
    split = jnp.pad(split, widths)
    return split.reshape(shape[:axis] + (shape[axis] // cols * cpad,) + shape[axis + 1 :])


def shards(chol_vv, chol_ov, t1_window, amplitudes, assignment):
    window, cols, aux_dev = chol_vv.shape
    n_aux, n_pair = lax.axis_size("aux"), lax.axis_size("pair")
    p = Plan(window, chol_ov.shape[0], cols, aux_dev, n_aux, n_pair, amplitudes.shape[0])
    me_aux, me_pair = lax.axis_index("aux"), lax.axis_index("pair")
    z = me_pair // CORES
    place = jnp.stack([z, me_aux % CORES, me_aux]).astype(jnp.int32)

    chol_vv = pad_columns(chol_vv, 1, cols, p.cpad)
    chol_ov = pad_columns(chol_ov, 1, cols, p.cpad)
    spread = spread_amplitudes(p, t1_window)

    def permute(array, target):
        pairs = []
        for a in range(n_aux):
            for q in range(n_pair):
                to_a, to_q = target(a, q)
                pairs.append((a * n_pair + q, to_a * n_pair + to_q))
        return lax.ppermute(array, ("aux", "pair"), pairs)

    def to_slice(array, o):
        return permute(
            array,
            lambda a, q: (
                a // CORES * CORES + q % CORES,
                CORES * ((q // CORES + o) % p.js) + a % CORES,
            ),
        )

    def along_x(array, r):
        return permute(array, lambda a, q: (CORES * ((a // CORES + r) % p.xs) + a % CORES, q))

    def to_core(array):
        return permute(array, lambda a, q: (a ^ 1, q))

    amplitudes = pad_columns(pad_columns(amplitudes, 1, cols, p.cpad), 2, cols, p.cpad)

    order = sorted(range(p.js), key=lambda o: min(o, p.js - o))
    units = [(o, 0, p.planes) for o in order]
    if p.js > 2:
        half = p.planes // 2
        units[-1:] = [(order[-1], 0, half), (order[-1], half, p.planes)]
    rounds = swaps = [[unit] for unit in units]

    def make(o, spread):
        return dress(p, o, place, spread, chol_vv, chol_ov)

    def cut(message, unit):
        if unit[1:] == (0, p.planes):
            return message
        return message[unit[1] : unit[2]]

    messages = {}
    for o, _, _ in rounds[0]:
        messages[o] = make(o, spread)
        messages[o], spread = lax.optimization_barrier((messages[o], spread))
    amps = [None] * AMPS
    sources = [amplitudes] * AMPS
    held = {}
    share_next = []
    count = len(rounds) + 2
    for n in range(count):
        new, made, laid = {}, {}, {}
        to_share, share_next = share_next, []
        if n < len(rounds):
            for unit in rounds[n]:
                new[unit, 0, 0] = to_slice(cut(messages[unit[0]], unit), unit[0])
                share_next.append((unit, 0))
        if 1 <= n <= len(swaps):
            for unit in swaps[n - 1]:
                for r in range(1, p.xs):
                    new[unit, r, 0] = along_x(held[unit, 0, 0], r)
                    share_next.append((unit, r))
        for unit, r in to_share:
            new[unit, r, 1] = to_core(held[unit, r, 0])
        if n + 1 < len(rounds):
            for o, _, _ in rounds[n + 1]:
                if o not in messages:
                    made[o] = make(o, spread)
        part = n - (len(rounds) - AMPS)
        if 0 <= part < AMPS:
            laid[part] = relayout(p, sources[part], part)
        moved = (list(new.values()), list(made.values()), list(laid.values()))
        kept = (list(held.values()), spread, sources)
        moved, (old, spread, sources) = lax.optimization_barrier((moved, kept))
        held = dict(zip(held, old))
        held.update(zip(new, moved[0]))
        messages.update(zip(made, moved[1]))
        for part, amp in zip(laid, moved[2]):
            amps[part] = amp
    amps = [amp.reshape(-1, p.d) for amp in amps]
    pieces = [
        held[unit, r, other] for unit in units for r in range(p.xs) for other in range(CORES)
    ]

    partial_terms = ladder(p, units, place, assignment, pieces, amps)
    share = p.ij // n_aux
    terms = partial_terms[:, : p.ij].reshape(n_pair, BLK, BLK, n_aux, share)
    terms = terms.transpose(3, 0, 4, 2, 1).reshape(n_aux * n_pair, share, BLK * BLK)
    terms = lax.all_to_all(terms, ("aux", "pair"), split_axis=0, concat_axis=0, tiled=True)
    return terms.sum(axis=0)


def solution(mesh):
    in_specs = (P(None, "pair", "aux"), P(None, "pair", "aux"), P(), P(None, "aux", None), P())
    out_specs = P("aux", "pair")
    return jax.shard_map(shards, mesh=mesh, in_specs=in_specs, out_specs=out_specs, check_vma=False)
```

```python
import functools

import jax
import jax.numpy as jnp
from jax import lax
from jax.experimental import pallas as pl
from jax.experimental.pallas import tpu as pltpu
from jax.sharding import PartitionSpec as P

BLK = 4
QUAD = 4
AMPS = 2
DEEP = 256
ROWS = 16
LANES = 128
CORES = 2
NT = (((1,), (1,)), ((), ()))
NN = (((1,), (0,)), ((), ()))


def round_up(value, unit):
    return (value + unit - 1) // unit * unit


class Plan:
    def __init__(self, window, occupied, cols, aux_dev, n_aux, n_pair, pairs_all):
        self.window, self.occupied, self.cols, self.aux_dev = window, occupied, cols, aux_dev
        self.n_aux, self.n_pair, self.ij = n_aux, n_pair, pairs_all
        self.xs = n_aux // CORES
        self.js = n_pair // CORES
        self.cpad = round_up(cols, ROWS)
        chunk = aux_dev // self.js
        self.main = chunk // LANES * LANES
        self.tail = chunk - self.main
        self.slot = 1
        while self.slot < self.tail:
            self.slot *= 2
        self.per_row = LANES // self.slot
        self.nm = self.main // LANES
        self.nt = window // self.per_row
        self.planes = self.nm * window + self.nt
        self.per = n_pair // n_aux
        self.c = self.per * self.cpad
        self.d = n_pair * self.cpad
        self.k = self.xs * LANES
        self.groups = n_pair
        self.blocks = window // BLK
        self.gf = self.groups * BLK
        self.tail_from = self.js * self.main
        self.tail_width = round_up(self.js * self.tail, LANES)


def spread_kernel(p, t1_ref, out_ref):
    def repeat(rows, cols, per_row, per_col):
        row = lax.broadcasted_iota(jnp.int32, (rows, cols), 0) // per_row
        col = lax.broadcasted_iota(jnp.int32, (rows, cols), 1) // per_col
        return (row == col).astype(jnp.float32).astype(jnp.bfloat16)

    rows, cols = p.window * ROWS, p.occupied * ROWS
    tall = lax.dot_general(
        repeat(rows, p.window, ROWS, 1), t1_ref[...], NT, preferred_element_type=jnp.float32
    ).astype(jnp.bfloat16)
    full = jnp.dot(
        tall, repeat(p.occupied, cols, 1, ROWS), preferred_element_type=jnp.float32
    )
    row = lax.broadcasted_iota(jnp.int32, (rows, cols), 0) % ROWS
    col = lax.broadcasted_iota(jnp.int32, (rows, cols), 1) % ROWS
    out_ref[...] = jnp.where(row == col, full, 0.0).astype(jnp.bfloat16)


def spread_amplitudes(p, t1_window):
    return pl.pallas_call(
        functools.partial(spread_kernel, p),
        out_shape=jax.ShapeDtypeStruct((p.window * ROWS, p.occupied * ROWS), jnp.bfloat16),
        compiler_params=pltpu.CompilerParams(vmem_limit_bytes=48 * 2**20),
        name="spread",
    )(t1_window)


def dress_kernel(p, offset, bounds, z_ref, a_ref, *refs):
    ov, vv, outs = refs[: p.nm + 1], refs[p.nm + 1 : 2 * p.nm + 2], refs[2 * p.nm + 2 :]

    def put(start, cols, planes):
        for out, (low, high) in zip(outs, bounds):
            first, last = max(low, start), min(high, start + planes.shape[0])
            if first < last:
                out[first - low : last - low, cols] = planes[first - start : last - start]

    w = p.window
    j = lax.rem(z_ref[0] + offset, p.js)
    lane = lax.broadcasted_iota(jnp.int32, (p.nt, ROWS, LANES), 2)
    for low in range(0, p.cpad, ROWS):
        cols = slice(low, low + ROWS)
        vectors = [ref[:, cols].reshape(p.occupied * ROWS, -1) for ref in ov]
        shift = lax.dot_general(
            a_ref[...], jnp.concatenate(vectors, axis=1), NN, preferred_element_type=jnp.float32
        )
        for m in range(p.nm):
            here = shift[:, m * LANES : (m + 1) * LANES].reshape(w, ROWS, LANES)
            here = vv[m][:, cols].astype(jnp.float32) - here
            put(m * w, cols, here.astype(jnp.bfloat16))
        here = shift[:, p.nm * LANES :].reshape(w, ROWS, p.tail_width)
        source = vv[p.nm][:, cols].astype(jnp.float32) - here
        source = source.reshape(p.nt, p.per_row, ROWS, p.tail_width)
        rest = jnp.zeros((p.nt, ROWS, LANES), jnp.float32)
        for s in range(p.per_row):
            turn = lax.rem(s * p.slot - j * p.tail + 2 * p.tail_width, p.tail_width)
            moved = pltpu.roll(source[:, s].reshape(p.nt * ROWS, p.tail_width), turn, 1)
            moved = moved[:, :LANES].reshape(p.nt, ROWS, LANES)
            keep = (lane >= s * p.slot) & (lane < s * p.slot + p.tail)
            rest = jnp.where(keep, moved, rest)
        put(p.nm * w, cols, rest.astype(jnp.bfloat16))


def dress(p, offset, bounds, z, spread, chol_vv, chol_ov):
    def specs(lead):
        found = []
        for m in range(p.nm):
            found.append(
                pl.BlockSpec(
                    (lead, p.cpad, LANES),
                    lambda i, z, m=m: (0, 0, lax.rem(z[0] + offset, p.js) * p.nm + m),
                )
            )
        found.append(
            pl.BlockSpec(
                (lead, p.cpad, p.tail_width),
                lambda i, z: (0, 0, p.tail_from // p.tail_width),
            )
        )
        return found

    count = p.nm + 1
    return pl.pallas_call(
        functools.partial(dress_kernel, p, offset, bounds),
        out_shape=[
            jax.ShapeDtypeStruct((high - low, p.cpad, LANES), jnp.bfloat16) for low, high in bounds
        ],
        grid_spec=pltpu.PrefetchScalarGridSpec(
            num_scalar_prefetch=1,
            grid=(1,),
            in_specs=[pl.BlockSpec((p.window * ROWS, p.occupied * ROWS), lambda i, z: (0, 0))]
            + specs(p.occupied)
            + specs(p.window),
            out_specs=[
                pl.BlockSpec((high - low, p.cpad, LANES), lambda i, z: (0, 0, 0))
                for low, high in bounds
            ],
        ),
        compiler_params=pltpu.CompilerParams(vmem_limit_bytes=48 * 2**20),
        cost_estimate=pl.CostEstimate(
            flops=2 * p.window * p.occupied * p.cpad * LANES * count * ROWS,
            bytes_accessed=2 * (p.occupied + 2 * p.window) * p.cpad * LANES * count,
            transcendentals=0,
        ),
        name="dress",
    )(z, spread, *([chol_ov] * count), *([chol_vv] * count))


def relayout_kernel(p, in_ref, out_ref):
    rows, half = ROWS * ROWS, LANES // 2
    to = lax.broadcasted_iota(jnp.int32, (rows, rows), 1)
    frm = lax.broadcasted_iota(jnp.int32, (rows, rows), 0)
    turn = (to % ROWS * ROWS + to // ROWS == frm).astype(jnp.float32).astype(jnp.bfloat16)
    lane = lax.broadcasted_iota(jnp.int32, (p.d, LANES), 1)
    for pair in range(p.ij // ROWS // 2):
        one, two = [
            lax.dot_general(
                in_ref[low : low + ROWS].reshape(rows, p.d),
                turn,
                (((0,), (0,)), ((), ())),
                preferred_element_type=jnp.float32,
            )
            for low in (2 * pair * ROWS, (2 * pair + 1) * ROWS)
        ]
        at = slice(pair * LANES, (pair + 1) * LANES)
        for tile in range(rows // LANES):
            span = slice(tile * LANES, (tile + 1) * LANES)
            even = jnp.where(lane < half, one[:, span], pltpu.roll(two[:, span], half, 1))
            odd = jnp.where(lane < half, pltpu.roll(one[:, span], half, 1), two[:, span])
            out_ref[2 * tile, :, at] = even.astype(jnp.bfloat16)
            out_ref[2 * tile + 1, :, at] = odd.astype(jnp.bfloat16)


def relayout(p, amplitudes, part):
    count = p.c // AMPS
    blocks = count // ROWS
    width = QUAD * p.ij
    return pl.pallas_call(
        functools.partial(relayout_kernel, p),
        out_shape=jax.ShapeDtypeStruct((count // QUAD, p.d, width), jnp.bfloat16),
        grid=(blocks,),
        in_specs=[pl.BlockSpec((p.ij, ROWS, p.d), lambda c: (0, part * blocks + c, 0))],
        out_specs=pl.BlockSpec((ROWS // QUAD, p.d, width), lambda c: (c, 0, 0)),
        compiler_params=pltpu.CompilerParams(vmem_limit_bytes=40 * 2**20),
        cost_estimate=pl.CostEstimate(
            flops=2 * count * p.ij * p.d * ROWS * ROWS,
            bytes_accessed=4 * count * p.ij * p.d,
            transcendentals=0,
        ),
        name="relayout",
    )(amplitudes)


def ladder_kernel(p, units, group, place_ref, blocks_ref, *refs):
    count = len(units) * p.xs * CORES
    pieces, amps, out = refs[:count], refs[count : count + AMPS], refs[count + AMPS]
    scratch = refs[count + AMPS + 1 :]
    vectors, left, spread_tail, tiles, held, total, piece_sem, amp_sem = scratch
    w, z, core, chunk = p.window, place_ref[0], place_ref[1], place_ref[2]
    quads = p.c // QUAD
    width = QUAD * p.ij
    steps = quads // group
    spans = [slice(low, min(low + DEEP, p.d)) for low in range(0, p.d, DEEP)]

    def fetches(span):
        each = quads // AMPS
        return [
            pltpu.make_async_copy(
                amp.at[:, span],
                held.at[n * each : (n + 1) * each, : span.stop - span.start],
                amp_sem.at[n],
            )
            for n, amp in enumerate(amps)
        ]

    copies = []
    for n, (o, low, high) in enumerate(units):
        for r in range(p.xs):
            for other in range(CORES):
                parity = core if other == 0 else 1 - core
                origin = CORES * lax.rem(z - o + p.js, p.js) + parity
                row = pl.multiple_of(origin * p.cpad, ROWS)
                number = (n * p.xs + r) * CORES + other
                copies.append(
                    pltpu.make_async_copy(
                        pieces[number],
                        vectors.at[
                            low:high, pl.ds(row, p.cpad), r * LANES : (r + 1) * LANES
                        ],
                        piece_sem.at[number],
                    )
                )
    for copy in copies:
        copy.start()
    total[...] = jnp.zeros_like(total)
    for copy in copies:
        copy.wait()

    mixed = QUAD * ROWS
    to = lax.broadcasted_iota(jnp.int32, (mixed, mixed), 0)
    frm = lax.broadcasted_iota(jnp.int32, (mixed, mixed), 1)
    weave = ((to % BLK) * ROWS + to // BLK == frm).astype(jnp.float32).astype(jnp.bfloat16)
    lane_in = lax.broadcasted_iota(jnp.int32, (LANES, LANES), 0)
    lane_out = lax.broadcasted_iota(jnp.int32, (LANES, LANES), 1)
    same = lane_in % p.slot == lane_out % p.slot
    first = pl.multiple_of(chunk * p.c, ROWS)

    def woven(stack):
        return lax.dot_general(weave, stack, NN, preferred_element_type=jnp.float32).astype(
            jnp.bfloat16
        )

    @pl.loop(0, p.blocks)
    def _(b):
        for e in range(BLK):
            index = b * BLK + e
            plane = p.nm * w + index // p.per_row
            copier = (same & (lane_in // p.slot == index % p.per_row)).astype(jnp.float32)
            copier = copier.astype(jnp.bfloat16)
            for r in range(p.xs):
                span = slice(r * LANES, (r + 1) * LANES)
                spread_tail[e, :, span] = lax.dot_general(
                    vectors[plane, pl.ds(first, p.c), span],
                    copier,
                    NN,
                    preferred_element_type=jnp.float32,
                ).astype(jnp.bfloat16)
        for i in range(p.c // ROWS):
            span = slice(i * mixed, (i + 1) * mixed)
            tail = [spread_tail[e, i * ROWS : (i + 1) * ROWS, :] for e in range(BLK)]
            left[b, span, p.nm * p.k :] = woven(jnp.concatenate(tail, axis=0))
            for m in range(p.nm):
                at = pl.ds(pl.multiple_of(first + i * ROWS, ROWS), ROWS)
                stack = [vectors[m * w + b * BLK + e, at] for e in range(BLK)]
                left[b, span, m * p.k : (m + 1) * p.k] = woven(jnp.concatenate(stack, axis=0))

    slot_of = lax.broadcasted_iota(jnp.int32, (1, p.k), 1) % LANES // p.slot

    for span in spans:
        size = span.stop - span.start
        for copy in fetches(span):
            copy.start()

        @pl.loop(0, p.gf)
        def _(gf):
            block = blocks_ref[gf // BLK, 0]
            index = blocks_ref[gf // BLK, 1] * BLK + gf % BLK
            only = (slot_of == index % p.per_row).astype(jnp.float32).astype(jnp.bfloat16)
            rhs = [vectors[m * w + index, span] for m in range(p.nm)]
            rhs.append(vectors[p.nm * w + index // p.per_row, span] * only)
            tile = lax.dot_general(
                left[block], jnp.concatenate(rhs, axis=1), NT, preferred_element_type=jnp.float32
            )
            tiles[:, gf, :, :size] = tile.astype(jnp.bfloat16).reshape(quads, ROWS, size)

        for copy in fetches(span):
            copy.wait()

        @pl.loop(0, steps)
        def _(step):
            lhs = [
                tiles[step * group + n, :, :, :size].reshape(p.gf * ROWS, size)
                for n in range(group)
            ]
            rhs = [held[step * group + n, :size] for n in range(group)]
            total[...] += lax.dot_general(
                jnp.concatenate(lhs, axis=1),
                jnp.concatenate(rhs, axis=0),
                NN,
                preferred_element_type=jnp.float32,
            )

    row = lax.broadcasted_iota(jnp.int32, (p.gf * ROWS, width), 0) % ROWS // BLK
    col = lax.broadcasted_iota(jnp.int32, (p.gf * ROWS, width), 1) // ROWS % QUAD
    kept = jnp.where(row == col, total[...], 0.0)
    kept += pltpu.roll(kept, width - ROWS, 1)
    kept += pltpu.roll(kept, width - 2 * ROWS, 1)
    kept = kept.reshape(p.gf, 2, 8, width).sum(axis=1)
    out[...] = kept[:, :4] + kept[:, 4:]


def ladder(p, units, place, blocks, pieces, amps):
    quads = p.c // QUAD
    group = 4 if quads % 4 == 0 else 2
    width = QUAD * p.ij
    return pl.pallas_call(
        functools.partial(ladder_kernel, p, units, group),
        out_shape=jax.ShapeDtypeStruct((p.gf, BLK, width), jnp.float32),
        in_specs=[pl.BlockSpec(memory_space=pltpu.SMEM)] * 2
        + [pl.BlockSpec(memory_space=pl.ANY)] * (len(pieces) + AMPS),
        out_specs=pl.BlockSpec(memory_space=pltpu.VMEM),
        scratch_shapes=[
            pltpu.VMEM((p.planes, p.d, p.k), jnp.bfloat16),
            pltpu.VMEM((p.blocks, BLK * p.c, (p.nm + 1) * p.k), jnp.bfloat16),
            pltpu.VMEM((BLK, p.c, p.k), jnp.bfloat16),
            pltpu.VMEM((quads, p.gf, ROWS, DEEP), jnp.bfloat16),
            pltpu.VMEM((quads, DEEP, width), jnp.bfloat16),
            pltpu.VMEM((p.gf * ROWS, width), jnp.float32),
            pltpu.SemaphoreType.DMA((len(pieces),)),
            pltpu.SemaphoreType.DMA((AMPS,)),
        ],
        compiler_params=pltpu.CompilerParams(vmem_limit_bytes=60 * 2**20),
        cost_estimate=pl.CostEstimate(
            flops=2 * p.gf * BLK * p.c * p.d * p.k,
            bytes_accessed=2 * (p.planes * p.d * p.k + p.c * p.ij * p.d),
            transcendentals=0,
        ),
        name="ladder",
    )(place, blocks, *pieces, *amps)


def pad_columns(array, axis, cols, cpad):
    if cols == cpad:
        return array
    shape = array.shape
    split = array.reshape(shape[:axis] + (shape[axis] // cols, cols) + shape[axis + 1 :])
    widths = [(0, 0)] * split.ndim
    widths[axis + 1] = (0, cpad - cols)
    split = jnp.pad(split, widths)
    return split.reshape(shape[:axis] + (shape[axis] // cols * cpad,) + shape[axis + 1 :])


def shards(chol_vv, chol_ov, t1_window, amplitudes, assignment):
    window, cols, aux_dev = chol_vv.shape
    n_aux, n_pair = lax.axis_size("aux"), lax.axis_size("pair")
    p = Plan(window, chol_ov.shape[0], cols, aux_dev, n_aux, n_pair, amplitudes.shape[0])
    me_aux, me_pair = lax.axis_index("aux"), lax.axis_index("pair")
    z = me_pair // CORES
    place = jnp.stack([z, me_aux % CORES, me_aux]).astype(jnp.int32)

    chol_vv = pad_columns(chol_vv, 1, cols, p.cpad)
    chol_ov = pad_columns(chol_ov, 1, cols, p.cpad)
    spread = spread_amplitudes(p, t1_window)

    def permute(array, target):
        pairs = []
        for a in range(n_aux):
            for q in range(n_pair):
                to_a, to_q = target(a, q)
                pairs.append((a * n_pair + q, to_a * n_pair + to_q))
        return lax.ppermute(array, ("aux", "pair"), pairs)

    def to_slice(array, o):
        return permute(
            array,
            lambda a, q: (
                a // CORES * CORES + q % CORES,
                CORES * ((q // CORES + o) % p.js) + a % CORES,
            ),
        )

    def along_x(array, r):
        return permute(array, lambda a, q: (CORES * ((a // CORES + r) % p.xs) + a % CORES, q))

    def to_core(array):
        return permute(array, lambda a, q: (a ^ 1, q))

    amplitudes = pad_columns(pad_columns(amplitudes, 1, cols, p.cpad), 2, cols, p.cpad)

    order = sorted(range(p.js), key=lambda o: min(o, p.js - o))
    whole = (0, p.planes)
    bounds = {o: [whole] for o in order}
    if p.js > 2:
        half = p.planes // 2
        bounds[order[-1]] = [(0, half), (half, p.planes)]
    units = [(o, *bound) for o in order for bound in bounds[o]]
    rounds = [units[:2]] + [[unit] for unit in units[2:]]
    swaps = [[], units[1:2]] + [[unit] for unit in units[2:]]

    messages = {}

    def make(o, spread):
        made = dress(p, o, bounds[o], place, spread, chol_vv, chol_ov)
        return dict(zip([(o, *bound) for bound in bounds[o]], made))

    for o in order[:2]:
        made, spread = lax.optimization_barrier((make(o, spread), spread))
        messages.update(made)
    amps = [None] * AMPS
    sources = [amplitudes] * AMPS
    held, raw = {}, {}
    share_next = []
    for n in range(len(swaps) + 1):
        new, made, laid, crossed = {}, {}, {}, {}
        to_share, share_next = share_next, []
        if n < len(rounds):
            for unit in rounds[n]:
                new[unit, 0, 0] = to_slice(messages[unit], unit[0])
                share_next.append((unit, 0))
        if n < len(swaps):
            for unit in swaps[n]:
                for r in range(1, p.xs):
                    new[unit, r, 0] = along_x(held[unit, 0, 0], r)
                    share_next.append((unit, r))
        for r in range(1, p.xs):
            if n == 0:
                crossed[r] = along_x(messages[units[0]], r)
            if n == 1:
                new[units[0], r, 0] = to_slice(raw[r], 0)
                share_next.append((units[0], r))
        for unit, r in to_share:
            new[unit, r, 1] = to_core(held[unit, r, 0])
        if n + 1 < len(rounds):
            for unit in rounds[n + 1]:
                if unit not in messages:
                    made.update(make(unit[0], spread))
        part = n - (len(rounds) - AMPS)
        if 0 <= part < AMPS:
            laid[part] = relayout(p, sources[part], part)
        moved = (list(new.values()), list(made.values()), list(laid.values()), crossed)
        kept = (list(held.values()), spread, sources)
        moved, (old, spread, sources) = lax.optimization_barrier((moved, kept))
        held = dict(zip(held, old))
        held.update(zip(new, moved[0]))
        messages.update(zip(made, moved[1]))
        raw = moved[3]
        for part, amp in zip(laid, moved[2]):
            amps[part] = amp
    pieces = [
        held[unit, r, other] for unit in units for r in range(p.xs) for other in range(CORES)
    ]

    partial_terms = ladder(p, units, place, assignment, pieces, amps)
    share = p.ij // n_aux
    terms = partial_terms.reshape(n_pair, BLK, BLK, p.ij // ROWS, QUAD * ROWS)[..., :ROWS]
    terms = terms.reshape(n_pair, BLK, BLK, n_aux, share)
    terms = terms.transpose(3, 0, 4, 2, 1).reshape(n_aux * n_pair, share, BLK * BLK)
    terms = lax.all_to_all(terms, ("aux", "pair"), split_axis=0, concat_axis=0, tiled=True)
    return terms.sum(axis=0)


def solution(mesh):
    in_specs = (P(None, "pair", "aux"), P(None, "pair", "aux"), P(), P(None, "aux", None), P())
    out_specs = P("aux", "pair")
    return jax.shard_map(shards, mesh=mesh, in_specs=in_specs, out_specs=out_specs, check_vma=False)
```

```python
import functools

import jax
import jax.numpy as jnp
from jax import lax
from jax.experimental import pallas as pl
from jax.experimental.pallas import tpu as pltpu
from jax.sharding import PartitionSpec as P

BLK = 4
QUAD = 4
AMPS = 2
PARTS = 4
SLOTS = 4
ROWS = 16
LANES = 128
CORES = 2
NT = (((1,), (1,)), ((), ()))
NN = (((1,), (0,)), ((), ()))


def round_up(value, unit):
    return (value + unit - 1) // unit * unit


class Plan:
    def __init__(self, window, occupied, cols, aux_dev, n_aux, n_pair, pairs_all):
        self.window, self.occupied, self.cols, self.aux_dev = window, occupied, cols, aux_dev
        self.n_aux, self.n_pair, self.ij = n_aux, n_pair, pairs_all
        self.xs = n_aux // CORES
        self.js = n_pair // CORES
        self.cpad = round_up(cols, ROWS)
        chunk = aux_dev // self.js
        self.main = chunk // LANES * LANES
        self.tail = chunk - self.main
        self.slot = 1
        while self.slot < self.tail:
            self.slot *= 2
        self.per_row = LANES // self.slot
        self.nm = self.main // LANES
        self.nt = window // self.per_row
        self.planes = self.nm * window + self.nt
        self.per = n_pair // n_aux
        self.c = self.per * self.cpad
        self.d = n_pair * self.cpad
        self.k = self.xs * LANES
        self.groups = n_pair
        self.blocks = window // BLK
        self.gf = self.groups * BLK
        self.tail_from = self.js * self.main
        self.tail_width = round_up(self.js * self.tail, LANES)


def spread_kernel(p, t1_ref, out_ref):
    def repeat(rows, cols, per_row, per_col):
        row = lax.broadcasted_iota(jnp.int32, (rows, cols), 0) // per_row
        col = lax.broadcasted_iota(jnp.int32, (rows, cols), 1) // per_col
        return (row == col).astype(jnp.float32).astype(jnp.bfloat16)

    rows, cols = p.window * ROWS, p.occupied * ROWS
    tall = lax.dot_general(
        repeat(rows, p.window, ROWS, 1), t1_ref[...], NT, preferred_element_type=jnp.float32
    ).astype(jnp.bfloat16)
    full = jnp.dot(
        tall, repeat(p.occupied, cols, 1, ROWS), preferred_element_type=jnp.float32
    )
    row = lax.broadcasted_iota(jnp.int32, (rows, cols), 0) % ROWS
    col = lax.broadcasted_iota(jnp.int32, (rows, cols), 1) % ROWS
    out_ref[...] = jnp.where(row == col, full, 0.0).astype(jnp.bfloat16)


def spread_amplitudes(p, t1_window):
    return pl.pallas_call(
        functools.partial(spread_kernel, p),
        out_shape=jax.ShapeDtypeStruct((p.window * ROWS, p.occupied * ROWS), jnp.bfloat16),
        compiler_params=pltpu.CompilerParams(vmem_limit_bytes=48 * 2**20),
        name="spread",
    )(t1_window)


def dress_kernel(p, offset, bounds, z_ref, a_ref, *refs):
    ov, vv, outs = refs[: p.nm + 1], refs[p.nm + 1 : 2 * p.nm + 2], refs[2 * p.nm + 2 :]

    def put(start, cols, planes):
        for out, (low, high) in zip(outs, bounds):
            first, last = max(low, start), min(high, start + planes.shape[0])
            if first < last:
                out[first - low : last - low, cols] = planes[first - start : last - start]

    w = p.window
    j = lax.rem(z_ref[0] + offset, p.js)
    lane = lax.broadcasted_iota(jnp.int32, (p.nt, ROWS, LANES), 2)
    for low in range(0, p.cpad, ROWS):
        cols = slice(low, low + ROWS)
        vectors = [ref[:, cols].reshape(p.occupied * ROWS, -1) for ref in ov]
        shift = lax.dot_general(
            a_ref[...], jnp.concatenate(vectors, axis=1), NN, preferred_element_type=jnp.float32
        )
        for m in range(p.nm):
            here = shift[:, m * LANES : (m + 1) * LANES].reshape(w, ROWS, LANES)
            here = vv[m][:, cols].astype(jnp.float32) - here
            put(m * w, cols, here.astype(jnp.bfloat16))
        here = shift[:, p.nm * LANES :].reshape(w, ROWS, p.tail_width)
        source = vv[p.nm][:, cols].astype(jnp.float32) - here
        source = source.reshape(p.nt, p.per_row, ROWS, p.tail_width)
        rest = jnp.zeros((p.nt, ROWS, LANES), jnp.float32)
        for s in range(p.per_row):
            turn = lax.rem(s * p.slot - j * p.tail + 2 * p.tail_width, p.tail_width)
            moved = pltpu.roll(source[:, s].reshape(p.nt * ROWS, p.tail_width), turn, 1)
            moved = moved[:, :LANES].reshape(p.nt, ROWS, LANES)
            keep = (lane >= s * p.slot) & (lane < s * p.slot + p.tail)
            rest = jnp.where(keep, moved, rest)
        put(p.nm * w, cols, rest.astype(jnp.bfloat16))


def dress(p, offset, bounds, z, spread, chol_vv, chol_ov):
    def specs(lead):
        found = []
        for m in range(p.nm):
            found.append(
                pl.BlockSpec(
                    (lead, p.cpad, LANES),
                    lambda i, z, m=m: (0, 0, lax.rem(z[0] + offset, p.js) * p.nm + m),
                )
            )
        found.append(
            pl.BlockSpec(
                (lead, p.cpad, p.tail_width),
                lambda i, z: (0, 0, p.tail_from // p.tail_width),
            )
        )
        return found

    count = p.nm + 1
    return pl.pallas_call(
        functools.partial(dress_kernel, p, offset, bounds),
        out_shape=[
            jax.ShapeDtypeStruct((high - low, p.cpad, LANES), jnp.bfloat16) for low, high in bounds
        ],
        grid_spec=pltpu.PrefetchScalarGridSpec(
            num_scalar_prefetch=1,
            grid=(1,),
            in_specs=[pl.BlockSpec((p.window * ROWS, p.occupied * ROWS), lambda i, z: (0, 0))]
            + specs(p.occupied)
            + specs(p.window),
            out_specs=[
                pl.BlockSpec((high - low, p.cpad, LANES), lambda i, z: (0, 0, 0))
                for low, high in bounds
            ],
        ),
        compiler_params=pltpu.CompilerParams(vmem_limit_bytes=48 * 2**20),
        cost_estimate=pl.CostEstimate(
            flops=2 * p.window * p.occupied * p.cpad * LANES * count * ROWS,
            bytes_accessed=2 * (p.occupied + 2 * p.window) * p.cpad * LANES * count,
            transcendentals=0,
        ),
        name="dress",
    )(z, spread, *([chol_ov] * count), *([chol_vv] * count))


def relayout_kernel(p, in_ref, out_ref):
    rows, half = ROWS * ROWS, LANES // 2
    to = lax.broadcasted_iota(jnp.int32, (rows, rows), 1)
    frm = lax.broadcasted_iota(jnp.int32, (rows, rows), 0)
    turn = (to % ROWS * ROWS + to // ROWS == frm).astype(jnp.float32).astype(jnp.bfloat16)
    lane = lax.broadcasted_iota(jnp.int32, (p.d, LANES), 1)
    for pair in range(p.ij // ROWS // 2):
        one, two = [
            lax.dot_general(
                in_ref[low : low + ROWS].reshape(rows, p.d),
                turn,
                (((0,), (0,)), ((), ())),
                preferred_element_type=jnp.float32,
            )
            for low in (2 * pair * ROWS, (2 * pair + 1) * ROWS)
        ]
        at = slice(pair * LANES, (pair + 1) * LANES)
        for tile in range(rows // LANES):
            span = slice(tile * LANES, (tile + 1) * LANES)
            even = jnp.where(lane < half, one[:, span], pltpu.roll(two[:, span], half, 1))
            odd = jnp.where(lane < half, pltpu.roll(one[:, span], half, 1), two[:, span])
            out_ref[2 * tile, :, at] = even.astype(jnp.bfloat16)
            out_ref[2 * tile + 1, :, at] = odd.astype(jnp.bfloat16)


def relayout(p, amplitudes, part):
    count = p.c // AMPS
    blocks = count // ROWS
    width = QUAD * p.ij
    return pl.pallas_call(
        functools.partial(relayout_kernel, p),
        out_shape=jax.ShapeDtypeStruct((count // QUAD, p.d, width), jnp.bfloat16),
        grid=(blocks,),
        in_specs=[pl.BlockSpec((p.ij, ROWS, p.d), lambda c: (0, part * blocks + c, 0))],
        out_specs=pl.BlockSpec((ROWS // QUAD, p.d, width), lambda c: (c, 0, 0)),
        compiler_params=pltpu.CompilerParams(vmem_limit_bytes=40 * 2**20),
        cost_estimate=pl.CostEstimate(
            flops=2 * count * p.ij * p.d * ROWS * ROWS,
            bytes_accessed=4 * count * p.ij * p.d,
            transcendentals=0,
        ),
        name="relayout",
    )(amplitudes)


def ladder_kernel(p, units, parts, group, place_ref, blocks_ref, *refs):
    count = len(units) * p.xs * CORES
    pieces, amps, out = refs[:count], refs[count : count + AMPS], refs[count + AMPS]
    scratch = refs[count + AMPS + 1 :]
    vectors, left, spread_tail, tiles, held, total, piece_sem, amp_sem = scratch
    w, z, core, chunk = p.window, place_ref[0], place_ref[1], place_ref[2]
    quads = p.c // QUAD
    here = quads // parts
    rows = here * ROWS
    steps = here // group
    each = parts * steps // AMPS

    class Fetch:
        def __init__(self, step, slot):
            self.step, self.slot = step, slot

        def copy(self, amp, step):
            at = pl.ds(step * group, group)
            return pltpu.make_async_copy(amp.at[at], held.at[self.slot], amp_sem.at[self.slot])

        def start(self):
            for n, amp in enumerate(amps):

                @pl.when(self.step // each == n)
                def _():
                    self.copy(amp, self.step - n * each).start()

        def wait(self):
            self.copy(amps[0], 0).wait()

    copies = []
    for n, (o, low, high) in enumerate(units):
        for r in range(p.xs):
            for other in range(CORES):
                parity = core if other == 0 else 1 - core
                origin = CORES * lax.rem(z - o + p.js, p.js) + parity
                row = pl.multiple_of(origin * p.cpad, ROWS)
                number = (n * p.xs + r) * CORES + other
                copies.append(
                    pltpu.make_async_copy(
                        pieces[number],
                        vectors.at[
                            low:high, pl.ds(row, p.cpad), r * LANES : (r + 1) * LANES
                        ],
                        piece_sem.at[number],
                    )
                )
    for copy in copies:
        copy.start()
    for ahead in range(min(SLOTS - 1, parts * steps)):
        Fetch(jnp.int32(ahead), ahead).start()
    for copy in copies:
        copy.wait()

    mixed = QUAD * ROWS
    to = lax.broadcasted_iota(jnp.int32, (mixed, mixed), 0)
    frm = lax.broadcasted_iota(jnp.int32, (mixed, mixed), 1)
    weave = ((to % BLK) * ROWS + to // BLK == frm).astype(jnp.float32).astype(jnp.bfloat16)
    lane_in = lax.broadcasted_iota(jnp.int32, (LANES, LANES), 0)
    lane_out = lax.broadcasted_iota(jnp.int32, (LANES, LANES), 1)
    same = lane_in % p.slot == lane_out % p.slot
    first = pl.multiple_of(chunk * p.c, ROWS)

    def woven(stack):
        return lax.dot_general(weave, stack, NN, preferred_element_type=jnp.float32).astype(
            jnp.bfloat16
        )

    @pl.loop(0, p.blocks)
    def _(b):
        for e in range(BLK):
            index = b * BLK + e
            plane = p.nm * w + index // p.per_row
            copier = (same & (lane_in // p.slot == index % p.per_row)).astype(jnp.float32)
            copier = copier.astype(jnp.bfloat16)
            for r in range(p.xs):
                span = slice(r * LANES, (r + 1) * LANES)
                spread_tail[e, :, span] = lax.dot_general(
                    vectors[plane, pl.ds(first, p.c), span],
                    copier,
                    NN,
                    preferred_element_type=jnp.float32,
                ).astype(jnp.bfloat16)
        for i in range(p.c // ROWS):
            span = slice(i * mixed, (i + 1) * mixed)
            tail = [spread_tail[e, i * ROWS : (i + 1) * ROWS, :] for e in range(BLK)]
            left[b, span, p.nm * p.k :] = woven(jnp.concatenate(tail, axis=0))
            for m in range(p.nm):
                at = pl.ds(pl.multiple_of(first + i * ROWS, ROWS), ROWS)
                stack = [vectors[m * w + b * BLK + e, at] for e in range(BLK)]
                left[b, span, m * p.k : (m + 1) * p.k] = woven(jnp.concatenate(stack, axis=0))

    total[...] = jnp.zeros_like(total)
    slot_of = lax.broadcasted_iota(jnp.int32, (1, p.k), 1) % LANES // p.slot

    @pl.loop(0, parts)
    def _(part):
        part_rows = pl.ds(pl.multiple_of(part * rows, rows), rows)

        @pl.loop(0, p.gf)
        def _(gf):
            first_block = blocks_ref[gf // BLK, 0]
            index = blocks_ref[gf // BLK, 1] * BLK + gf % BLK
            only = (slot_of == index % p.per_row).astype(jnp.float32).astype(jnp.bfloat16)
            lhs = left[first_block, part_rows]
            for low in range(0, p.d, 256):
                span = slice(low, min(low + 256, p.d))
                rhs = [vectors[m * w + index, span] for m in range(p.nm)]
                rhs.append(vectors[p.nm * w + index // p.per_row, span] * only)
                rhs = jnp.concatenate(rhs, axis=1)
                block = lax.dot_general(lhs, rhs, NT, preferred_element_type=jnp.float32)
                block = block.astype(jnp.bfloat16).reshape(here, ROWS, span.stop - low)
                tiles[:, gf, :, span] = block

        @pl.loop(0, steps)
        def _(step):
            at = part * steps + step
            slot = lax.rem(at, SLOTS)

            @pl.when(at + SLOTS - 1 < parts * steps)
            def _():
                Fetch(at + SLOTS - 1, lax.rem(at + SLOTS - 1, SLOTS)).start()

            Fetch(at, slot).wait()
            for n in range(group):
                total[...] += lax.dot_general(
                    tiles[step * group + n].reshape(p.gf * ROWS, p.d),
                    held[slot, n],
                    NN,
                    preferred_element_type=jnp.float32,
                )

    width = QUAD * p.ij
    row = lax.broadcasted_iota(jnp.int32, (p.gf * ROWS, width), 0) % ROWS // BLK
    col = lax.broadcasted_iota(jnp.int32, (p.gf * ROWS, width), 1) // ROWS % QUAD
    kept = jnp.where(row == col, total[...], 0.0)
    kept += pltpu.roll(kept, width - ROWS, 1)
    kept += pltpu.roll(kept, width - 2 * ROWS, 1)
    kept = kept.reshape(p.gf, 2, 8, width).sum(axis=1)
    out[...] = kept[:, :4] + kept[:, 4:]


def ladder(p, units, place, blocks, pieces, amps):
    parts, group = PARTS, 2
    quads = p.c // QUAD
    width = QUAD * p.ij
    return pl.pallas_call(
        functools.partial(ladder_kernel, p, units, parts, group),
        out_shape=jax.ShapeDtypeStruct((p.gf, BLK, width), jnp.float32),
        in_specs=[pl.BlockSpec(memory_space=pltpu.SMEM)] * 2
        + [pl.BlockSpec(memory_space=pl.ANY)] * (len(pieces) + AMPS),
        out_specs=pl.BlockSpec(memory_space=pltpu.VMEM),
        scratch_shapes=[
            pltpu.VMEM((p.planes, p.d, p.k), jnp.bfloat16),
            pltpu.VMEM((p.blocks, BLK * p.c, (p.nm + 1) * p.k), jnp.bfloat16),
            pltpu.VMEM((BLK, p.c, p.k), jnp.bfloat16),
            pltpu.VMEM((quads // parts, p.gf, ROWS, p.d), jnp.bfloat16),
            pltpu.VMEM((SLOTS, group, p.d, width), jnp.bfloat16),
            pltpu.VMEM((p.gf * ROWS, width), jnp.float32),
            pltpu.SemaphoreType.DMA((len(pieces),)),
            pltpu.SemaphoreType.DMA((SLOTS,)),
        ],
        compiler_params=pltpu.CompilerParams(vmem_limit_bytes=60 * 2**20),
        cost_estimate=pl.CostEstimate(
            flops=2 * p.gf * BLK * p.c * p.d * p.k,
            bytes_accessed=2 * (p.js * p.n_aux * p.planes * p.cpad * LANES + p.c * p.ij * p.d),
            transcendentals=0,
        ),
        name="ladder",
    )(place, blocks, *pieces, *amps)


def pad_columns(array, axis, cols, cpad):
    if cols == cpad:
        return array
    shape = array.shape
    split = array.reshape(shape[:axis] + (shape[axis] // cols, cols) + shape[axis + 1 :])
    widths = [(0, 0)] * split.ndim
    widths[axis + 1] = (0, cpad - cols)
    split = jnp.pad(split, widths)
    return split.reshape(shape[:axis] + (shape[axis] // cols * cpad,) + shape[axis + 1 :])


def shards(chol_vv, chol_ov, t1_window, amplitudes, assignment):
    window, cols, aux_dev = chol_vv.shape
    n_aux, n_pair = lax.axis_size("aux"), lax.axis_size("pair")
    p = Plan(window, chol_ov.shape[0], cols, aux_dev, n_aux, n_pair, amplitudes.shape[0])
    me_aux, me_pair = lax.axis_index("aux"), lax.axis_index("pair")
    z = me_pair // CORES
    place = jnp.stack([z, me_aux % CORES, me_aux]).astype(jnp.int32)

    chol_vv = pad_columns(chol_vv, 1, cols, p.cpad)
    chol_ov = pad_columns(chol_ov, 1, cols, p.cpad)
    spread = spread_amplitudes(p, t1_window)

    def permute(array, target):
        pairs = []
        for a in range(n_aux):
            for q in range(n_pair):
                to_a, to_q = target(a, q)
                pairs.append((a * n_pair + q, to_a * n_pair + to_q))
        return lax.ppermute(array, ("aux", "pair"), pairs)

    def to_slice(array, o):
        return permute(
            array,
            lambda a, q: (
                a // CORES * CORES + q % CORES,
                CORES * ((q // CORES + o) % p.js) + a % CORES,
            ),
        )

    def along_x(array, r):
        return permute(array, lambda a, q: (CORES * ((a // CORES + r) % p.xs) + a % CORES, q))

    def to_core(array):
        return permute(array, lambda a, q: (a ^ 1, q))

    amplitudes = pad_columns(pad_columns(amplitudes, 1, cols, p.cpad), 2, cols, p.cpad)

    order = sorted(range(p.js), key=lambda o: min(o, p.js - o))
    whole = (0, p.planes)
    bounds = {o: [whole] for o in order}
    if p.js > 2:
        half = p.planes // 2
        bounds[order[-1]] = [(0, half), (half, p.planes)]
    units = [(o, *bound) for o in order for bound in bounds[o]]
    rounds = [units[:2]] + [[unit] for unit in units[2:]]
    swaps = [[], units[1:2]] + [[unit] for unit in units[2:]]

    messages = {}

    def make(o, spread):
        made = dress(p, o, bounds[o], place, spread, chol_vv, chol_ov)
        return dict(zip([(o, *bound) for bound in bounds[o]], made))

    for o in order[:2]:
        made, spread = lax.optimization_barrier((make(o, spread), spread))
        messages.update(made)
    amps = [None] * AMPS
    sources = [amplitudes] * AMPS
    held, raw = {}, {}
    share_next = []
    for n in range(len(swaps) + 1):
        new, made, laid, crossed = {}, {}, {}, {}
        to_share, share_next = share_next, []
        if n < len(rounds):
            for unit in rounds[n]:
                new[unit, 0, 0] = to_slice(messages[unit], unit[0])
                share_next.append((unit, 0))
        if n < len(swaps):
            for unit in swaps[n]:
                for r in range(1, p.xs):
                    new[unit, r, 0] = along_x(held[unit, 0, 0], r)
                    share_next.append((unit, r))
        for r in range(1, p.xs):
            if n == 0:
                crossed[r] = along_x(messages[units[0]], r)
            if n == 1:
                new[units[0], r, 0] = to_slice(raw[r], 0)
                share_next.append((units[0], r))
        for unit, r in to_share:
            new[unit, r, 1] = to_core(held[unit, r, 0])
        if n + 1 < len(rounds):
            for unit in rounds[n + 1]:
                if unit not in messages:
                    made.update(make(unit[0], spread))
        part = n - (len(rounds) - AMPS)
        if 0 <= part < AMPS:
            laid[part] = relayout(p, sources[part], part)
        moved = (list(new.values()), list(made.values()), list(laid.values()), crossed)
        kept = (list(held.values()), spread, sources)
        moved, (old, spread, sources) = lax.optimization_barrier((moved, kept))
        held = dict(zip(held, old))
        held.update(zip(new, moved[0]))
        messages.update(zip(made, moved[1]))
        raw = moved[3]
        for part, amp in zip(laid, moved[2]):
            amps[part] = amp
    pieces = [
        held[unit, r, other] for unit in units for r in range(p.xs) for other in range(CORES)
    ]

    partial_terms = ladder(p, units, place, assignment, pieces, amps)
    share = p.ij // n_aux
    terms = partial_terms.reshape(n_pair, BLK, BLK, p.ij // ROWS, QUAD * ROWS)[..., :ROWS]
    terms = terms.reshape(n_pair, BLK, BLK, n_aux, share)
    terms = terms.transpose(3, 0, 4, 2, 1).reshape(n_aux * n_pair, share, BLK * BLK)
    terms = lax.all_to_all(terms, ("aux", "pair"), split_axis=0, concat_axis=0, tiled=True)
    return terms.sum(axis=0)


def solution(mesh):
    in_specs = (P(None, "pair", "aux"), P(None, "pair", "aux"), P(), P(None, "aux", None), P())
    out_specs = P("aux", "pair")
    return jax.shard_map(shards, mesh=mesh, in_specs=in_specs, out_specs=out_specs, check_vma=False)
```

```python
import functools

import jax
import jax.numpy as jnp
from jax import lax
from jax.experimental import pallas as pl
from jax.experimental.pallas import tpu as pltpu
from jax.sharding import PartitionSpec as P

BLK = 4
QUAD = 4
AMPS = 2
DEEP = 256
ROWS = 16
LANES = 128
CORES = 2
NT = (((1,), (1,)), ((), ()))
NN = (((1,), (0,)), ((), ()))


def round_up(value, unit):
    return (value + unit - 1) // unit * unit


class Plan:
    def __init__(self, window, occupied, cols, aux_dev, n_aux, n_pair, pairs_all):
        self.window, self.occupied, self.cols, self.aux_dev = window, occupied, cols, aux_dev
        self.n_aux, self.n_pair, self.ij = n_aux, n_pair, pairs_all
        self.xs = n_aux // CORES
        self.js = n_pair // CORES
        self.cpad = round_up(cols, ROWS)
        chunk = aux_dev // self.js
        self.main = chunk // LANES * LANES
        self.tail = chunk - self.main
        self.slot = 1
        while self.slot < self.tail:
            self.slot *= 2
        self.per_row = LANES // self.slot
        self.nm = self.main // LANES
        self.nt = window // self.per_row
        self.planes = self.nm * window + self.nt
        self.per = n_pair // n_aux
        self.c = self.per * self.cpad
        self.d = n_pair * self.cpad
        self.k = self.xs * LANES
        self.groups = n_pair
        self.blocks = window // BLK
        self.gf = self.groups * BLK
        self.tail_from = self.js * self.main
        self.tail_width = round_up(self.js * self.tail, LANES)


def spread_kernel(p, t1_ref, out_ref):
    def repeat(rows, cols, per_row, per_col):
        row = lax.broadcasted_iota(jnp.int32, (rows, cols), 0) // per_row
        col = lax.broadcasted_iota(jnp.int32, (rows, cols), 1) // per_col
        return (row == col).astype(jnp.float32).astype(jnp.bfloat16)

    rows, cols = p.window * ROWS, p.occupied * ROWS
    tall = lax.dot_general(
        repeat(rows, p.window, ROWS, 1), t1_ref[...], NT, preferred_element_type=jnp.float32
    ).astype(jnp.bfloat16)
    full = jnp.dot(
        tall, repeat(p.occupied, cols, 1, ROWS), preferred_element_type=jnp.float32
    )
    row = lax.broadcasted_iota(jnp.int32, (rows, cols), 0) % ROWS
    col = lax.broadcasted_iota(jnp.int32, (rows, cols), 1) % ROWS
    out_ref[...] = jnp.where(row == col, full, 0.0).astype(jnp.bfloat16)


def spread_amplitudes(p, t1_window):
    return pl.pallas_call(
        functools.partial(spread_kernel, p),
        out_shape=jax.ShapeDtypeStruct((p.window * ROWS, p.occupied * ROWS), jnp.bfloat16),
        compiler_params=pltpu.CompilerParams(vmem_limit_bytes=48 * 2**20),
        name="spread",
    )(t1_window)


def dress_kernel(p, offset, bounds, z_ref, a_ref, *refs):
    ov, vv, outs = refs[: p.nm + 1], refs[p.nm + 1 : 2 * p.nm + 2], refs[2 * p.nm + 2 :]

    def put(start, cols, planes):
        for out, (low, high) in zip(outs, bounds):
            first, last = max(low, start), min(high, start + planes.shape[0])
            if first < last:
                out[first - low : last - low, cols] = planes[first - start : last - start]

    w = p.window
    j = lax.rem(z_ref[0] + offset, p.js)
    lane = lax.broadcasted_iota(jnp.int32, (p.nt, ROWS, LANES), 2)
    for low in range(0, p.cpad, ROWS):
        cols = slice(low, low + ROWS)
        vectors = [ref[:, cols].reshape(p.occupied * ROWS, -1) for ref in ov]
        shift = lax.dot_general(
            a_ref[...], jnp.concatenate(vectors, axis=1), NN, preferred_element_type=jnp.float32
        )
        for m in range(p.nm):
            here = shift[:, m * LANES : (m + 1) * LANES].reshape(w, ROWS, LANES)
            here = vv[m][:, cols].astype(jnp.float32) - here
            put(m * w, cols, here.astype(jnp.bfloat16))
        here = shift[:, p.nm * LANES :].reshape(w, ROWS, p.tail_width)
        source = vv[p.nm][:, cols].astype(jnp.float32) - here
        source = source.reshape(p.nt, p.per_row, ROWS, p.tail_width)
        rest = jnp.zeros((p.nt, ROWS, LANES), jnp.float32)
        for s in range(p.per_row):
            turn = lax.rem(s * p.slot - j * p.tail + 2 * p.tail_width, p.tail_width)
            moved = pltpu.roll(source[:, s].reshape(p.nt * ROWS, p.tail_width), turn, 1)
            moved = moved[:, :LANES].reshape(p.nt, ROWS, LANES)
            keep = (lane >= s * p.slot) & (lane < s * p.slot + p.tail)
            rest = jnp.where(keep, moved, rest)
        put(p.nm * w, cols, rest.astype(jnp.bfloat16))


def dress(p, offset, bounds, z, spread, chol_vv, chol_ov):
    def specs(lead):
        found = []
        for m in range(p.nm):
            found.append(
                pl.BlockSpec(
                    (lead, p.cpad, LANES),
                    lambda i, z, m=m: (0, 0, lax.rem(z[0] + offset, p.js) * p.nm + m),
                )
            )
        found.append(
            pl.BlockSpec(
                (lead, p.cpad, p.tail_width),
                lambda i, z: (0, 0, p.tail_from // p.tail_width),
            )
        )
        return found

    count = p.nm + 1
    return pl.pallas_call(
        functools.partial(dress_kernel, p, offset, bounds),
        out_shape=[
            jax.ShapeDtypeStruct((high - low, p.cpad, LANES), jnp.bfloat16) for low, high in bounds
        ],
        grid_spec=pltpu.PrefetchScalarGridSpec(
            num_scalar_prefetch=1,
            grid=(1,),
            in_specs=[pl.BlockSpec((p.window * ROWS, p.occupied * ROWS), lambda i, z: (0, 0))]
            + specs(p.occupied)
            + specs(p.window),
            out_specs=[
                pl.BlockSpec((high - low, p.cpad, LANES), lambda i, z: (0, 0, 0))
                for low, high in bounds
            ],
        ),
        compiler_params=pltpu.CompilerParams(vmem_limit_bytes=48 * 2**20),
        cost_estimate=pl.CostEstimate(
            flops=2 * p.window * p.occupied * p.cpad * LANES * count * ROWS,
            bytes_accessed=2 * (p.occupied + 2 * p.window) * p.cpad * LANES * count,
            transcendentals=0,
        ),
        name="dress",
    )(z, spread, *([chol_ov] * count), *([chol_vv] * count))


def relayout_kernel(p, in_ref, out_ref):
    rows = ROWS * ROWS
    to = lax.broadcasted_iota(jnp.int32, (rows, rows), 0)
    frm = lax.broadcasted_iota(jnp.int32, (rows, rows), 1)
    turn = (to % ROWS * ROWS + to // ROWS == frm).astype(jnp.float32).astype(jnp.bfloat16)
    for low in range(0, p.ij, ROWS):
        block = in_ref[low : low + ROWS].reshape(rows, p.d)
        turned = lax.dot_general(turn, block, NN, preferred_element_type=jnp.float32)
        out_ref[:, low : low + ROWS] = turned.astype(jnp.bfloat16).reshape(ROWS, ROWS, p.d)


def relayout(p, amplitudes, part):
    count = p.c // AMPS
    blocks = count // ROWS
    return pl.pallas_call(
        functools.partial(relayout_kernel, p),
        out_shape=jax.ShapeDtypeStruct((count, p.ij, p.d), jnp.bfloat16),
        grid=(blocks,),
        in_specs=[pl.BlockSpec((p.ij, ROWS, p.d), lambda c: (0, part * blocks + c, 0))],
        out_specs=pl.BlockSpec((ROWS, p.ij, p.d), lambda c: (c, 0, 0)),
        compiler_params=pltpu.CompilerParams(vmem_limit_bytes=40 * 2**20),
        cost_estimate=pl.CostEstimate(
            flops=2 * count * p.ij * p.d * ROWS * ROWS,
            bytes_accessed=4 * count * p.ij * p.d,
            transcendentals=0,
        ),
        name="relayout",
    )(amplitudes)


def ladder_kernel(p, units, group, place_ref, blocks_ref, *refs):
    count = len(units) * p.xs * CORES
    pieces, amps, out = refs[:count], refs[count : count + AMPS], refs[count + AMPS]
    scratch = refs[count + AMPS + 1 :]
    vectors, left, spread_tail, tiles, held, total, piece_sem, amp_sem = scratch
    w, z, core, chunk = p.window, place_ref[0], place_ref[1], place_ref[2]
    quads = p.c // QUAD
    width = QUAD * p.ij
    steps = quads // group
    spans = [slice(low, min(low + DEEP, p.d)) for low in range(0, p.d, DEEP)]

    def fetches(span):
        rows = p.c * p.ij // AMPS
        return [
            pltpu.make_async_copy(
                amp.at[:, span],
                held.at[n * rows : (n + 1) * rows, : span.stop - span.start],
                amp_sem.at[n],
            )
            for n, amp in enumerate(amps)
        ]

    copies = []
    for n, (o, low, high) in enumerate(units):
        for r in range(p.xs):
            for other in range(CORES):
                parity = core if other == 0 else 1 - core
                origin = CORES * lax.rem(z - o + p.js, p.js) + parity
                row = pl.multiple_of(origin * p.cpad, ROWS)
                number = (n * p.xs + r) * CORES + other
                copies.append(
                    pltpu.make_async_copy(
                        pieces[number],
                        vectors.at[
                            low:high, pl.ds(row, p.cpad), r * LANES : (r + 1) * LANES
                        ],
                        piece_sem.at[number],
                    )
                )
    for copy in copies:
        copy.start()
    total[...] = jnp.zeros_like(total)
    for copy in copies:
        copy.wait()

    mixed = QUAD * ROWS
    to = lax.broadcasted_iota(jnp.int32, (mixed, mixed), 0)
    frm = lax.broadcasted_iota(jnp.int32, (mixed, mixed), 1)
    weave = ((to % BLK) * ROWS + to // BLK == frm).astype(jnp.float32).astype(jnp.bfloat16)
    lane_in = lax.broadcasted_iota(jnp.int32, (LANES, LANES), 0)
    lane_out = lax.broadcasted_iota(jnp.int32, (LANES, LANES), 1)
    same = lane_in % p.slot == lane_out % p.slot
    first = pl.multiple_of(chunk * p.c, ROWS)

    def woven(stack):
        return lax.dot_general(weave, stack, NN, preferred_element_type=jnp.float32).astype(
            jnp.bfloat16
        )

    @pl.loop(0, p.blocks)
    def _(b):
        for e in range(BLK):
            index = b * BLK + e
            plane = p.nm * w + index // p.per_row
            copier = (same & (lane_in // p.slot == index % p.per_row)).astype(jnp.float32)
            copier = copier.astype(jnp.bfloat16)
            for r in range(p.xs):
                span = slice(r * LANES, (r + 1) * LANES)
                spread_tail[e, :, span] = lax.dot_general(
                    vectors[plane, pl.ds(first, p.c), span],
                    copier,
                    NN,
                    preferred_element_type=jnp.float32,
                ).astype(jnp.bfloat16)
        for i in range(p.c // ROWS):
            span = slice(i * mixed, (i + 1) * mixed)
            tail = [spread_tail[e, i * ROWS : (i + 1) * ROWS, :] for e in range(BLK)]
            left[b, span, p.nm * p.k :] = woven(jnp.concatenate(tail, axis=0))
            for m in range(p.nm):
                at = pl.ds(pl.multiple_of(first + i * ROWS, ROWS), ROWS)
                stack = [vectors[m * w + b * BLK + e, at] for e in range(BLK)]
                left[b, span, m * p.k : (m + 1) * p.k] = woven(jnp.concatenate(stack, axis=0))

    slot_of = lax.broadcasted_iota(jnp.int32, (1, p.k), 1) % LANES // p.slot

    for span in spans:
        size = span.stop - span.start
        for copy in fetches(span):
            copy.start()

        @pl.loop(0, p.gf)
        def _(gf):
            block = blocks_ref[gf // BLK, 0]
            index = blocks_ref[gf // BLK, 1] * BLK + gf % BLK
            only = (slot_of == index % p.per_row).astype(jnp.float32).astype(jnp.bfloat16)
            rhs = [vectors[m * w + index, span] for m in range(p.nm)]
            rhs.append(vectors[p.nm * w + index // p.per_row, span] * only)
            tile = lax.dot_general(
                left[block], jnp.concatenate(rhs, axis=1), NT, preferred_element_type=jnp.float32
            )
            tiles[:, gf, :, :size] = tile.astype(jnp.bfloat16).reshape(quads, ROWS, size)

        for copy in fetches(span):
            copy.wait()

        @pl.loop(0, steps)
        def _(step):
            lhs = [
                tiles[step * group + n, :, :, :size].reshape(p.gf * ROWS, size)
                for n in range(group)
            ]
            low = pl.multiple_of(step * group * width, width)
            rhs = [held[pl.ds(low + n * width, width), :size] for n in range(group)]
            total[...] += lax.dot_general(
                jnp.concatenate(lhs, axis=1),
                jnp.concatenate(rhs, axis=1),
                NT,
                preferred_element_type=jnp.float32,
            )

    row = lax.broadcasted_iota(jnp.int32, (p.gf * ROWS, width), 0) % ROWS // BLK
    col = lax.broadcasted_iota(jnp.int32, (p.gf * ROWS, width), 1) // p.ij
    kept = jnp.where(row == col, total[...], 0.0)
    folded = kept[:, :LANES]
    for low in range(LANES, width, LANES):
        folded += kept[:, low : low + LANES]
    shift = LANES
    while shift > p.ij:
        shift //= 2
        folded += pltpu.roll(folded, shift, 1)
    folded = folded.reshape(p.gf, 2, 8, LANES).sum(axis=1)
    out[...] = folded[:, :4] + folded[:, 4:]


def ladder(p, units, place, blocks, pieces, amps):
    quads = p.c // QUAD
    group = 4 if quads % 4 == 0 else 2
    width = QUAD * p.ij
    return pl.pallas_call(
        functools.partial(ladder_kernel, p, units, group),
        out_shape=jax.ShapeDtypeStruct((p.gf, BLK, LANES), jnp.float32),
        in_specs=[pl.BlockSpec(memory_space=pltpu.SMEM)] * 2
        + [pl.BlockSpec(memory_space=pl.ANY)] * (len(pieces) + AMPS),
        out_specs=pl.BlockSpec(memory_space=pltpu.VMEM),
        scratch_shapes=[
            pltpu.VMEM((p.planes, p.d, p.k), jnp.bfloat16),
            pltpu.VMEM((p.blocks, BLK * p.c, (p.nm + 1) * p.k), jnp.bfloat16),
            pltpu.VMEM((BLK, p.c, p.k), jnp.bfloat16),
            pltpu.VMEM((quads, p.gf, ROWS, DEEP), jnp.bfloat16),
            pltpu.VMEM((p.c * p.ij, DEEP), jnp.bfloat16),
            pltpu.VMEM((p.gf * ROWS, width), jnp.float32),
            pltpu.SemaphoreType.DMA((len(pieces),)),
            pltpu.SemaphoreType.DMA((AMPS,)),
        ],
        compiler_params=pltpu.CompilerParams(vmem_limit_bytes=60 * 2**20),
        cost_estimate=pl.CostEstimate(
            flops=2 * p.gf * BLK * p.c * p.d * p.k,
            bytes_accessed=2 * (p.planes * p.d * p.k + p.c * p.ij * p.d),
            transcendentals=0,
        ),
        name="ladder",
    )(place, blocks, *pieces, *amps)


def pad_columns(array, axis, cols, cpad):
    if cols == cpad:
        return array
    shape = array.shape
    split = array.reshape(shape[:axis] + (shape[axis] // cols, cols) + shape[axis + 1 :])
    widths = [(0, 0)] * split.ndim
    widths[axis + 1] = (0, cpad - cols)
    split = jnp.pad(split, widths)
    return split.reshape(shape[:axis] + (shape[axis] // cols * cpad,) + shape[axis + 1 :])


def shards(chol_vv, chol_ov, t1_window, amplitudes, assignment):
    window, cols, aux_dev = chol_vv.shape
    n_aux, n_pair = lax.axis_size("aux"), lax.axis_size("pair")
    p = Plan(window, chol_ov.shape[0], cols, aux_dev, n_aux, n_pair, amplitudes.shape[0])
    me_aux, me_pair = lax.axis_index("aux"), lax.axis_index("pair")
    z = me_pair // CORES
    place = jnp.stack([z, me_aux % CORES, me_aux]).astype(jnp.int32)

    chol_vv = pad_columns(chol_vv, 1, cols, p.cpad)
    chol_ov = pad_columns(chol_ov, 1, cols, p.cpad)
    spread = spread_amplitudes(p, t1_window)

    def permute(array, target):
        pairs = []
        for a in range(n_aux):
            for q in range(n_pair):
                to_a, to_q = target(a, q)
                pairs.append((a * n_pair + q, to_a * n_pair + to_q))
        return lax.ppermute(array, ("aux", "pair"), pairs)

    def to_slice(array, o):
        return permute(
            array,
            lambda a, q: (
                a // CORES * CORES + q % CORES,
                CORES * ((q // CORES + o) % p.js) + a % CORES,
            ),
        )

    def along_x(array, r):
        return permute(array, lambda a, q: (CORES * ((a // CORES + r) % p.xs) + a % CORES, q))

    def to_core(array):
        return permute(array, lambda a, q: (a ^ 1, q))

    amplitudes = pad_columns(pad_columns(amplitudes, 1, cols, p.cpad), 2, cols, p.cpad)

    order = sorted(range(p.js), key=lambda o: min(o, p.js - o))
    whole = (0, p.planes)
    bounds = {o: [whole] for o in order}
    units = [(o, *bound) for o in order for bound in bounds[o]]
    rounds = [units[:2]] + [[unit] for unit in units[2:]]
    swaps = [[], units[1:2]] + [[unit] for unit in units[2:]]

    messages = {}

    def make(o, spread):
        made = dress(p, o, bounds[o], place, spread, chol_vv, chol_ov)
        return dict(zip([(o, *bound) for bound in bounds[o]], made))

    for o in order[:2]:
        made, spread = lax.optimization_barrier((make(o, spread), spread))
        messages.update(made)
    amps = [None] * AMPS
    sources = [amplitudes] * AMPS
    held, raw = {}, {}
    share_next = []
    for n in range(len(swaps) + 1):
        new, made, laid, crossed = {}, {}, {}, {}
        to_share = []
        if n != len(rounds) - 1:
            to_share, share_next = share_next, []
        if n < len(rounds):
            for unit in rounds[n]:
                new[unit, 0, 0] = to_slice(messages[unit], unit[0])
                share_next.append((unit, 0))
        if n < len(swaps):
            for unit in swaps[n]:
                for r in range(1, p.xs):
                    new[unit, r, 0] = along_x(held[unit, 0, 0], r)
                    share_next.append((unit, r))
        for r in range(1, p.xs):
            if n == 0:
                crossed[r] = along_x(messages[units[0]], r)
            if n == 1:
                new[units[0], r, 0] = to_slice(raw[r], 0)
                share_next.append((units[0], r))
        if n + 1 < len(rounds):
            for unit in rounds[n + 1]:
                if unit not in messages:
                    made.update(make(unit[0], spread))
        if n == len(rounds) - 1:
            laid = {part: relayout(p, sources[part], part) for part in range(AMPS)}
        for unit, r in to_share:
            new[unit, r, 1] = to_core(held[unit, r, 0])
        moved = (list(new.values()), list(made.values()), list(laid.values()), crossed)
        kept = (list(held.values()), spread, sources)
        moved, (old, spread, sources) = lax.optimization_barrier((moved, kept))
        held = dict(zip(held, old))
        held.update(zip(new, moved[0]))
        messages.update(zip(made, moved[1]))
        raw = moved[3]
        for part, amp in zip(laid, moved[2]):
            amps[part] = amp
    amps = [amp.reshape(-1, p.d) for amp in amps]
    pieces = [
        held[unit, r, other] for unit in units for r in range(p.xs) for other in range(CORES)
    ]

    partial_terms = ladder(p, units, place, assignment, pieces, amps)
    share = p.ij // n_aux
    terms = partial_terms[:, :, : p.ij].reshape(n_pair, BLK, BLK, n_aux, share)
    terms = terms.transpose(3, 0, 4, 2, 1).reshape(n_aux * n_pair, share, BLK * BLK)
    terms = lax.all_to_all(terms, ("aux", "pair"), split_axis=0, concat_axis=0, tiled=True)
    return terms.sum(axis=0)


def solution(mesh):
    in_specs = (P(None, "pair", "aux"), P(None, "pair", "aux"), P(), P(None, "aux", None), P())
    out_specs = P("aux", "pair")
    return jax.shard_map(shards, mesh=mesh, in_specs=in_specs, out_specs=out_specs, check_vma=False)
```

```python
import functools

import jax
import jax.numpy as jnp
from jax import lax
from jax.experimental import pallas as pl
from jax.experimental.pallas import tpu as pltpu
from jax.sharding import PartitionSpec as P

BLK = 4
QUAD = 4
AMPS = 2
SLOTS = 3
ROWS = 16
LANES = 128
CORES = 2
NT = (((1,), (1,)), ((), ()))
NN = (((1,), (0,)), ((), ()))


def round_up(value, unit):
    return (value + unit - 1) // unit * unit


class Plan:
    def __init__(self, window, occupied, cols, aux_dev, n_aux, n_pair, pairs_all):
        self.window, self.occupied, self.cols, self.aux_dev = window, occupied, cols, aux_dev
        self.n_aux, self.n_pair, self.ij = n_aux, n_pair, pairs_all
        self.xs = n_aux // CORES
        self.js = n_pair // CORES
        self.cpad = round_up(cols, ROWS)
        chunk = aux_dev // self.js
        self.main = chunk // LANES * LANES
        self.tail = chunk - self.main
        self.slot = 1
        while self.slot < self.tail:
            self.slot *= 2
        self.per_row = LANES // self.slot
        self.nm = self.main // LANES
        self.nt = window // self.per_row
        self.planes = self.nm * window + self.nt
        self.per = n_pair // n_aux
        self.c = self.per * self.cpad
        self.d = n_pair * self.cpad
        self.k = self.xs * LANES
        self.groups = n_pair
        self.blocks = window // BLK
        self.gf = self.groups * BLK
        self.tail_from = self.js * self.main
        self.tail_width = round_up(self.js * self.tail, LANES)


def spread_kernel(p, t1_ref, out_ref):
    def repeat(rows, cols, per_row, per_col):
        row = lax.broadcasted_iota(jnp.int32, (rows, cols), 0) // per_row
        col = lax.broadcasted_iota(jnp.int32, (rows, cols), 1) // per_col
        return (row == col).astype(jnp.float32).astype(jnp.bfloat16)

    rows, cols = p.window * ROWS, p.occupied * ROWS
    tall = lax.dot_general(
        repeat(rows, p.window, ROWS, 1), t1_ref[...], NT, preferred_element_type=jnp.float32
    ).astype(jnp.bfloat16)
    full = jnp.dot(
        tall, repeat(p.occupied, cols, 1, ROWS), preferred_element_type=jnp.float32
    )
    row = lax.broadcasted_iota(jnp.int32, (rows, cols), 0) % ROWS
    col = lax.broadcasted_iota(jnp.int32, (rows, cols), 1) % ROWS
    out_ref[...] = jnp.where(row == col, full, 0.0).astype(jnp.bfloat16)


def spread_amplitudes(p, t1_window):
    return pl.pallas_call(
        functools.partial(spread_kernel, p),
        out_shape=jax.ShapeDtypeStruct((p.window * ROWS, p.occupied * ROWS), jnp.bfloat16),
        compiler_params=pltpu.CompilerParams(vmem_limit_bytes=48 * 2**20),
        name="spread",
    )(t1_window)


def dress_kernel(p, offset, bounds, z_ref, a_ref, *refs):
    ov, vv, outs = refs[: p.nm + 1], refs[p.nm + 1 : 2 * p.nm + 2], refs[2 * p.nm + 2 :]

    def put(start, cols, planes):
        for out, (low, high) in zip(outs, bounds):
            first, last = max(low, start), min(high, start + planes.shape[0])
            if first < last:
                out[first - low : last - low, cols] = planes[first - start : last - start]

    w = p.window
    j = lax.rem(z_ref[0] + offset, p.js)
    lane = lax.broadcasted_iota(jnp.int32, (p.nt, ROWS, LANES), 2)
    for low in range(0, p.cpad, ROWS):
        cols = slice(low, low + ROWS)
        vectors = [ref[:, cols].reshape(p.occupied * ROWS, -1) for ref in ov]
        shift = lax.dot_general(
            a_ref[...], jnp.concatenate(vectors, axis=1), NN, preferred_element_type=jnp.float32
        )
        for m in range(p.nm):
            here = shift[:, m * LANES : (m + 1) * LANES].reshape(w, ROWS, LANES)
            here = vv[m][:, cols].astype(jnp.float32) - here
            put(m * w, cols, here.astype(jnp.bfloat16))
        here = shift[:, p.nm * LANES :].reshape(w, ROWS, p.tail_width)
        source = vv[p.nm][:, cols].astype(jnp.float32) - here
        source = source.reshape(p.nt, p.per_row, ROWS, p.tail_width)
        rest = jnp.zeros((p.nt, ROWS, LANES), jnp.float32)
        for s in range(p.per_row):
            turn = lax.rem(s * p.slot - j * p.tail + 2 * p.tail_width, p.tail_width)
            moved = pltpu.roll(source[:, s].reshape(p.nt * ROWS, p.tail_width), turn, 1)
            moved = moved[:, :LANES].reshape(p.nt, ROWS, LANES)
            keep = (lane >= s * p.slot) & (lane < s * p.slot + p.tail)
            rest = jnp.where(keep, moved, rest)
        put(p.nm * w, cols, rest.astype(jnp.bfloat16))


def dress(p, offset, bounds, z, spread, chol_vv, chol_ov):
    def specs(lead):
        found = []
        for m in range(p.nm):
            found.append(
                pl.BlockSpec(
                    (lead, p.cpad, LANES),
                    lambda i, z, m=m: (0, 0, lax.rem(z[0] + offset, p.js) * p.nm + m),
                )
            )
        found.append(
            pl.BlockSpec(
                (lead, p.cpad, p.tail_width),
                lambda i, z: (0, 0, p.tail_from // p.tail_width),
            )
        )
        return found

    count = p.nm + 1
    return pl.pallas_call(
        functools.partial(dress_kernel, p, offset, bounds),
        out_shape=[
            jax.ShapeDtypeStruct((high - low, p.cpad, LANES), jnp.bfloat16) for low, high in bounds
        ],
        grid_spec=pltpu.PrefetchScalarGridSpec(
            num_scalar_prefetch=1,
            grid=(1,),
            in_specs=[pl.BlockSpec((p.window * ROWS, p.occupied * ROWS), lambda i, z: (0, 0))]
            + specs(p.occupied)
            + specs(p.window),
            out_specs=[
                pl.BlockSpec((high - low, p.cpad, LANES), lambda i, z: (0, 0, 0))
                for low, high in bounds
            ],
        ),
        compiler_params=pltpu.CompilerParams(vmem_limit_bytes=48 * 2**20),
        cost_estimate=pl.CostEstimate(
            flops=2 * p.window * p.occupied * p.cpad * LANES * count * ROWS,
            bytes_accessed=2 * (p.occupied + 2 * p.window) * p.cpad * LANES * count,
            transcendentals=0,
        ),
        name="dress",
    )(z, spread, *([chol_ov] * count), *([chol_vv] * count))


def relayout_kernel(p, in_ref, out_ref):
    rows = ROWS * ROWS
    to = lax.broadcasted_iota(jnp.int32, (rows, rows), 0)
    frm = lax.broadcasted_iota(jnp.int32, (rows, rows), 1)
    turn = (to % ROWS * ROWS + to // ROWS == frm).astype(jnp.float32).astype(jnp.bfloat16)
    for low in range(0, p.ij, ROWS):
        block = in_ref[low : low + ROWS].reshape(rows, p.d)
        turned = lax.dot_general(turn, block, NN, preferred_element_type=jnp.float32)
        out_ref[:, low : low + ROWS] = turned.astype(jnp.bfloat16).reshape(ROWS, ROWS, p.d)


def relayout(p, amplitudes, part):
    count = p.c // AMPS
    blocks = count // ROWS
    return pl.pallas_call(
        functools.partial(relayout_kernel, p),
        out_shape=jax.ShapeDtypeStruct((count, p.ij, p.d), jnp.bfloat16),
        grid=(blocks,),
        in_specs=[pl.BlockSpec((p.ij, ROWS, p.d), lambda c: (0, part * blocks + c, 0))],
        out_specs=pl.BlockSpec((ROWS, p.ij, p.d), lambda c: (c, 0, 0)),
        compiler_params=pltpu.CompilerParams(vmem_limit_bytes=40 * 2**20),
        cost_estimate=pl.CostEstimate(
            flops=2 * count * p.ij * p.d * ROWS * ROWS,
            bytes_accessed=4 * count * p.ij * p.d,
            transcendentals=0,
        ),
        name="relayout",
    )(amplitudes)


def ladder_kernel(p, units, parts, group, place_ref, blocks_ref, *refs):
    count = len(units) * p.xs * CORES
    pieces, amps, out = refs[:count], refs[count : count + AMPS], refs[count + AMPS]
    scratch = refs[count + AMPS + 1 :]
    vectors, left_main, left_tail, spread_tail, tiles, held, total, piece_sem, amp_sem = scratch
    w, z, core, chunk = p.window, place_ref[0], place_ref[1], place_ref[2]
    quads = p.c // QUAD
    here = quads // parts
    rows = here * ROWS
    steps = here // group
    wide = group * QUAD * p.ij
    each = parts * steps // AMPS

    class Fetch:
        def __init__(self, step, slot):
            self.step, self.slot = step, slot

        def copy(self, amp, step):
            at = pl.ds(pl.multiple_of(step * wide, wide), wide)
            return pltpu.make_async_copy(amp.at[at], held.at[self.slot], amp_sem.at[self.slot])

        def start(self):
            for n, amp in enumerate(amps):

                @pl.when(self.step // each == n)
                def _():
                    self.copy(amp, self.step - n * each).start()

        def wait(self):
            self.copy(amps[0], 0).wait()

    copies = []
    for n, (o, low, high) in enumerate(units):
        for r in range(p.xs):
            for other in range(CORES):
                parity = core if other == 0 else 1 - core
                origin = CORES * lax.rem(z - o + p.js, p.js) + parity
                row = pl.multiple_of(origin * p.cpad, ROWS)
                number = (n * p.xs + r) * CORES + other
                copies.append(
                    pltpu.make_async_copy(
                        pieces[number],
                        vectors.at[
                            low:high, pl.ds(row, p.cpad), r * LANES : (r + 1) * LANES
                        ],
                        piece_sem.at[number],
                    )
                )
    for copy in copies:
        copy.start()
    for ahead in range(min(SLOTS - 1, parts * steps)):
        Fetch(jnp.int32(ahead), ahead).start()
    for copy in copies:
        copy.wait()

    mixed = QUAD * ROWS
    to = lax.broadcasted_iota(jnp.int32, (mixed, mixed), 0)
    frm = lax.broadcasted_iota(jnp.int32, (mixed, mixed), 1)
    weave = ((to % BLK) * ROWS + to // BLK == frm).astype(jnp.float32).astype(jnp.bfloat16)
    lane_in = lax.broadcasted_iota(jnp.int32, (LANES, LANES), 0)
    lane_out = lax.broadcasted_iota(jnp.int32, (LANES, LANES), 1)
    same = lane_in % p.slot == lane_out % p.slot
    first = pl.multiple_of(chunk * p.c, ROWS)

    def woven(stack):
        return lax.dot_general(weave, stack, NN, preferred_element_type=jnp.float32).astype(
            jnp.bfloat16
        )

    @pl.loop(0, p.blocks)
    def _(b):
        for e in range(BLK):
            index = b * BLK + e
            plane = p.nm * w + index // p.per_row
            copier = (same & (lane_in // p.slot == index % p.per_row)).astype(jnp.float32)
            copier = copier.astype(jnp.bfloat16)
            for r in range(p.xs):
                span = slice(r * LANES, (r + 1) * LANES)
                spread_tail[e, :, span] = lax.dot_general(
                    vectors[plane, pl.ds(first, p.c), span],
                    copier,
                    NN,
                    preferred_element_type=jnp.float32,
                ).astype(jnp.bfloat16)
        for i in range(p.c // ROWS):
            span = slice(i * mixed, (i + 1) * mixed)
            tail = [spread_tail[e, i * ROWS : (i + 1) * ROWS, :] for e in range(BLK)]
            left_tail[b, span] = woven(jnp.concatenate(tail, axis=0))
            for m in range(p.nm):
                at = pl.ds(pl.multiple_of(first + i * ROWS, ROWS), ROWS)
                stack = [vectors[m * w + b * BLK + e, at] for e in range(BLK)]
                left_main[m, b, span] = woven(jnp.concatenate(stack, axis=0))

    total[...] = jnp.zeros_like(total)
    slot_of = lax.broadcasted_iota(jnp.int32, (1, p.k), 1) % LANES // p.slot

    @pl.loop(0, parts)
    def _(part):
        part_rows = pl.ds(pl.multiple_of(part * rows, rows), rows)

        @pl.loop(0, p.gf)
        def _(gf):
            left = blocks_ref[gf // BLK, 0]
            index = blocks_ref[gf // BLK, 1] * BLK + gf % BLK
            only = (slot_of == index % p.per_row).astype(jnp.float32).astype(jnp.bfloat16)
            lhs = [left_main[m, left, part_rows] for m in range(p.nm)]
            lhs = jnp.concatenate(lhs + [left_tail[left, part_rows]], axis=1)
            for low in range(0, p.d, 256):
                span = slice(low, min(low + 256, p.d))
                rhs = [vectors[m * w + index, span] for m in range(p.nm)]
                rhs.append(vectors[p.nm * w + index // p.per_row, span] * only)
                rhs = jnp.concatenate(rhs, axis=1)
                block = lax.dot_general(lhs, rhs, NT, preferred_element_type=jnp.float32)
                block = block.astype(jnp.bfloat16).reshape(here, ROWS, span.stop - low)
                tiles[:, gf, :, span] = block

        @pl.loop(0, steps)
        def _(step):
            at = part * steps + step
            slot = lax.rem(at, SLOTS)

            @pl.when(at + SLOTS - 1 < parts * steps)
            def _():
                Fetch(at + SLOTS - 1, lax.rem(at + SLOTS - 1, SLOTS)).start()

            Fetch(at, slot).wait()
            width = QUAD * p.ij
            for n in range(group):
                total[...] += lax.dot_general(
                    tiles[step * group + n].reshape(p.gf * ROWS, p.d),
                    held[slot, n * width : (n + 1) * width],
                    NT,
                    preferred_element_type=jnp.float32,
                )

    width = QUAD * p.ij
    row = lax.broadcasted_iota(jnp.int32, (p.gf * ROWS, width), 0) % ROWS // BLK
    col = lax.broadcasted_iota(jnp.int32, (p.gf * ROWS, width), 1) // p.ij
    kept = jnp.where(row == col, total[...], 0.0)
    folded = kept[:, :LANES]
    for low in range(LANES, width, LANES):
        folded += kept[:, low : low + LANES]
    shift = LANES
    while shift > p.ij:
        shift //= 2
        folded += pltpu.roll(folded, shift, 1)
    folded = folded.reshape(p.gf, 2, 8, LANES).sum(axis=1)
    out[...] = folded[:, :4] + folded[:, 4:]


def ladder(p, units, place, blocks, pieces, amps):
    parts, group = 2, 1
    quads = p.c // QUAD
    for wanted in (4, 2):
        if quads // parts % wanted == 0:
            group = wanted
            break
    width = QUAD * p.ij
    return pl.pallas_call(
        functools.partial(ladder_kernel, p, units, parts, group),
        out_shape=jax.ShapeDtypeStruct((p.gf, BLK, LANES), jnp.float32),
        in_specs=[pl.BlockSpec(memory_space=pltpu.SMEM)] * 2
        + [pl.BlockSpec(memory_space=pl.ANY)] * (len(pieces) + AMPS),
        out_specs=pl.BlockSpec(memory_space=pltpu.VMEM),
        scratch_shapes=[
            pltpu.VMEM((p.planes, p.d, p.k), jnp.bfloat16),
            pltpu.VMEM((max(p.nm, 1), p.blocks, BLK * p.c if p.nm else ROWS, p.k), jnp.bfloat16),
            pltpu.VMEM((p.blocks, BLK * p.c, p.k), jnp.bfloat16),
            pltpu.VMEM((BLK, p.c, p.k), jnp.bfloat16),
            pltpu.VMEM((quads // parts, p.gf, ROWS, p.d), jnp.bfloat16),
            pltpu.VMEM((SLOTS, group * width, p.d), jnp.bfloat16),
            pltpu.VMEM((p.gf * ROWS, width), jnp.float32),
            pltpu.SemaphoreType.DMA((len(pieces),)),
            pltpu.SemaphoreType.DMA((SLOTS,)),
        ],
        compiler_params=pltpu.CompilerParams(vmem_limit_bytes=60 * 2**20),
        cost_estimate=pl.CostEstimate(
            flops=2 * p.gf * BLK * p.c * p.d * p.k,
            bytes_accessed=2 * (p.js * p.n_aux * p.planes * p.cpad * LANES + p.c * p.ij * p.d),
            transcendentals=0,
        ),
        name="ladder",
    )(place, blocks, *pieces, *amps)


def pad_columns(array, axis, cols, cpad):
    if cols == cpad:
        return array
    shape = array.shape
    split = array.reshape(shape[:axis] + (shape[axis] // cols, cols) + shape[axis + 1 :])
    widths = [(0, 0)] * split.ndim
    widths[axis + 1] = (0, cpad - cols)
    split = jnp.pad(split, widths)
    return split.reshape(shape[:axis] + (shape[axis] // cols * cpad,) + shape[axis + 1 :])


def shards(chol_vv, chol_ov, t1_window, amplitudes, assignment):
    window, cols, aux_dev = chol_vv.shape
    n_aux, n_pair = lax.axis_size("aux"), lax.axis_size("pair")
    p = Plan(window, chol_ov.shape[0], cols, aux_dev, n_aux, n_pair, amplitudes.shape[0])
    me_aux, me_pair = lax.axis_index("aux"), lax.axis_index("pair")
    z = me_pair // CORES
    place = jnp.stack([z, me_aux % CORES, me_aux]).astype(jnp.int32)

    chol_vv = pad_columns(chol_vv, 1, cols, p.cpad)
    chol_ov = pad_columns(chol_ov, 1, cols, p.cpad)
    spread = spread_amplitudes(p, t1_window)

    def permute(array, target):
        pairs = []
        for a in range(n_aux):
            for q in range(n_pair):
                to_a, to_q = target(a, q)
                pairs.append((a * n_pair + q, to_a * n_pair + to_q))
        return lax.ppermute(array, ("aux", "pair"), pairs)

    def to_slice(array, o):
        return permute(
            array,
            lambda a, q: (
                a // CORES * CORES + q % CORES,
                CORES * ((q // CORES + o) % p.js) + a % CORES,
            ),
        )

    def along_x(array, r):
        return permute(array, lambda a, q: (CORES * ((a // CORES + r) % p.xs) + a % CORES, q))

    def to_core(array):
        return permute(array, lambda a, q: (a ^ 1, q))

    amplitudes = pad_columns(pad_columns(amplitudes, 1, cols, p.cpad), 2, cols, p.cpad)

    order = sorted(range(p.js), key=lambda o: min(o, p.js - o))
    units = [(o, 0, p.planes) for o in order]
    rounds = [units[1:2], units[2:3] + units[:1]] + [[unit] for unit in units[3:]]
    rounds = [members for members in rounds if members]

    def make(unit, spread):
        return dress(p, unit[0], [unit[1:]], place, spread, chol_vv, chol_ov)[0]

    messages = {}
    for unit in rounds[0]:
        messages[unit], spread = lax.optimization_barrier((make(unit, spread), spread))
    amps = [None] * AMPS
    sources = [amplitudes] * AMPS
    held = {}
    share_next = []
    for n in range(len(rounds) + 2):
        new, made, laid = {}, {}, {}
        to_share = []
        if n != len(rounds) - 1:
            to_share, share_next = share_next, []
        if n < len(rounds):
            for unit in rounds[n]:
                new[unit, 0, 0] = to_slice(messages[unit], unit[0])
                share_next.append((unit, 0))
        if 1 <= n <= len(rounds):
            for unit in rounds[n - 1]:
                for r in range(1, p.xs):
                    new[unit, r, 0] = along_x(held[unit, 0, 0], r)
                    share_next.append((unit, r))
        for unit, r in to_share:
            new[unit, r, 1] = to_core(held[unit, r, 0])
        if n + 1 < len(rounds):
            made = {unit: make(unit, spread) for unit in rounds[n + 1]}
        if n == len(rounds) - 1:
            laid = {part: relayout(p, sources[part], part) for part in range(AMPS)}
        moved = (list(new.values()), list(made.values()), list(laid.values()))
        kept = (list(held.values()), spread, sources)
        moved, (old, spread, sources) = lax.optimization_barrier((moved, kept))
        held = dict(zip(held, old))
        held.update(zip(new, moved[0]))
        messages.update(zip(made, moved[1]))
        for part, amp in zip(laid, moved[2]):
            amps[part] = amp
    amps = [amp.reshape(-1, p.d) for amp in amps]
    pieces = [
        held[unit, r, other] for unit in units for r in range(p.xs) for other in range(CORES)
    ]

    partial_terms = ladder(p, units, place, assignment, pieces, amps)
    share = p.ij // n_aux
    terms = partial_terms[:, :, : p.ij].reshape(n_pair, BLK, BLK, n_aux, share)
    terms = terms.transpose(3, 0, 4, 2, 1).reshape(n_aux * n_pair, share, BLK * BLK)
    terms = lax.all_to_all(terms, ("aux", "pair"), split_axis=0, concat_axis=0, tiled=True)
    return terms.sum(axis=0)


def solution(mesh):
    in_specs = (P(None, "pair", "aux"), P(None, "pair", "aux"), P(), P(None, "aux", None), P())
    out_specs = P("aux", "pair")
    return jax.shard_map(shards, mesh=mesh, in_specs=in_specs, out_specs=out_specs, check_vma=False)
```

```python
import functools

import jax
import jax.numpy as jnp
from jax import lax
from jax.experimental import pallas as pl
from jax.experimental.pallas import tpu as pltpu
from jax.sharding import PartitionSpec as P

BLK = 4
QUAD = 4
AMPS = 2
SLOTS = 3
ROWS = 16
LANES = 128
CORES = 2
NT = (((1,), (1,)), ((), ()))
NN = (((1,), (0,)), ((), ()))


def round_up(value, unit):
    return (value + unit - 1) // unit * unit


class Plan:
    def __init__(self, window, occupied, cols, aux_dev, n_aux, n_pair, pairs_all):
        self.window, self.occupied, self.cols, self.aux_dev = window, occupied, cols, aux_dev
        self.n_aux, self.n_pair, self.ij = n_aux, n_pair, pairs_all
        self.xs = n_aux // CORES
        self.js = n_pair // CORES
        self.cpad = round_up(cols, ROWS)
        chunk = aux_dev // self.js
        self.main = chunk // LANES * LANES
        self.tail = chunk - self.main
        self.slot = 1
        while self.slot < self.tail:
            self.slot *= 2
        self.per_row = LANES // self.slot
        self.nm = self.main // LANES
        self.nt = window // self.per_row
        self.planes = self.nm * window + self.nt
        self.per = n_pair // n_aux
        self.c = self.per * self.cpad
        self.d = n_pair * self.cpad
        self.k = self.xs * LANES
        self.groups = n_pair
        self.blocks = window // BLK
        self.gf = self.groups * BLK
        self.tail_from = self.js * self.main
        self.tail_width = round_up(self.js * self.tail, LANES)


def spread_kernel(p, t1_ref, out_ref):
    def repeat(rows, cols, per_row, per_col):
        row = lax.broadcasted_iota(jnp.int32, (rows, cols), 0) // per_row
        col = lax.broadcasted_iota(jnp.int32, (rows, cols), 1) // per_col
        return (row == col).astype(jnp.float32).astype(jnp.bfloat16)

    rows, cols = p.window * ROWS, p.occupied * ROWS
    tall = lax.dot_general(
        repeat(rows, p.window, ROWS, 1), t1_ref[...], NT, preferred_element_type=jnp.float32
    ).astype(jnp.bfloat16)
    full = jnp.dot(
        tall, repeat(p.occupied, cols, 1, ROWS), preferred_element_type=jnp.float32
    )
    row = lax.broadcasted_iota(jnp.int32, (rows, cols), 0) % ROWS
    col = lax.broadcasted_iota(jnp.int32, (rows, cols), 1) % ROWS
    out_ref[...] = jnp.where(row == col, full, 0.0).astype(jnp.bfloat16)


def spread_amplitudes(p, t1_window):
    return pl.pallas_call(
        functools.partial(spread_kernel, p),
        out_shape=jax.ShapeDtypeStruct((p.window * ROWS, p.occupied * ROWS), jnp.bfloat16),
        compiler_params=pltpu.CompilerParams(vmem_limit_bytes=48 * 2**20),
        name="spread",
    )(t1_window)


def dress_kernel(p, offset, bounds, z_ref, a_ref, *refs):
    ov, vv, outs = refs[: p.nm + 1], refs[p.nm + 1 : 2 * p.nm + 2], refs[2 * p.nm + 2 :]

    def put(start, cols, planes):
        for out, (low, high) in zip(outs, bounds):
            first, last = max(low, start), min(high, start + planes.shape[0])
            if first < last:
                out[first - low : last - low, cols] = planes[first - start : last - start]

    w = p.window
    j = lax.rem(z_ref[0] + offset, p.js)
    lane = lax.broadcasted_iota(jnp.int32, (p.nt, ROWS, LANES), 2)
    for low in range(0, p.cpad, ROWS):
        cols = slice(low, low + ROWS)
        vectors = [ref[:, cols].reshape(p.occupied * ROWS, -1) for ref in ov]
        shift = lax.dot_general(
            a_ref[...], jnp.concatenate(vectors, axis=1), NN, preferred_element_type=jnp.float32
        )
        for m in range(p.nm):
            here = shift[:, m * LANES : (m + 1) * LANES].reshape(w, ROWS, LANES)
            here = vv[m][:, cols].astype(jnp.float32) - here
            put(m * w, cols, here.astype(jnp.bfloat16))
        here = shift[:, p.nm * LANES :].reshape(w, ROWS, p.tail_width)
        source = vv[p.nm][:, cols].astype(jnp.float32) - here
        source = source.reshape(p.nt, p.per_row, ROWS, p.tail_width)
        rest = jnp.zeros((p.nt, ROWS, LANES), jnp.float32)
        for s in range(p.per_row):
            turn = lax.rem(s * p.slot - j * p.tail + 2 * p.tail_width, p.tail_width)
            moved = pltpu.roll(source[:, s].reshape(p.nt * ROWS, p.tail_width), turn, 1)
            moved = moved[:, :LANES].reshape(p.nt, ROWS, LANES)
            keep = (lane >= s * p.slot) & (lane < s * p.slot + p.tail)
            rest = jnp.where(keep, moved, rest)
        put(p.nm * w, cols, rest.astype(jnp.bfloat16))


def dress(p, offset, bounds, z, spread, chol_vv, chol_ov):
    def specs(lead):
        found = []
        for m in range(p.nm):
            found.append(
                pl.BlockSpec(
                    (lead, p.cpad, LANES),
                    lambda i, z, m=m: (0, 0, lax.rem(z[0] + offset, p.js) * p.nm + m),
                )
            )
        found.append(
            pl.BlockSpec(
                (lead, p.cpad, p.tail_width),
                lambda i, z: (0, 0, p.tail_from // p.tail_width),
            )
        )
        return found

    count = p.nm + 1
    return pl.pallas_call(
        functools.partial(dress_kernel, p, offset, bounds),
        out_shape=[
            jax.ShapeDtypeStruct((high - low, p.cpad, LANES), jnp.bfloat16) for low, high in bounds
        ],
        grid_spec=pltpu.PrefetchScalarGridSpec(
            num_scalar_prefetch=1,
            grid=(1,),
            in_specs=[pl.BlockSpec((p.window * ROWS, p.occupied * ROWS), lambda i, z: (0, 0))]
            + specs(p.occupied)
            + specs(p.window),
            out_specs=[
                pl.BlockSpec((high - low, p.cpad, LANES), lambda i, z: (0, 0, 0))
                for low, high in bounds
            ],
        ),
        compiler_params=pltpu.CompilerParams(vmem_limit_bytes=48 * 2**20),
        cost_estimate=pl.CostEstimate(
            flops=2 * p.window * p.occupied * p.cpad * LANES * count * ROWS,
            bytes_accessed=2 * (p.occupied + 2 * p.window) * p.cpad * LANES * count,
            transcendentals=0,
        ),
        name="dress",
    )(z, spread, *([chol_ov] * count), *([chol_vv] * count))


def relayout_kernel(p, in_ref, out_ref):
    rows = ROWS * ROWS
    to = lax.broadcasted_iota(jnp.int32, (rows, rows), 0)
    frm = lax.broadcasted_iota(jnp.int32, (rows, rows), 1)
    turn = (to % ROWS * ROWS + to // ROWS == frm).astype(jnp.float32).astype(jnp.bfloat16)
    for low in range(0, p.ij, ROWS):
        block = in_ref[low : low + ROWS].reshape(rows, p.d)
        turned = lax.dot_general(turn, block, NN, preferred_element_type=jnp.float32)
        out_ref[:, low : low + ROWS] = turned.astype(jnp.bfloat16).reshape(ROWS, ROWS, p.d)


def relayout(p, amplitudes, part):
    count = p.c // AMPS
    blocks = count // ROWS
    return pl.pallas_call(
        functools.partial(relayout_kernel, p),
        out_shape=jax.ShapeDtypeStruct((count, p.ij, p.d), jnp.bfloat16),
        grid=(blocks,),
        in_specs=[pl.BlockSpec((p.ij, ROWS, p.d), lambda c: (0, part * blocks + c, 0))],
        out_specs=pl.BlockSpec((ROWS, p.ij, p.d), lambda c: (c, 0, 0)),
        compiler_params=pltpu.CompilerParams(vmem_limit_bytes=40 * 2**20),
        cost_estimate=pl.CostEstimate(
            flops=2 * count * p.ij * p.d * ROWS * ROWS,
            bytes_accessed=4 * count * p.ij * p.d,
            transcendentals=0,
        ),
        name="relayout",
    )(amplitudes)


def ladder_kernel(p, units, parts, group, place_ref, blocks_ref, *refs):
    count = len(units) * p.xs * CORES
    pieces, amps, out = refs[:count], refs[count : count + AMPS], refs[count + AMPS]
    scratch = refs[count + AMPS + 1 :]
    vectors, left_main, left_tail, spread_tail, tiles, held, total, piece_sem, amp_sem = scratch
    w, z, core, chunk = p.window, place_ref[0], place_ref[1], place_ref[2]
    quads = p.c // QUAD
    here = quads // parts
    rows = here * ROWS
    steps = here // group
    wide = group * QUAD * p.ij
    each = parts * steps // AMPS

    class Fetch:
        def __init__(self, step, slot):
            self.step, self.slot = step, slot

        def copy(self, amp, step):
            at = pl.ds(pl.multiple_of(step * wide, wide), wide)
            return pltpu.make_async_copy(amp.at[at], held.at[self.slot], amp_sem.at[self.slot])

        def start(self):
            for n, amp in enumerate(amps):

                @pl.when(self.step // each == n)
                def _():
                    self.copy(amp, self.step - n * each).start()

        def wait(self):
            self.copy(amps[0], 0).wait()

    copies = []
    for n, (o, low, high) in enumerate(units):
        for r in range(p.xs):
            for other in range(CORES):
                parity = core if other == 0 else 1 - core
                origin = CORES * lax.rem(z - o + p.js, p.js) + parity
                row = pl.multiple_of(origin * p.cpad, ROWS)
                number = (n * p.xs + r) * CORES + other
                copies.append(
                    pltpu.make_async_copy(
                        pieces[number],
                        vectors.at[
                            low:high, pl.ds(row, p.cpad), r * LANES : (r + 1) * LANES
                        ],
                        piece_sem.at[number],
                    )
                )
    for copy in copies:
        copy.start()
    for ahead in range(min(SLOTS - 1, parts * steps)):
        Fetch(jnp.int32(ahead), ahead).start()
    for copy in copies:
        copy.wait()

    mixed = QUAD * ROWS
    to = lax.broadcasted_iota(jnp.int32, (mixed, mixed), 0)
    frm = lax.broadcasted_iota(jnp.int32, (mixed, mixed), 1)
    weave = ((to % BLK) * ROWS + to // BLK == frm).astype(jnp.float32).astype(jnp.bfloat16)
    lane_in = lax.broadcasted_iota(jnp.int32, (LANES, LANES), 0)
    lane_out = lax.broadcasted_iota(jnp.int32, (LANES, LANES), 1)
    same = lane_in % p.slot == lane_out % p.slot
    first = pl.multiple_of(chunk * p.c, ROWS)

    def woven(stack):
        return lax.dot_general(weave, stack, NN, preferred_element_type=jnp.float32).astype(
            jnp.bfloat16
        )

    @pl.loop(0, p.blocks)
    def _(b):
        for e in range(BLK):
            index = b * BLK + e
            plane = p.nm * w + index // p.per_row
            copier = (same & (lane_in // p.slot == index % p.per_row)).astype(jnp.float32)
            copier = copier.astype(jnp.bfloat16)
            for r in range(p.xs):
                span = slice(r * LANES, (r + 1) * LANES)
                spread_tail[e, :, span] = lax.dot_general(
                    vectors[plane, pl.ds(first, p.c), span],
                    copier,
                    NN,
                    preferred_element_type=jnp.float32,
                ).astype(jnp.bfloat16)
        for i in range(p.c // ROWS):
            span = slice(i * mixed, (i + 1) * mixed)
            tail = [spread_tail[e, i * ROWS : (i + 1) * ROWS, :] for e in range(BLK)]
            left_tail[b, span] = woven(jnp.concatenate(tail, axis=0))
            for m in range(p.nm):
                at = pl.ds(pl.multiple_of(first + i * ROWS, ROWS), ROWS)
                stack = [vectors[m * w + b * BLK + e, at] for e in range(BLK)]
                left_main[m, b, span] = woven(jnp.concatenate(stack, axis=0))

    total[...] = jnp.zeros_like(total)
    slot_of = lax.broadcasted_iota(jnp.int32, (1, p.k), 1) % LANES // p.slot

    @pl.loop(0, parts)
    def _(part):
        part_rows = pl.ds(pl.multiple_of(part * rows, rows), rows)

        @pl.loop(0, p.gf)
        def _(gf):
            left = blocks_ref[gf // BLK, 0]
            index = blocks_ref[gf // BLK, 1] * BLK + gf % BLK
            only = (slot_of == index % p.per_row).astype(jnp.float32).astype(jnp.bfloat16)
            lhs = [left_main[m, left, part_rows] for m in range(p.nm)]
            lhs = jnp.concatenate(lhs + [left_tail[left, part_rows]], axis=1)
            for low in range(0, p.d, 256):
                span = slice(low, min(low + 256, p.d))
                rhs = [vectors[m * w + index, span] for m in range(p.nm)]
                rhs.append(vectors[p.nm * w + index // p.per_row, span] * only)
                rhs = jnp.concatenate(rhs, axis=1)
                block = lax.dot_general(lhs, rhs, NT, preferred_element_type=jnp.float32)
                block = block.astype(jnp.bfloat16).reshape(here, ROWS, span.stop - low)
                tiles[:, gf, :, span] = block

        @pl.loop(0, steps)
        def _(step):
            at = part * steps + step
            slot = lax.rem(at, SLOTS)

            @pl.when(at + SLOTS - 1 < parts * steps)
            def _():
                Fetch(at + SLOTS - 1, lax.rem(at + SLOTS - 1, SLOTS)).start()

            Fetch(at, slot).wait()
            width = QUAD * p.ij
            terms = [
                lax.dot_general(
                    tiles[step * group + n].reshape(p.gf * ROWS, p.d),
                    held[slot, n * width : (n + 1) * width],
                    NT,
                    preferred_element_type=jnp.float32,
                )
                for n in range(group)
            ]
            total[...] += functools.reduce(jnp.add, terms)

    width = QUAD * p.ij
    row = lax.broadcasted_iota(jnp.int32, (p.gf * ROWS, width), 0) % ROWS // BLK
    col = lax.broadcasted_iota(jnp.int32, (p.gf * ROWS, width), 1) // p.ij
    kept = jnp.where(row == col, total[...], 0.0)
    folded = kept[:, :LANES]
    for low in range(LANES, width, LANES):
        folded += kept[:, low : low + LANES]
    shift = LANES
    while shift > p.ij:
        shift //= 2
        folded += pltpu.roll(folded, shift, 1)
    folded = folded.reshape(p.gf, 2, 8, LANES).sum(axis=1)
    out[...] = folded[:, :4] + folded[:, 4:]


def ladder(p, units, place, blocks, pieces, amps):
    parts, group = 2, 1
    quads = p.c // QUAD
    for wanted in (4, 2):
        if quads // parts % wanted == 0:
            group = wanted
            break
    width = QUAD * p.ij
    return pl.pallas_call(
        functools.partial(ladder_kernel, p, units, parts, group),
        out_shape=jax.ShapeDtypeStruct((p.gf, BLK, LANES), jnp.float32),
        in_specs=[pl.BlockSpec(memory_space=pltpu.SMEM)] * 2
        + [pl.BlockSpec(memory_space=pl.ANY)] * (len(pieces) + AMPS),
        out_specs=pl.BlockSpec(memory_space=pltpu.VMEM),
        scratch_shapes=[
            pltpu.VMEM((p.planes, p.d, p.k), jnp.bfloat16),
            pltpu.VMEM((max(p.nm, 1), p.blocks, BLK * p.c if p.nm else ROWS, p.k), jnp.bfloat16),
            pltpu.VMEM((p.blocks, BLK * p.c, p.k), jnp.bfloat16),
            pltpu.VMEM((BLK, p.c, p.k), jnp.bfloat16),
            pltpu.VMEM((quads // parts, p.gf, ROWS, p.d), jnp.bfloat16),
            pltpu.VMEM((SLOTS, group * width, p.d), jnp.bfloat16),
            pltpu.VMEM((p.gf * ROWS, width), jnp.float32),
            pltpu.SemaphoreType.DMA((len(pieces),)),
            pltpu.SemaphoreType.DMA((SLOTS,)),
        ],
        compiler_params=pltpu.CompilerParams(vmem_limit_bytes=60 * 2**20),
        cost_estimate=pl.CostEstimate(
            flops=2 * p.gf * BLK * p.c * p.d * p.k,
            bytes_accessed=2 * (p.js * p.n_aux * p.planes * p.cpad * LANES + p.c * p.ij * p.d),
            transcendentals=0,
        ),
        name="ladder",
    )(place, blocks, *pieces, *amps)


def pad_columns(array, axis, cols, cpad):
    if cols == cpad:
        return array
    shape = array.shape
    split = array.reshape(shape[:axis] + (shape[axis] // cols, cols) + shape[axis + 1 :])
    widths = [(0, 0)] * split.ndim
    widths[axis + 1] = (0, cpad - cols)
    split = jnp.pad(split, widths)
    return split.reshape(shape[:axis] + (shape[axis] // cols * cpad,) + shape[axis + 1 :])


def shards(chol_vv, chol_ov, t1_window, amplitudes, assignment):
    window, cols, aux_dev = chol_vv.shape
    n_aux, n_pair = lax.axis_size("aux"), lax.axis_size("pair")
    p = Plan(window, chol_ov.shape[0], cols, aux_dev, n_aux, n_pair, amplitudes.shape[0])
    me_aux, me_pair = lax.axis_index("aux"), lax.axis_index("pair")
    z = me_pair // CORES
    place = jnp.stack([z, me_aux % CORES, me_aux]).astype(jnp.int32)

    chol_vv = pad_columns(chol_vv, 1, cols, p.cpad)
    chol_ov = pad_columns(chol_ov, 1, cols, p.cpad)
    spread = spread_amplitudes(p, t1_window)

    def permute(array, target):
        pairs = []
        for a in range(n_aux):
            for q in range(n_pair):
                to_a, to_q = target(a, q)
                pairs.append((a * n_pair + q, to_a * n_pair + to_q))
        return lax.ppermute(array, ("aux", "pair"), pairs)

    def to_slice(array, o):
        return permute(
            array,
            lambda a, q: (
                a // CORES * CORES + q % CORES,
                CORES * ((q // CORES + o) % p.js) + a % CORES,
            ),
        )

    def along_x(array, r):
        return permute(array, lambda a, q: (CORES * ((a // CORES + r) % p.xs) + a % CORES, q))

    def to_core(array):
        return permute(array, lambda a, q: (a ^ 1, q))

    amplitudes = pad_columns(pad_columns(amplitudes, 1, cols, p.cpad), 2, cols, p.cpad)

    order = sorted(range(p.js), key=lambda o: min(o, p.js - o))
    units = [(o, 0, p.planes) for o in order]
    rounds = [units[1:2], units[2:3] + units[:1]] + [[unit] for unit in units[3:]]
    rounds = [members for members in rounds if members]

    def make(unit, spread):
        return dress(p, unit[0], [unit[1:]], place, spread, chol_vv, chol_ov)[0]

    messages = {}
    for unit in rounds[0]:
        messages[unit], spread = lax.optimization_barrier((make(unit, spread), spread))
    amps = [None] * AMPS
    sources = [amplitudes] * AMPS
    held = {}
    share_next = []
    for n in range(len(rounds) + 2):
        new, made, laid = {}, {}, {}
        to_share = []
        if n != len(rounds) - 1:
            to_share, share_next = share_next, []
        if n < len(rounds):
            for unit in rounds[n]:
                new[unit, 0, 0] = to_slice(messages[unit], unit[0])
                share_next.append((unit, 0))
        if 1 <= n <= len(rounds):
            for unit in rounds[n - 1]:
                for r in range(1, p.xs):
                    new[unit, r, 0] = along_x(held[unit, 0, 0], r)
                    share_next.append((unit, r))
        for unit, r in to_share:
            new[unit, r, 1] = to_core(held[unit, r, 0])
        if n + 1 < len(rounds):
            made = {unit: make(unit, spread) for unit in rounds[n + 1]}
        if n == len(rounds) - 1:
            laid = {part: relayout(p, sources[part], part) for part in range(AMPS)}
        moved = (list(new.values()), list(made.values()), list(laid.values()))
        kept = (list(held.values()), spread, sources)
        moved, (old, spread, sources) = lax.optimization_barrier((moved, kept))
        held = dict(zip(held, old))
        held.update(zip(new, moved[0]))
        messages.update(zip(made, moved[1]))
        for part, amp in zip(laid, moved[2]):
            amps[part] = amp
    amps = [amp.reshape(-1, p.d) for amp in amps]
    pieces = [
        held[unit, r, other] for unit in units for r in range(p.xs) for other in range(CORES)
    ]

    partial_terms = ladder(p, units, place, assignment, pieces, amps)
    share = p.ij // n_aux
    terms = partial_terms[:, :, : p.ij].reshape(n_pair, BLK, BLK, n_aux, share)
    terms = terms.transpose(3, 0, 4, 2, 1).reshape(n_aux * n_pair, share, BLK * BLK)
    terms = lax.all_to_all(terms, ("aux", "pair"), split_axis=0, concat_axis=0, tiled=True)
    return terms.sum(axis=0)


def solution(mesh):
    in_specs = (P(None, "pair", "aux"), P(None, "pair", "aux"), P(), P(None, "aux", None), P())
    out_specs = P("aux", "pair")
    return jax.shard_map(shards, mesh=mesh, in_specs=in_specs, out_specs=out_specs, check_vma=False)
```
